128 devices in a mesh: row: 32 (over z, y, core), col: 4 (over x).
Axes of the slice: x: 4, y: 4, z: 4, core: 2. Of those that a mesh axis runs over, the one named last changes fastest.
Arguments:
- latent: bfloat16 [32, 4, 512, 256], P('row', 'col'), may hold values from -6 to 6
- cotangent: bfloat16 [32, 4, 512, 256], P('row', 'col'), may hold values from -6 to 6
- fine_w1: bfloat16 [512, 512], replicated, may hold values from -0.25 to 0.25
- fine_w2: bfloat16 [512, 256], replicated, may hold values from -0.25 to 0.25
- fine_gain: float32 [256], replicated, may hold values from 0.1 to 1.9
- coarse_w1: bfloat16 [512, 512], replicated, may hold values from -0.25 to 0.25
- coarse_w2: bfloat16 [512, 256], replicated, may hold values from -0.25 to 0.25
- coarse_gain: float32 [256], replicated, may hold values from 0.1 to 1.9
- fine_src: int32 [32, 4, 2048], P('row', 'col'), may hold values from 0 to 1023
- fine_dst: int32 [32, 4, 2048], P('row', 'col'), may hold values from 0 to 511
- live_blocks: int32 [32, 4], P('row', 'col'), may hold values from 8 to 16, as said below
- export_rows: int32 [32, 4, 128], P('row', 'col'), may hold values from 0 to 511
- pool_assign: int32 [32, 4, 512], P('row', 'col'), may hold values from 0 to 511
- coarse_src: int32 [32, 3072], P('row'), may hold values from 0 to 511
- coarse_dst: int32 [32, 3072], P('row'), may hold values from 0 to 511
Outputs:
- grad_latent: float32 [32, 4, 512, 256], P('row', 'col')
- grad_fine_w1: float32 [512, 512], replicated
- grad_fine_w2: float32 [512, 256], replicated
- grad_coarse_w1: float32 [512, 512], replicated
- grad_coarse_w2: float32 [512, 256], replicated
The draws below stay inside these ranges and needn't reach their ends.
Inputs may be any that keep to these rules, and one draw needn't show every extreme that they name: `live_blocks`: some partition has all 16 blocks live.
All inputs are finite; a program needn't handle non-finite values.
Results may differ from the reference program's by a relative error of at most 0.0075.
Values may be sent and summed in bfloat16 or wider, within the bound.
No kernel may reach another device: no remote copies, remote signals or barrier semaphores. Data moves between devices by JAX's collectives and lax.ppermute only.
A program may use at most 128 MiB of HBM per device.

```python
import math
import jax
import jax.numpy as jnp
from jax import lax

D = 256
H = 512
NODE_DEV = 512
EBLK = 16
BND = 128
CNODE = 512
EDGE_DEV = 2048
CEDGE_DEV = 3072
FINE_EDGES = 262144
COARSE_EDGES = 98304
N_ROW = 32
N_COL = 4


def draw_live_blocks(key, part):
    key = jax.random.fold_in(key, 7)
    first_key, second_key = jax.random.split(key)
    counts = jax.random.randint(first_key, (N_ROW * N_COL,), (EBLK + 1) // 2, EBLK + 1)
    chosen = jax.random.randint(second_key, (), 0, N_ROW * N_COL)
    counts = counts.at[chosen].set(EBLK)
    return counts.reshape(N_ROW, N_COL).astype(jnp.int32)


def with_ends(drawn, own_key, least, top_value):
    spot = [jax.random.randint(jax.random.fold_in(own_key, axis), (), 0, length) for axis, length in enumerate(drawn.shape)]
    longest = drawn.shape.index(max(drawn.shape))
    next_to = spot[:longest] + [(spot[longest] + 1) % drawn.shape[longest]] + spot[longest + 1:]
    return drawn.at[tuple(spot)].set(least).at[tuple(next_to)].set(top_value)


def block_levels(own_key, extent, cuts, least, largest):
    factor_of = 1.0
    for position, blocks in cuts:
        heights = jax.random.uniform(jax.random.fold_in(jax.random.fold_in(own_key, 6), position), (blocks,), jnp.float32, least / len(cuts), largest / len(cuts))
        factor_of = factor_of * jnp.repeat(jnp.exp(heights), extent[position] // blocks).reshape((-1,) + (1,) * (len(extent) - 1 - position))
    return factor_of


def centred(stream_key, dims, scale, bound, shards=(), kind=jnp.bfloat16):
    factor_of = block_levels(stream_key, dims, shards, -0.22, 0.18) if shards else 1.0
    entries = jax.random.normal(stream_key, dims, jnp.float32) * scale * factor_of
    return jnp.minimum(jnp.maximum(entries, -bound), bound).astype(kind)


def setup_inputs(seed: int = 0) -> dict:
    seeds = jax.random.split(jax.random.key(seed), 16)
    latent = centred(seeds[0], (N_ROW, N_COL, NODE_DEV, D), 1.0, 6.0, ((0, 32), (1, 4)))
    cotangent = centred(seeds[1], (N_ROW, N_COL, NODE_DEV, D), 1.0, 6.0, ((0, 32), (1, 4)))
    fine_w1 = centred(seeds[2], (2 * D, H), (2 * D) ** -0.5, 0.25)
    fine_w2 = centred(seeds[3], (H, D), H ** -0.5, 0.25)
    fine_gain = jnp.clip(1.0 + 0.18 * jax.random.normal(seeds[4], (D,), jnp.float32), 0.1, 1.9)
    coarse_w1 = centred(seeds[5], (2 * D, H), (2 * D) ** -0.5, 0.25)
    coarse_w2 = centred(seeds[6], (H, D), H ** -0.5, 0.25)
    coarse_gain = jnp.clip(1.0 + 0.18 * jax.random.normal(seeds[7], (D,), jnp.float32), 0.1, 1.9)
    fine_src = with_ends(jax.random.randint(seeds[8], (N_ROW, N_COL, EDGE_DEV), 0, NODE_DEV + 4 * BND), jax.random.fold_in(seeds[8], 1), 0, (NODE_DEV + 4 * BND) - 1).astype(jnp.int32)
    fine_dst = with_ends(jax.random.randint(seeds[9], (N_ROW, N_COL, EDGE_DEV), 0, NODE_DEV), jax.random.fold_in(seeds[9], 1), 0, NODE_DEV - 1).astype(jnp.int32)
    live_blocks = draw_live_blocks(jax.random.fold_in(seeds[15], 71), 0)
    export_rows = with_ends(jax.random.randint(seeds[11], (N_ROW, N_COL, BND), 0, NODE_DEV), jax.random.fold_in(seeds[11], 1), 0, NODE_DEV - 1).astype(jnp.int32)
    pool_assign = with_ends(jax.random.randint(seeds[12], (N_ROW, N_COL, NODE_DEV), 0, CNODE), jax.random.fold_in(seeds[12], 1), 0, CNODE - 1).astype(jnp.int32)
    coarse_src = with_ends(jax.random.randint(seeds[13], (N_ROW, CEDGE_DEV), 0, CNODE), jax.random.fold_in(seeds[13], 1), 0, CNODE - 1).astype(jnp.int32)
    coarse_dst = with_ends(jax.random.randint(seeds[14], (N_ROW, CEDGE_DEV), 0, CNODE), jax.random.fold_in(seeds[14], 1), 0, CNODE - 1).astype(jnp.int32)
    return {"latent": latent, "cotangent": cotangent, "fine_w1": fine_w1, "fine_w2": fine_w2, "fine_gain": fine_gain, "coarse_w1": coarse_w1, "coarse_w2": coarse_w2, "coarse_gain": coarse_gain, "fine_src": fine_src, "fine_dst": fine_dst, "live_blocks": live_blocks, "export_rows": export_rows, "pool_assign": pool_assign, "coarse_src": coarse_src, "coarse_dst": coarse_dst}


EPS = 1e-05

def inner_left(left, right):
    return lax.dot_general(left, right, (((0,), (0,)), ((), ())), preferred_element_type=jnp.float32)

def inner_right(left, right):
    return lax.dot_general(left, right, (((1,), (1,)), ((), ())), preferred_element_type=jnp.float32)

def edge_forward(lookup, senders, receivers, live_mask, first_w, second_w, node_count):
    paired = jnp.concatenate([lookup[senders], lookup[receivers]], axis=1)
    preact = jnp.dot(paired, first_w, preferred_element_type=jnp.float32)
    hidden = jax.nn.silu(preact).astype(jnp.bfloat16)
    message = jnp.dot(hidden, second_w, preferred_element_type=jnp.float32) * live_mask[:, None]
    summed = jax.ops.segment_sum(message, receivers, num_segments=node_count)
    return (paired, preact, hidden, summed)

def norm_forward(summed, gain):
    inverse = lax.rsqrt(lax.optimization_barrier(jnp.mean(summed * summed, axis=-1, keepdims=True)) + EPS)
    normed = summed * inverse
    return (normed * gain, inverse, normed)

def edge_backward(grad_new, gain, inverse, normed, paired, preact, hidden, senders, receivers, live_mask, first_w, second_w, rows):
    grad_normed = grad_new * gain
    grad_summed = inverse * (grad_normed - normed * lax.optimization_barrier(jnp.mean(grad_normed * normed, axis=-1, keepdims=True)))
    grad_message = (grad_summed[receivers] * live_mask[:, None]).astype(jnp.bfloat16)
    grad_second = inner_left(hidden, grad_message)
    grad_hidden = inner_right(grad_message, second_w)
    sigmoid_val = jax.nn.sigmoid(preact)
    grad_preact = (grad_hidden * sigmoid_val * (1.0 + preact * (1.0 - sigmoid_val))).astype(jnp.bfloat16)
    grad_first = inner_left(paired, grad_preact)
    grad_paired = inner_right(grad_preact, first_w)
    halfway = grad_paired.shape[1] // 2
    grad_lookup = jax.ops.segment_sum(grad_paired[:, :halfway], senders, num_segments=rows)
    grad_lookup = grad_lookup + jax.ops.segment_sum(grad_paired[:, halfway:], receivers, num_segments=rows)
    return (grad_lookup, grad_first, grad_second)

def pick_rows(values, picks):
    return values[picks]

def group_sum(values, picks):
    return jax.ops.segment_sum(values, picks, num_segments=CNODE)

def reference(latent, cotangent, fine_w1, fine_w2, fine_gain, coarse_w1, coarse_w2, coarse_gain, fine_src, fine_dst, live_blocks, export_rows, pool_assign, coarse_src, coarse_dst):
    devices_all = N_ROW * N_COL
    rim_rows = jax.vmap(jax.vmap(pick_rows))(latent, export_rows)
    padded = jnp.pad(rim_rows, ((1, 1), (1, 1), (0, 0), (0, 0)))
    lookup_all = jnp.concatenate([latent, padded[:-2, 1:-1], padded[2:, 1:-1], padded[1:-1, :-2], padded[1:-1, 2:]], axis=2)
    live_all = (jnp.arange(EDGE_DEV, dtype=jnp.int32)[None, None, :] < 128 * live_blocks[:, :, None]).astype(jnp.float32)

    def flatten(arr):
        return arr.reshape((devices_all,) + arr.shape[2:])

    def fine_forward(items):
        lookup, senders, receivers, live_mask, owned = items
        paired, preact, hidden, summed = edge_forward(lookup, senders, receivers, live_mask, fine_w1, fine_w2, NODE_DEV)
        update, inverse, normed = norm_forward(summed, fine_gain)
        return (owned.astype(jnp.float32) + update, inverse, normed)
    fine_items = (flatten(lookup_all), flatten(fine_src), flatten(fine_dst), flatten(live_all), flatten(latent))
    fine_new, fine_inverse, fine_normed = lax.map(fine_forward, fine_items)
    row_new = fine_new.reshape(N_ROW, N_COL * NODE_DEV, D)
    row_assign = pool_assign.reshape(N_ROW, N_COL * NODE_DEV)
    pooled_sum = jax.vmap(group_sum)(row_new, row_assign)
    pooled_count = jax.vmap(group_sum)(jnp.ones(row_assign.shape, jnp.float32), row_assign)
    weighting = 1.0 / jnp.maximum(pooled_count, 1.0)
    coarse0 = pooled_sum * weighting[:, :, None]
    coarse_lookup = coarse0.astype(jnp.bfloat16)
    grad_out = cotangent.astype(jnp.float32).reshape(N_ROW, N_COL * NODE_DEV, D)
    grad_c1 = jax.vmap(group_sum)(grad_out, row_assign)

    def coarse_pass(items):
        lookup, senders, receivers, grad_new = items
        live_mask = jnp.ones(senders.shape, jnp.float32)
        paired, preact, hidden, summed = edge_forward(lookup, senders, receivers, live_mask, coarse_w1, coarse_w2, CNODE)
        update, inverse, normed = norm_forward(summed, coarse_gain)
        return edge_backward(grad_new, coarse_gain, inverse, normed, paired, preact, hidden, senders, receivers, live_mask, coarse_w1, coarse_w2, CNODE)
    grad_clookup, grad_cfirst, grad_csecond = lax.map(coarse_pass, (coarse_lookup, coarse_src, coarse_dst, grad_c1))
    grad_c0 = grad_c1 + grad_clookup
    spread_back = jax.vmap(pick_rows)(grad_c0 * weighting[:, :, None], row_assign)
    grad_fine = (grad_out + spread_back).reshape(devices_all, NODE_DEV, D)

    def fine_backward(items):
        grad_new, inverse, normed, lookup, senders, receivers, live_mask = items
        paired, preact, hidden, summed = edge_forward(lookup, senders, receivers, live_mask, fine_w1, fine_w2, NODE_DEV)
        return edge_backward(grad_new, fine_gain, inverse, normed, paired, preact, hidden, senders, receivers, live_mask, fine_w1, fine_w2, NODE_DEV + 4 * BND)
    back_items = (grad_fine, fine_inverse, fine_normed, flatten(lookup_all), flatten(fine_src), flatten(fine_dst), flatten(live_all))
    grad_lookup, grad_first, grad_second = lax.map(fine_backward, back_items)
    grad_lookup = grad_lookup.reshape(N_ROW, N_COL, NODE_DEV + 4 * BND, D)
    ghost_grad = grad_lookup[:, :, NODE_DEV:].reshape(N_ROW, N_COL, 4, BND, D)
    ghost_pad = jnp.pad(ghost_grad, ((1, 1), (1, 1), (0, 0), (0, 0), (0, 0)))
    arrived = ghost_pad[2:, 1:-1, 0] + ghost_pad[:-2, 1:-1, 1] + ghost_pad[1:-1, 2:, 2] + ghost_pad[1:-1, :-2, 3]

    def return_rows(values, picks):
        return jax.ops.segment_sum(values, picks, num_segments=NODE_DEV)
    returned = jax.vmap(jax.vmap(return_rows))(arrived, export_rows)
    grad_latent = grad_fine.reshape(N_ROW, N_COL, NODE_DEV, D) + grad_lookup[:, :, :NODE_DEV] + returned
    fine_scale = 1.0 / math.sqrt(FINE_EDGES)
    coarse_scale = 1.0 / math.sqrt(COARSE_EDGES)
    return (grad_latent, lax.optimization_barrier(jnp.sum(grad_first, axis=0)) * fine_scale, lax.optimization_barrier(jnp.sum(grad_second, axis=0)) * fine_scale, lax.optimization_barrier(jnp.sum(grad_cfirst, axis=0)) * coarse_scale, lax.optimization_barrier(jnp.sum(grad_csecond, axis=0)) * coarse_scale)
```

```python
import math

import jax
import jax.numpy as jnp
from jax import lax
from jax.experimental import pallas as pl
from jax.experimental.pallas import tpu as pltpu
from jax.sharding import PartitionSpec as P

EPS = 1e-05
CNODE = 512
CHUNK = 512
BF = jnp.bfloat16
F32 = jnp.float32
LIMIT = 56 * 1024 * 1024


def dot(left, right):
    return lax.dot_general(left, right, (((1,), (0,)), ((), ())), preferred_element_type=F32)


def dot_rt(left, right):
    return lax.dot_general(left, right, (((1,), (1,)), ((), ())), preferred_element_type=F32)


def dot_lt(left, right):
    return lax.dot_general(left, right, (((0,), (0,)), ((), ())), preferred_element_type=F32)


def halves(value):
    high = value.astype(BF)
    return high, (value - high.astype(F32)).astype(BF)


def spread_row(row):
    count = row.shape[1]
    return jnp.concatenate(
        [
            jnp.broadcast_to(row[:, at : at + 128], (128, 128)).T
            for at in range(0, count, 128)
        ],
        axis=0,
    )


def pick_matrix(row, width):
    column = spread_row(row)
    wide = jnp.concatenate([column] * (width // 128), axis=1)
    hit = wide == lax.broadcasted_iota(jnp.int32, wide.shape, 1)
    return jnp.where(hit, 1.0, 0.0).astype(BF)


def sum_matrix(row, width):
    shape = (width, row.shape[1])
    hit = lax.broadcasted_iota(jnp.int32, shape, 0) == row
    return jnp.where(hit, 1.0, 0.0).astype(BF)


def receivers_of(dst_ref, live_ref, at):
    row = dst_ref[:, at : at + CHUNK]
    slot = lax.broadcasted_iota(jnp.int32, row.shape, 1) + at
    return jnp.where(slot < 128 * live_ref[0, 0], row, -1)


def norm_of(summed):
    inverse = lax.rsqrt(jnp.mean(summed * summed, axis=-1, keepdims=True) + EPS)
    return inverse, summed * inverse


def summed_grad(grad_new, gain, summed):
    inverse, normed = norm_of(summed)
    grad_normed = grad_new * gain
    mean = jnp.mean(grad_normed * normed, axis=-1, keepdims=True)
    return (inverse * (grad_normed - normed * mean)).astype(BF)


def activations(preact):
    sig = jax.nn.sigmoid(preact)
    return (preact * sig).astype(BF), sig * (1.0 + preact * (1.0 - sig))


def rim_kernel(own_ref, export_ref, rim_ref):
    rim_ref[...] = dot(pick_matrix(export_ref[...], own_ref.shape[0]), own_ref[...]).astype(BF)


def pool_grad_kernel(cot_ref, assign_ref, out_ref):
    pool = sum_matrix(assign_ref[...], CNODE)
    out_ref[0:CNODE, :] = dot(pool, cot_ref[...]).astype(BF)
    count = dot_rt(jnp.ones((16, pool.shape[1]), BF), pool)
    coarse_part = jnp.floor(count * (1.0 / 256.0)) * 256.0
    upper = lax.broadcasted_iota(jnp.int32, count.shape, 0) < 8
    packed = jnp.where(upper, coarse_part, count - coarse_part).astype(BF)
    out_ref[CNODE : CNODE + 16, :] = packed[:, :256]
    out_ref[CNODE + 16 : CNODE + 32, :] = packed[:, 256:]


def fine_forward_kernel(
    own_ref, r0, r1, r2, r3, src_ref, dst_ref, live_ref, w1_ref, w2_ref, gain_ref, assign_ref,
    slope_ref, acc_out, summed_ref, pooled_ref, table, acc,
):
    nodes, feature = own_ref.shape
    rim = r0.shape[0]
    table[0:nodes, :] = own_ref[...]
    for i, ref in enumerate((r0, r1, r2, r3)):
        table[nodes + i * rim : nodes + (i + 1) * rim, :] = ref[...]
    for at in range(0, src_ref.shape[1], CHUNK):
        send = pick_matrix(src_ref[:, at : at + CHUNK], table.shape[0])
        left = dot(send, table[...]).astype(BF)
        target = receivers_of(dst_ref, live_ref, at)
        right = dot(pick_matrix(target, nodes), own_ref[...]).astype(BF)
        preact = dot(left, w1_ref[0:feature, :]) + dot(right, w1_ref[feature:, :])
        hidden, slope = activations(preact)
        slope_ref[at : at + CHUNK, :] = slope
        part = dot(sum_matrix(target, nodes), hidden)
        if at == 0:
            acc[...] = part
        else:
            acc[...] += part
    high, low = halves(acc[...])
    acc_out[...] = high
    summed = dot(high, w2_ref[...]) + dot(low, w2_ref[...])
    summed_ref[...] = summed
    _, normed = norm_of(summed)
    fine_new = own_ref[...].astype(F32) + normed * gain_ref[...]
    high, low = halves(fine_new)
    pool = sum_matrix(assign_ref[...], CNODE)
    pooled_ref[...] = (dot(pool, high) + dot(pool, low)).astype(BF)


def coarse_kernel(
    p0, p1, p2, p3, g0, g1, g2, g3, src_ref, dst_ref, w1_ref, w2_ref, gain_ref, cot_ref,
    assign_ref, col_ref, grad_fine_ref, pack_ref,
    table, slope, pick_t, sum_t, acc, by_src, by_dst,
):
    feature = p0.shape[1]
    edges = src_ref.shape[1]
    count = sum(
        jnp.concatenate(
            [
                ref[CNODE : CNODE + 1, :].astype(F32) + ref[CNODE + 8 : CNODE + 9, :].astype(F32),
                ref[CNODE + 16 : CNODE + 17, :].astype(F32)
                + ref[CNODE + 24 : CNODE + 25, :].astype(F32),
            ],
            axis=1,
        )
        for ref in (g0, g1, g2, g3)
    )
    weight = spread_row(1.0 / jnp.maximum(count, 1.0))
    weight = jnp.concatenate([weight] * (feature // 128), axis=1)
    pooled = (p0[...].astype(F32) + p1[...].astype(F32)) + (
        p2[...].astype(F32) + p3[...].astype(F32)
    )
    table[...] = (pooled * weight).astype(BF)
    for at in range(0, edges, CHUNK):
        here = slice(at, at + CHUNK)
        left = dot(pick_matrix(src_ref[:, here], CNODE), table[...]).astype(BF)
        pick = pick_matrix(dst_ref[:, here], CNODE)
        pick_t[here, :] = pick
        right = dot(pick, table[...]).astype(BF)
        preact = dot(left, w1_ref[0:feature, :]) + dot(right, w1_ref[feature:, :])
        hidden, slope[here, :] = activations(preact)
        adds = sum_matrix(dst_ref[:, here], CNODE)
        sum_t[:, here] = adds
        part = dot(adds, hidden)
        if at == 0:
            acc[...] = part
        else:
            acc[...] += part
    high, low = halves(acc[...])
    summed = dot(high, w2_ref[...]) + dot(low, w2_ref[...])
    grad_c1 = (g0[0:CNODE, :].astype(F32) + g1[0:CNODE, :].astype(F32)) + (
        g2[0:CNODE, :].astype(F32) + g3[0:CNODE, :].astype(F32)
    )
    grad_summed = summed_grad(grad_c1, gain_ref[...], summed)
    for at in range(0, edges, CHUNK):
        here = slice(at, at + CHUNK)
        grad_message = dot(pick_t[here, :], grad_summed).astype(BF)
        grad_preact = (dot_rt(grad_message, w2_ref[...]) * slope[here, :]).astype(BF)
        part_src = dot(sum_matrix(src_ref[:, here], CNODE), grad_preact)
        part_dst = dot(sum_t[:, here], grad_preact)
        if at == 0:
            by_src[...] = part_src
            by_dst[...] = part_dst
        else:
            by_src[...] += part_src
            by_dst[...] += part_dst
    grad_c0 = (
        grad_c1
        + dot_rt(by_src[...].astype(BF), w1_ref[0:feature, :])
        + dot_rt(by_dst[...].astype(BF), w1_ref[feature:, :])
    )
    high, low = halves(grad_c0 * weight)
    spread = pick_matrix(assign_ref[...], CNODE)
    grad_fine_ref[...] = cot_ref[...].astype(F32) + dot(spread, high) + dot(spread, low)
    own = pl.ds(pl.multiple_of(col_ref[0] * 128, 128), 128)
    pack_ref[0:256, 0:128] = dot_lt(table[...], by_src[:, own].astype(BF)).astype(BF)
    pack_ref[0:256, 128:256] = dot_lt(table[...], by_dst[:, own].astype(BF)).astype(BF)
    pack_ref[256:384, :] = dot_lt(acc[:, own].astype(BF), grad_summed).astype(BF)


def fine_backward_kernel(
    grad_fine_ref, summed_ref, slope_ref, acc_ref, own_ref, r0, r1, r2, r3, src_ref, dst_ref,
    live_ref, w1_ref, w2_ref, gain_ref, local_ref, ghost_ref, pack_ref, table, by_src, by_dst,
):
    nodes, feature = own_ref.shape
    rim = r0.shape[0]
    table[0:nodes, :] = own_ref[...]
    for i, ref in enumerate((r0, r1, r2, r3)):
        table[nodes + i * rim : nodes + (i + 1) * rim, :] = ref[...]
    grad_fine = grad_fine_ref[...]
    grad_summed = summed_grad(grad_fine, gain_ref[...], summed_ref[...])
    for at in range(0, src_ref.shape[1], CHUNK):
        here = slice(at, at + CHUNK)
        target = receivers_of(dst_ref, live_ref, at)
        grad_message = dot(pick_matrix(target, nodes), grad_summed).astype(BF)
        grad_preact = (dot_rt(grad_message, w2_ref[...]) * slope_ref[here, :]).astype(BF)
        part_src = dot(sum_matrix(src_ref[:, here], table.shape[0]), grad_preact)
        part_dst = dot(sum_matrix(target, nodes), grad_preact)
        if at == 0:
            by_src[...] = part_src
            by_dst[...] = part_dst
        else:
            by_src[...] += part_src
            by_dst[...] += part_dst
    from_src = by_src[...].astype(BF)
    from_dst = by_dst[...].astype(BF)
    grad_table = dot_rt(from_src, w1_ref[0:feature, :])
    local_ref[...] = (
        grad_fine + grad_table[0:nodes, :] + dot_rt(from_dst, w1_ref[feature:, :])
    )
    ghost_ref[...] = grad_table[nodes:, :].astype(BF)
    first = dot_lt(table[...], from_src).astype(BF)
    second = dot_lt(own_ref[...], from_dst).astype(BF)
    pack_ref[0:256, :] = first[:, 0:256]
    pack_ref[256:512, :] = second[:, 0:256]
    pack_ref[512:768, :] = first[:, 256:512]
    pack_ref[768:1024, :] = second[:, 256:512]
    pack_ref[1024:1536, :] = dot_lt(acc_ref[...], grad_summed).astype(BF)


def return_kernel(local_ref, a0, a1, a2, a3, export_ref, out_ref):
    adds = sum_matrix(export_ref[...], local_ref.shape[0])
    arrived = (a0[...].astype(F32) + a1[...].astype(F32)) + (
        a2[...].astype(F32) + a3[...].astype(F32)
    )
    high, low = halves(arrived)
    out_ref[...] = local_ref[...] + dot(adds, high) + dot(adds, low)


def run(kernel, outs, operands, scratch=(), scalars=(), flops=0):
    shapes = [jax.ShapeDtypeStruct(shape, kind) for shape, kind in outs]
    specs = [
        pl.BlockSpec(memory_space=pltpu.SMEM if i in scalars else pltpu.VMEM)
        for i in range(len(operands))
    ]
    size = sum(math.prod(x.shape) * x.dtype.itemsize for x in list(operands) + shapes)
    return pl.pallas_call(
        kernel,
        out_shape=shapes,
        in_specs=specs,
        out_specs=[pl.BlockSpec(memory_space=pltpu.VMEM)] * len(shapes),
        scratch_shapes=[pltpu.VMEM(shape, kind) for shape, kind in scratch],
        compiler_params=pltpu.CompilerParams(vmem_limit_bytes=LIMIT),
        cost_estimate=pl.CostEstimate(flops=flops, bytes_accessed=size, transcendentals=0),
    )(*operands)


def ring_pairs(kind, step):
    if kind == "x":
        return "col", [(i, (i + step) % 4) for i in range(4)]
    pairs = []
    for row in range(32):
        z, y, core = row // 8, (row // 2) % 4, row % 2
        if kind == "core":
            core = (core + step) % 2
        elif kind == "y":
            y = (y + step) % 4
        else:
            z = (z + step) % 4
        pairs.append((row, z * 8 + y * 2 + core))
    return "row", pairs


SIZES = {"x": 4, "y": 4, "z": 4, "core": 2}


def place(kind):
    row = lax.axis_index("row")
    return {
        "x": lax.axis_index("col"),
        "y": (row // 2) % 4,
        "z": row // 8,
        "core": row % 2,
    }[kind]


def send(value, kind, step):
    axis, pairs = ring_pairs(kind, step)
    return lax.ppermute(value, axis, pairs)


def scatter_sum(value, kind):
    size = SIZES[kind]
    part = value.shape[0] // size
    me = place(kind)

    def block(step):
        return lax.dynamic_slice_in_dim(value, lax.rem(me + step, size) * part, part, 0)

    total = block(0).astype(F32)
    for got in [send(block(step), kind, step) for step in range(1, size)]:
        total = total + got.astype(F32)
    return total.astype(BF)


def all_sum(value, kind):
    size = SIZES[kind]
    me = place(kind)
    held = [value] + [send(value, kind, step) for step in range(1, size)]
    total = None
    for owner in range(size):
        away = lax.rem(me - owner + size, size)
        term = held[size - 1]
        for step in range(size - 2, -1, -1):
            term = jnp.where(away == step, held[step], term)
        term = term.astype(F32)
        total = term if total is None else total + term
    return total.astype(BF)


def collect(value, kind):
    size = SIZES[kind]
    me = place(kind)
    full = jnp.zeros((size,) + value.shape, value.dtype)
    full = lax.dynamic_update_index_in_dim(full, value, me, 0)
    for step in range(1, size):
        got = send(value, kind, step)
        full = lax.dynamic_update_index_in_dim(full, got, lax.rem(me - step + size, size), 0)
    return full


def shards(
    latent, cotangent, fine_w1, fine_w2, fine_gain, coarse_w1, coarse_w2, coarse_gain,
    fine_src, fine_dst, live_blocks, export_rows, pool_assign, coarse_src, coarse_dst,
):
    own = latent[0, 0]
    cot = cotangent[0, 0]
    nodes, feature = own.shape
    export = export_rows[0]
    assign = pool_assign[0]
    src, dst = fine_src[0], fine_dst[0]
    rim_count = export.shape[1]
    hidden = fine_w1.shape[1]
    edges, coarse_edges = src.shape[1], coarse_src.shape[1]
    rows, cols = lax.axis_size("row"), lax.axis_size("col")
    fine_gain = fine_gain[None, :]
    coarse_gain = coarse_gain[None, :]

    up = [(i, i + 1) for i in range(rows - 1)]
    down = [(i + 1, i) for i in range(rows - 1)]
    east = [(i, i + 1) for i in range(cols - 1)]
    west = [(i + 1, i) for i in range(cols - 1)]

    (rim,) = run(rim_kernel, [((rim_count, feature), BF)], [own, export])
    rims = [
        lax.ppermute(rim, "row", up),
        lax.ppermute(rim, "row", down),
        lax.ppermute(rim, "col", east),
        lax.ppermute(rim, "col", west),
    ]
    (pool_grad,) = run(pool_grad_kernel, [((CNODE + 32, feature), BF)], [cot, assign])
    pool_grads = [pool_grad] + [send(pool_grad, "x", step) for step in (1, 2, 3)]

    slope, acc, summed, pooled = run(
        fine_forward_kernel,
        [
            ((edges, hidden), F32),
            ((nodes, hidden), BF),
            ((nodes, feature), F32),
            ((CNODE, feature), BF),
        ],
        [own, *rims, src, dst, live_blocks, fine_w1, fine_w2, fine_gain, assign],
        [((nodes + 4 * rim_count, feature), BF), ((nodes, hidden), F32)],
        scalars=(7,),
    )
    pooleds = [pooled] + [send(pooled, "x", step) for step in (1, 2, 3)]

    column = lax.axis_index("col").astype(jnp.int32)[None]
    grad_fine, coarse_pack = run(
        coarse_kernel,
        [((nodes, feature), F32), ((384, 256), BF)],
        [
            *pooleds, *pool_grads, coarse_src, coarse_dst, coarse_w1, coarse_w2, coarse_gain,
            cot, assign, column,
        ],
        [
            ((CNODE, feature), BF),
            ((coarse_edges, hidden), F32),
            ((coarse_edges, CNODE), BF),
            ((CNODE, coarse_edges), BF),
            ((CNODE, hidden), F32),
            ((CNODE, hidden), F32),
            ((CNODE, hidden), F32),
        ],
        scalars=(15,),
    )

    local, ghost, fine_pack = run(
        fine_backward_kernel,
        [((nodes, feature), F32), ((4 * rim_count, feature), BF), ((1536, 256), BF)],
        [
            grad_fine, summed, slope, acc, own, *rims, src, dst, live_blocks,
            fine_w1, fine_w2, fine_gain,
        ],
        [
            ((nodes + 4 * rim_count, feature), BF),
            ((nodes + 4 * rim_count, hidden), F32),
            ((nodes, hidden), F32),
        ],
        scalars=(11,),
    )
    arrived = [
        lax.ppermute(ghost[0:rim_count], "row", down),
        lax.ppermute(ghost[rim_count : 2 * rim_count], "row", up),
        lax.ppermute(ghost[2 * rim_count : 3 * rim_count], "col", west),
        lax.ppermute(ghost[3 * rim_count :], "col", east),
    ]
    (grad_latent,) = run(return_kernel, [((nodes, feature), F32)], [local, *arrived, export])

    joint = jnp.concatenate(
        [fine_pack.reshape(2, 768, 256), coarse_pack.reshape(2, 192, 256)], axis=1
    ).reshape(1920, 256)
    half = scatter_sum(joint, "core")
    fine_part = scatter_sum(half[0:768], "x")
    both = jnp.concatenate(
        [fine_part.reshape(4, 48, 256), half[768:].reshape(4, 48, 256)], axis=1
    ).reshape(384, 256)
    part = scatter_sum(both, "y")
    part = all_sum(part, "z")
    part = collect(part, "y")
    part = collect(part, "x")
    part = collect(part, "core")
    fine_all = part[:, :, :, 0:48].reshape(1536, 256)
    coarse_all = part[:, :, :, 48:96]
    fine_scale = 1.0 / math.sqrt(edges * rows * cols)
    coarse_scale = 1.0 / math.sqrt(coarse_edges * rows)
    grad_fine_w1 = jnp.concatenate([fine_all[0:512], fine_all[512:1024]], axis=1)
    grad_fine_w2 = fine_all[1024:]
    coarse_all = jnp.moveaxis(coarse_all, 0, 1).reshape(4, 384, 256)
    first = coarse_all[:, 0:256].reshape(4, 256, 2, 128)
    grad_coarse_w1 = jnp.transpose(first, (2, 1, 0, 3)).reshape(512, 512)
    grad_coarse_w2 = coarse_all[:, 256:].reshape(512, 256)
    return (
        grad_latent[None, None],
        grad_fine_w1.astype(F32) * fine_scale,
        grad_fine_w2.astype(F32) * fine_scale,
        grad_coarse_w1.astype(F32) * coarse_scale,
        grad_coarse_w2.astype(F32) * coarse_scale,
    )


def solution(mesh):
    placed = (
        P("row", "col", None, None),
        P("row", "col", None, None),
        P(),
        P(),
        P(),
        P(),
        P(),
        P(),
        P("row", "col", None),
        P("row", "col", None),
        P("row", "col"),
        P("row", "col", None),
        P("row", "col", None),
        P("row", None),
        P("row", None),
    )
    return jax.shard_map(
        shards,
        mesh=mesh,
        in_specs=placed,
        out_specs=(P("row", "col", None, None), P(), P(), P(), P()),
        check_vma=False,
    )
```

```python
import functools
import math

import jax
import jax.numpy as jnp
from jax import lax
from jax.experimental import pallas as pl
from jax.experimental.pallas import tpu as pltpu
from jax.sharding import PartitionSpec as P

EPS = 1e-05
CNODE = 512
CHUNK = 512
LIMITS = (20, 30, 20)
BF = jnp.bfloat16
F32 = jnp.float32


def dot(left, right):
    return lax.dot_general(left, right, (((1,), (0,)), ((), ())), preferred_element_type=F32)


def dot_rt(left, right):
    return lax.dot_general(left, right, (((1,), (1,)), ((), ())), preferred_element_type=F32)


def dot_lt(left, right):
    return lax.dot_general(left, right, (((0,), (0,)), ((), ())), preferred_element_type=F32)


def halves(value):
    high = value.astype(BF)
    return high, (value - high.astype(F32)).astype(BF)


def spread_row(row):
    count = row.shape[1]
    return jnp.concatenate(
        [
            jnp.broadcast_to(row[:, at : at + 128], (128, 128)).T
            for at in range(0, count, 128)
        ],
        axis=0,
    )


def pick_matrix(row, width):
    column = spread_row(row)
    wide = jnp.concatenate([column] * (width // 128), axis=1)
    hit = wide == lax.broadcasted_iota(jnp.int32, wide.shape, 1)
    return jnp.where(hit, 1.0, 0.0).astype(BF)


def sum_matrix(row, width):
    shape = (width, row.shape[1])
    hit = lax.broadcasted_iota(jnp.int32, shape, 0) == row
    return jnp.where(hit, 1.0, 0.0).astype(BF)


def receivers_of(dst_ref, live_ref, at):
    row = dst_ref[:, at : at + CHUNK]
    slot = lax.broadcasted_iota(jnp.int32, row.shape, 1) + at
    return jnp.where(slot < 128 * live_ref[0, 0], row, -1)


def norm_of(summed):
    inverse = lax.rsqrt(jnp.mean(summed * summed, axis=-1, keepdims=True) + EPS)
    return inverse, summed * inverse


def summed_grad(grad_new, gain, summed):
    inverse, normed = norm_of(summed)
    grad_normed = grad_new * gain
    mean = jnp.mean(grad_normed * normed, axis=-1, keepdims=True)
    return (inverse * (grad_normed - normed * mean)).astype(BF)


def activations(preact):
    sig = jax.nn.sigmoid(preact)
    return (preact * sig).astype(BF), sig * (1.0 + preact * (1.0 - sig))


def rim_kernel(own_ref, export_ref, rim_ref):
    rim_ref[...] = dot(pick_matrix(export_ref[...], own_ref.shape[0]), own_ref[...]).astype(BF)


def pool_grad_kernel(cot_ref, assign_ref, out_ref):
    pool = sum_matrix(assign_ref[...], CNODE)
    out_ref[0:CNODE, :] = dot(pool, cot_ref[...]).astype(BF)
    count = dot_rt(jnp.ones((16, pool.shape[1]), BF), pool)
    coarse_part = jnp.floor(count * (1.0 / 256.0)) * 256.0
    upper = lax.broadcasted_iota(jnp.int32, count.shape, 0) < 8
    packed = jnp.where(upper, coarse_part, count - coarse_part).astype(BF)
    out_ref[CNODE : CNODE + 16, :] = packed[:, :256]
    out_ref[CNODE + 16 : CNODE + 32, :] = packed[:, 256:]


def fill_table(table, own_ref, rims, core_ref):
    nodes, rim = own_ref.shape[0], rims[0].shape[0]
    core = core_ref[0]
    table[0:nodes, :] = own_ref[...]
    table[pl.ds(pl.multiple_of(nodes + rim * (1 - core), rim), rim), :] = rims[0][...]
    table[pl.ds(pl.multiple_of(nodes + rim * core, rim), rim), :] = rims[1][...]
    table[nodes + 2 * rim : nodes + 3 * rim, :] = rims[2][...]
    table[nodes + 3 * rim :, :] = rims[3][...]


def fine_forward_kernel(
    own_ref, ra, rb, rw, re, src_ref, dst_ref, live_ref, core_ref, w1_ref, w2_ref, gain_ref,
    assign_ref, slope_ref, acc_out, summed_ref, pooled_ref, table_out, acc,
):
    nodes, feature = own_ref.shape
    table = table_out
    fill_table(table, own_ref, (ra, rb, rw, re), core_ref)
    for at in range(0, src_ref.shape[1], CHUNK):
        send = pick_matrix(src_ref[:, at : at + CHUNK], table.shape[0])
        left = dot(send, table[...]).astype(BF)
        target = receivers_of(dst_ref, live_ref, at)
        right = dot(pick_matrix(target, nodes), own_ref[...]).astype(BF)
        preact = dot(left, w1_ref[0:feature, :]) + dot(right, w1_ref[feature:, :])
        hidden, slope = activations(preact)
        slope_ref[at : at + CHUNK, :] = slope
        part = dot(sum_matrix(target, nodes), hidden)
        if at == 0:
            acc[...] = part
        else:
            acc[...] += part
    high, low = halves(acc[...])
    acc_out[...] = high
    summed = dot(high, w2_ref[...]) + dot(low, w2_ref[...])
    summed_ref[...] = summed
    _, normed = norm_of(summed)
    fine_new = own_ref[...].astype(F32) + normed * gain_ref[...]
    high, low = halves(fine_new)
    pool = sum_matrix(assign_ref[...], CNODE)
    pooled_ref[...] = (dot(pool, high) + dot(pool, low)).astype(BF)


def coarse_kernel(
    p0, p1, p2, p3, grads_ref, src_ref, dst_ref, w1_ref, w2_ref, gain_ref, cot_ref,
    assign_ref, col_ref, grad_fine_ref, pack_ref,
    table, slope, pick_t, sum_t, acc, by_src, by_dst,
):
    feature = p0.shape[1]
    edges = src_ref.shape[1]
    count = None
    for i in range(4):
        tail = [
            grads_ref[i, at : at + 1, :].astype(F32) + grads_ref[i, at + 8 : at + 9, :].astype(F32)
            for at in (CNODE, CNODE + 16)
        ]
        tail = jnp.concatenate(tail, axis=1)
        count = tail if count is None else count + tail
    weight = spread_row(1.0 / jnp.maximum(count, 1.0))
    weight = jnp.concatenate([weight] * (feature // 128), axis=1)
    pooled = (p0[...].astype(F32) + p1[...].astype(F32)) + (
        p2[...].astype(F32) + p3[...].astype(F32)
    )
    table[...] = (pooled * weight).astype(BF)
    for at in range(0, edges, CHUNK):
        here = slice(at, at + CHUNK)
        left = dot(pick_matrix(src_ref[:, here], CNODE), table[...]).astype(BF)
        pick = pick_matrix(dst_ref[:, here], CNODE)
        pick_t[here, :] = pick
        right = dot(pick, table[...]).astype(BF)
        preact = dot(left, w1_ref[0:feature, :]) + dot(right, w1_ref[feature:, :])
        hidden, slope[here, :] = activations(preact)
        adds = sum_matrix(dst_ref[:, here], CNODE)
        sum_t[:, here] = adds
        part = dot(adds, hidden)
        if at == 0:
            acc[...] = part
        else:
            acc[...] += part
    high, low = halves(acc[...])
    summed = dot(high, w2_ref[...]) + dot(low, w2_ref[...])
    grad_c1 = (grads_ref[0, 0:CNODE, :].astype(F32) + grads_ref[1, 0:CNODE, :].astype(F32)) + (
        grads_ref[2, 0:CNODE, :].astype(F32) + grads_ref[3, 0:CNODE, :].astype(F32)
    )
    grad_summed = summed_grad(grad_c1, gain_ref[...], summed)
    for at in range(0, edges, CHUNK):
        here = slice(at, at + CHUNK)
        grad_message = dot(pick_t[here, :], grad_summed).astype(BF)
        grad_preact = (dot_rt(grad_message, w2_ref[...]) * slope[here, :]).astype(BF)
        part_src = dot(sum_matrix(src_ref[:, here], CNODE), grad_preact)
        part_dst = dot(sum_t[:, here], grad_preact)
        if at == 0:
            by_src[...] = part_src
            by_dst[...] = part_dst
        else:
            by_src[...] += part_src
            by_dst[...] += part_dst
    grad_c0 = (
        grad_c1
        + dot_rt(by_src[...].astype(BF), w1_ref[0:feature, :])
        + dot_rt(by_dst[...].astype(BF), w1_ref[feature:, :])
    )
    high, low = halves(grad_c0 * weight)
    spread = pick_matrix(assign_ref[...], CNODE)
    grad_fine_ref[...] = cot_ref[...].astype(F32) + dot(spread, high) + dot(spread, low)
    own = pl.ds(pl.multiple_of(col_ref[0] * 128, 128), 128)
    for half, rows in enumerate((by_src, by_dst)):
        first = dot_lt(table[...], rows[:, own].astype(BF))
        pack_ref[half, 0:128, 0:128] = first[0:128, :]
        pack_ref[half, 0:128, 128:256] = first[128:256, :]
    second = dot_lt(acc[:, own].astype(BF), grad_summed)
    pack_ref[0, 128:192, :] = second[0:64, :]
    pack_ref[1, 128:192, :] = second[64:128, :]


def fine_backward_kernel(
    grad_fine_ref, summed_ref, slope_ref, acc_ref, table_ref, src_ref, dst_ref,
    live_ref, core_ref, w1_ref, w2_ref, gain_ref, coarse_ref,
    local_ref, give_ref, keep_ref, ghost_b, ghost_w, ghost_e, by_src, by_dst, ghost,
):
    nodes, feature = grad_fine_ref.shape
    rim = ghost_b.shape[0]
    core = core_ref[0]
    grad_fine = grad_fine_ref[...]
    grad_summed = summed_grad(grad_fine, gain_ref[...], summed_ref[...])
    for at in range(0, src_ref.shape[1], CHUNK):
        here = slice(at, at + CHUNK)
        target = receivers_of(dst_ref, live_ref, at)
        grad_message = dot(pick_matrix(target, nodes), grad_summed).astype(BF)
        grad_preact = (dot_rt(grad_message, w2_ref[...]) * slope_ref[here, :]).astype(BF)
        part_src = dot(sum_matrix(src_ref[:, here], table_ref.shape[0]), grad_preact)
        part_dst = dot(sum_matrix(target, nodes), grad_preact)
        if at == 0:
            by_src[...] = part_src
            by_dst[...] = part_dst
        else:
            by_src[...] += part_src
            by_dst[...] += part_dst
    grad_table = dot_rt(by_src[...].astype(BF), w1_ref[0:feature, :])
    local_ref[...] = (
        grad_fine
        + grad_table[0:nodes, :]
        + dot_rt(by_dst[...].astype(BF), w1_ref[feature:, :])
    )
    ghost[...] = grad_table[nodes:, :].astype(BF)
    give_ref[960:, :] = ghost[pl.ds(pl.multiple_of(rim * (1 - core), rim), rim), :]
    ghost_b[...] = ghost[pl.ds(pl.multiple_of(rim * core, rim), rim), :]
    ghost_w[...] = ghost[2 * rim : 3 * rim, :]
    ghost_e[...] = ghost[3 * rim :, :]
    for out, half in ((give_ref, 1 - core), (keep_ref, core)):
        part = pl.ds(pl.multiple_of(half * 256, 256), 256)
        out[0:256, :] = dot_lt(table_ref[...], by_src[:, part].astype(BF)).astype(out.dtype)
        out[256:512, :] = dot_lt(table_ref[0:nodes, :], by_dst[:, part].astype(BF)).astype(
            out.dtype
        )
        out[512:768, :] = dot_lt(acc_ref[:, part], grad_summed).astype(out.dtype)
        out[768:960, :] = coarse_ref[half].astype(out.dtype)


def return_kernel(local_ref, from_core, from_b, from_west, from_east, export_ref, col_ref, out_ref):
    rim = export_ref.shape[1]
    adds = sum_matrix(export_ref[...], local_ref.shape[0])
    col = col_ref[0]
    west = from_west[192:, :].astype(F32) * jnp.where(col > 0, 1.0, 0.0)
    east = from_east[192:, :].astype(F32) * jnp.where(col < 3, 1.0, 0.0)
    arrived = (from_core[960:, :].astype(F32) + from_b[...].astype(F32)) + (west + east)
    high, low = halves(arrived)
    out_ref[...] = local_ref[...] + dot(adds, high) + dot(adds, low)


def unpack_kernel(
    mine_ref, other_ref, core_ref, fine1_ref, fine2_ref, coarse1_ref, coarse2_ref,
    *, fine_scale, coarse_scale,
):
    for ref, half in ((mine_ref, core_ref[0]), (other_ref, 1 - core_ref[0])):
        for x in range(4):
            for y in range(4):
                for lo, hi in ((0, 32), (32, 48)):
                    row = x * 192 + y * 48 + lo
                    values = ref[x, y, lo:hi, :].astype(F32) * fine_scale
                    if row < 512:
                        lanes = pl.ds(pl.multiple_of(half * 256, 256), 256)
                        fine1_ref[row : row + hi - lo, lanes] = values
                    else:
                        start = pl.multiple_of(half * 256 + row - 512, 16)
                        fine2_ref[pl.ds(start, hi - lo), :] = values
                    row = y * 48 + lo
                    values = ref[x, y, 48 + lo : 48 + hi, :].astype(F32) * coarse_scale
                    if row < 128:
                        lanes = slice(x * 128, x * 128 + 128)
                        for k in range(2):
                            start = pl.multiple_of(half * 256 + k * 128 + row, 16)
                            coarse1_ref[pl.ds(start, hi - lo), lanes] = values[
                                :, k * 128 : k * 128 + 128
                            ]
                    else:
                        start = pl.multiple_of(half * 64 + x * 128 + row - 128, 16)
                        coarse2_ref[pl.ds(start, hi - lo), :] = values


def run(kernel, outs, operands, scratch=(), scalars=(), limit=16):
    shapes = [jax.ShapeDtypeStruct(shape, kind) for shape, kind in outs]
    specs = [
        pl.BlockSpec(memory_space=pltpu.SMEM if i in scalars else pltpu.VMEM)
        for i in range(len(operands))
    ]
    size = sum(math.prod(x.shape) * x.dtype.itemsize for x in list(operands) + shapes)
    return pl.pallas_call(
        kernel,
        out_shape=shapes,
        in_specs=specs,
        out_specs=[pl.BlockSpec(memory_space=pltpu.VMEM)] * len(shapes),
        scratch_shapes=[pltpu.VMEM(shape, kind) for shape, kind in scratch],
        compiler_params=pltpu.CompilerParams(vmem_limit_bytes=limit * 1024 * 1024),
        cost_estimate=pl.CostEstimate(flops=0, bytes_accessed=size, transcendentals=0),
    )(*operands)


def ring_pairs(kind, step):
    if kind == "x":
        return "col", [(i, (i + step) % 4) for i in range(4)]
    pairs = []
    for row in range(32):
        z, y, core = row // 8, (row // 2) % 4, row % 2
        if kind == "core":
            core = (core + step) % 2
        elif kind == "y":
            y = (y + step) % 4
        else:
            z = (z + step) % 4
        pairs.append((row, z * 8 + y * 2 + core))
    return "row", pairs


SIZES = {"x": 4, "y": 4, "z": 4, "core": 2}


def place(kind):
    row = lax.axis_index("row")
    return {
        "x": lax.axis_index("col"),
        "y": (row // 2) % 4,
        "z": row // 8,
        "core": row % 2,
    }[kind]


def send(value, kind, step):
    axis, pairs = ring_pairs(kind, step)
    return lax.ppermute(value, axis, pairs)


def scatter_blocks(value, size, me):
    part = value.shape[0] // size

    def block(step):
        return lax.dynamic_slice_in_dim(value, lax.rem(me + step, size) * part, part, 0)

    return block(0), [block(step).astype(BF) for step in range(1, size)]


def all_sum(value, kind):
    size = SIZES[kind]
    me = place(kind)
    value = value.astype(BF)
    held = [value] + [send(value, kind, step) for step in range(1, size)]
    total = None
    for owner in range(size):
        away = lax.rem(me - owner + size, size)
        term = held[size - 1]
        for step in range(size - 2, -1, -1):
            term = jnp.where(away == step, held[step], term)
        term = term.astype(F32)
        total = term if total is None else total + term
    return total.astype(BF)


def collect(value, kind):
    size = SIZES[kind]
    me = place(kind)
    full = jnp.zeros((size,) + value.shape, value.dtype)
    full = lax.dynamic_update_index_in_dim(full, value, me, 0)
    for step in range(1, size):
        got = send(value, kind, step)
        full = lax.dynamic_update_index_in_dim(full, got, lax.rem(me - step + size, size), 0)
    return full


def shards(
    latent, cotangent, fine_w1, fine_w2, fine_gain, coarse_w1, coarse_w2, coarse_gain,
    fine_src, fine_dst, live_blocks, export_rows, pool_assign, coarse_src, coarse_dst,
):
    own = latent[0, 0]
    cot = cotangent[0, 0]
    nodes, feature = own.shape
    export = export_rows[0]
    assign = pool_assign[0]
    src, dst = fine_src[0], fine_dst[0]
    rim_count = export.shape[1]
    hidden = fine_w1.shape[1]
    edges, coarse_edges = src.shape[1], coarse_src.shape[1]
    rows, cols = lax.axis_size("row"), lax.axis_size("col")
    fine_gain = fine_gain[None, :]
    coarse_gain = coarse_gain[None, :]

    east = [(i, i + 1) for i in range(cols - 1)]
    west = [(i + 1, i) for i in range(cols - 1)]
    between = [(i, i + 1) for i in range(1, rows - 1, 2)]
    between = between + [(target, source) for source, target in between]
    column = lax.axis_index("col").astype(jnp.int32)[None]
    core = place("core").astype(jnp.int32)[None]

    (rim,) = run(rim_kernel, [((rim_count, feature), BF)], [own, export])
    rims = [
        send(rim, "core", 1),
        lax.ppermute(rim, "row", between),
        lax.ppermute(rim, "col", east),
        lax.ppermute(rim, "col", west),
    ]
    cot_later, _ = lax.optimization_barrier((cot, rim))
    (pool_grad,) = run(pool_grad_kernel, [((CNODE + 32, feature), BF)], [cot_later, assign])
    pool_grads = lax.all_gather(pool_grad, "col")

    slope, acc, summed, pooled, table = run(
        fine_forward_kernel,
        [
            ((edges, hidden), F32),
            ((nodes, hidden), BF),
            ((nodes, feature), F32),
            ((CNODE, feature), BF),
            ((nodes + 4 * rim_count, feature), BF),
        ],
        [own, *rims, src, dst, live_blocks, core, fine_w1, fine_w2, fine_gain, assign],
        [((nodes, hidden), F32)],
        scalars=(7, 8),
        limit=LIMITS[0],
    )
    pooleds = [pooled] + [send(pooled, "x", step) for step in (1, 2, 3)]

    grad_fine, coarse_pack = run(
        coarse_kernel,
        [((nodes, feature), F32), ((2, 192, 256), F32)],
        [
            *pooleds, pool_grads, coarse_src, coarse_dst, coarse_w1, coarse_w2, coarse_gain,
            cot, assign, column,
        ],
        [
            ((CNODE, feature), BF),
            ((coarse_edges, hidden), F32),
            ((coarse_edges, CNODE), BF),
            ((CNODE, coarse_edges), BF),
            ((CNODE, hidden), F32),
            ((CNODE, hidden), F32),
            ((CNODE, hidden), F32),
        ],
        scalars=(12,),
        limit=LIMITS[1],
    )

    local, give, keep, ghost_b, ghost_w, ghost_e = run(
        fine_backward_kernel,
        [
            ((nodes, feature), F32),
            ((960 + rim_count, 256), BF),
            ((960, 256), F32),
            ((rim_count, feature), BF),
            ((rim_count, feature), BF),
            ((rim_count, feature), BF),
        ],
        [
            grad_fine, summed, slope, acc, table, src, dst, live_blocks, core,
            fine_w1, fine_w2, fine_gain, coarse_pack,
        ],
        [
            ((nodes + 4 * rim_count, hidden), F32),
            ((nodes, hidden), F32),
            ((4 * rim_count, feature), BF),
        ],
        scalars=(7, 8),
        limit=LIMITS[2],
    )
    from_core = send(give, "core", 1)
    from_b = lax.ppermute(ghost_b, "row", between)
    half = keep + from_core[0:960].astype(F32)
    total, away = scatter_blocks(half[0:768], 4, place("x"))
    to_east = jnp.concatenate([away[0], ghost_e], axis=0)
    to_west = jnp.concatenate([away[2], ghost_w], axis=0)
    from_west = send(to_east, "x", 1)
    from_cross = send(away[1], "x", 2)
    from_east = send(to_west, "x", 3)
    total = (
        total
        + from_west[0:192].astype(F32)
        + from_cross.astype(F32)
        + from_east[0:192].astype(F32)
    )
    both = jnp.concatenate([total.reshape(4, 48, 256), half[768:].reshape(4, 48, 256)], axis=1)
    total, away = scatter_blocks(both.reshape(384, 256), 4, place("y"))
    for got in [send(block, "y", step) for step, block in enumerate(away, 1)]:
        total = total + got.astype(F32)
    (grad_latent,) = run(
        return_kernel,
        [((nodes, feature), F32)],
        [local, from_core, from_b, from_west, from_east, export, column],
        scalars=(6,),
    )
    total, grad_latent = lax.optimization_barrier((total, grad_latent))
    part = all_sum(total, "z")
    part = collect(part, "y")
    part = collect(part, "x")
    other = send(part, "core", 1)
    unpack = functools.partial(
        unpack_kernel,
        fine_scale=1.0 / math.sqrt(edges * rows * cols),
        coarse_scale=1.0 / math.sqrt(coarse_edges * rows),
    )
    weight_grads = run(
        unpack,
        [
            ((2 * feature, hidden), F32),
            ((hidden, feature), F32),
            ((2 * feature, hidden), F32),
            ((hidden, feature), F32),
        ],
        [part, other, core],
        scalars=(2,),
    )
    return (grad_latent[None, None], *weight_grads)


def solution(mesh):
    placed = (
        P("row", "col", None, None),
        P("row", "col", None, None),
        P(),
        P(),
        P(),
        P(),
        P(),
        P(),
        P("row", "col", None),
        P("row", "col", None),
        P("row", "col"),
        P("row", "col", None),
        P("row", "col", None),
        P("row", None),
        P("row", None),
    )
    return jax.shard_map(
        shards,
        mesh=mesh,
        in_specs=placed,
        out_specs=(P("row", "col", None, None), P(), P(), P(), P()),
        check_vma=False,
    )
```

```python
import functools
import math

import jax
import jax.numpy as jnp
from jax import lax
from jax.experimental import pallas as pl
from jax.experimental.pallas import tpu as pltpu
from jax.sharding import PartitionSpec as P

EPS = 1e-05
CNODE = 512
CHUNK = 512
LIMITS = (20, 30, 20)
BF = jnp.bfloat16
F32 = jnp.float32


def dot(left, right):
    return lax.dot_general(left, right, (((1,), (0,)), ((), ())), preferred_element_type=F32)


def dot_rt(left, right):
    return lax.dot_general(left, right, (((1,), (1,)), ((), ())), preferred_element_type=F32)


def dot_lt(left, right):
    return lax.dot_general(left, right, (((0,), (0,)), ((), ())), preferred_element_type=F32)


def halves(value):
    high = value.astype(BF)
    return high, (value - high.astype(F32)).astype(BF)


def spread_row(row):
    count = row.shape[1]
    return jnp.concatenate(
        [
            jnp.broadcast_to(row[:, at : at + 128], (128, 128)).T
            for at in range(0, count, 128)
        ],
        axis=0,
    )


def pick_matrix(row, width):
    column = spread_row(row)
    wide = jnp.concatenate([column] * (width // 128), axis=1)
    hit = wide == lax.broadcasted_iota(jnp.int32, wide.shape, 1)
    return jnp.where(hit, 1.0, 0.0).astype(BF)


def sum_matrix(row, width):
    shape = (width, row.shape[1])
    hit = lax.broadcasted_iota(jnp.int32, shape, 0) == row
    return jnp.where(hit, 1.0, 0.0).astype(BF)


def receivers_of(dst_ref, live_ref, at):
    row = dst_ref[:, at : at + CHUNK]
    slot = lax.broadcasted_iota(jnp.int32, row.shape, 1) + at
    return jnp.where(slot < 128 * live_ref[0, 0], row, -1)


def norm_of(summed):
    inverse = lax.rsqrt(jnp.mean(summed * summed, axis=-1, keepdims=True) + EPS)
    return inverse, summed * inverse


def summed_grad(grad_new, gain, summed):
    inverse, normed = norm_of(summed)
    grad_normed = grad_new * gain
    mean = jnp.mean(grad_normed * normed, axis=-1, keepdims=True)
    return (inverse * (grad_normed - normed * mean)).astype(BF)


def activations(preact):
    sig = jax.nn.sigmoid(preact)
    return (preact * sig).astype(BF), sig * (1.0 + preact * (1.0 - sig))


def rim_kernel(own_ref, export_ref, rim_ref):
    rim_ref[...] = dot(pick_matrix(export_ref[...], own_ref.shape[0]), own_ref[...]).astype(BF)


def pool_grad_kernel(cot_ref, assign_ref, out_ref):
    pool = sum_matrix(assign_ref[...], CNODE)
    out_ref[0:CNODE, :] = dot(pool, cot_ref[...]).astype(BF)
    count = dot_rt(jnp.ones((16, pool.shape[1]), BF), pool)
    coarse_part = jnp.floor(count * (1.0 / 256.0)) * 256.0
    upper = lax.broadcasted_iota(jnp.int32, count.shape, 0) < 8
    packed = jnp.where(upper, coarse_part, count - coarse_part).astype(BF)
    out_ref[CNODE : CNODE + 16, :] = packed[:, :256]
    out_ref[CNODE + 16 : CNODE + 32, :] = packed[:, 256:]


def fill_table(table, own_ref, rims, core_ref):
    nodes, rim = own_ref.shape[0], rims[0].shape[0]
    core = core_ref[0]
    table[0:nodes, :] = own_ref[...]
    table[pl.ds(pl.multiple_of(nodes + rim * (1 - core), rim), rim), :] = rims[0][...]
    table[pl.ds(pl.multiple_of(nodes + rim * core, rim), rim), :] = rims[1][...]
    table[nodes + 2 * rim : nodes + 3 * rim, :] = rims[2][...]
    table[nodes + 3 * rim :, :] = rims[3][...]


def fine_forward_kernel(
    own_ref, ra, rb, rw, re, src_ref, dst_ref, live_ref, core_ref, w1_ref, w2_ref, gain_ref,
    assign_ref, slope_ref, acc_out, summed_ref, pooled_ref, table_out, acc,
):
    nodes, feature = own_ref.shape
    table = table_out
    fill_table(table, own_ref, (ra, rb, rw, re), core_ref)
    for at in range(0, src_ref.shape[1], CHUNK):
        send = pick_matrix(src_ref[:, at : at + CHUNK], table.shape[0])
        left = dot(send, table[...]).astype(BF)
        target = receivers_of(dst_ref, live_ref, at)
        right = dot(pick_matrix(target, nodes), own_ref[...]).astype(BF)
        preact = dot(left, w1_ref[0:feature, :]) + dot(right, w1_ref[feature:, :])
        hidden, slope = activations(preact)
        slope_ref[at : at + CHUNK, :] = slope
        part = dot(sum_matrix(target, nodes), hidden)
        if at == 0:
            acc[...] = part
        else:
            acc[...] += part
    high, low = halves(acc[...])
    acc_out[...] = high
    summed = dot(high, w2_ref[...]) + dot(low, w2_ref[...])
    summed_ref[...] = summed
    _, normed = norm_of(summed)
    fine_new = own_ref[...].astype(F32) + normed * gain_ref[...]
    high, low = halves(fine_new)
    pool = sum_matrix(assign_ref[...], CNODE)
    pooled_ref[...] = (dot(pool, high) + dot(pool, low)).astype(BF)


def coarse_kernel(
    p0, p1, p2, p3, g0, g1, g2, g3, src_ref, dst_ref, w1_ref, w2_ref, gain_ref, cot_ref,
    assign_ref, col_ref, grad_fine_ref, pack_ref,
    table, slope, pick_t, sum_t, acc, by_src, by_dst,
):
    feature = p0.shape[1]
    edges = src_ref.shape[1]
    count = None
    for ref in (g0, g1, g2, g3):
        tail = [
            ref[at : at + 1, :].astype(F32) + ref[at + 8 : at + 9, :].astype(F32)
            for at in (CNODE, CNODE + 16)
        ]
        tail = jnp.concatenate(tail, axis=1)
        count = tail if count is None else count + tail
    weight = spread_row(1.0 / jnp.maximum(count, 1.0))
    weight = jnp.concatenate([weight] * (feature // 128), axis=1)
    pooled = (p0[...].astype(F32) + p1[...].astype(F32)) + (
        p2[...].astype(F32) + p3[...].astype(F32)
    )
    table[...] = (pooled * weight).astype(BF)
    for at in range(0, edges, CHUNK):
        here = slice(at, at + CHUNK)
        left = dot(pick_matrix(src_ref[:, here], CNODE), table[...]).astype(BF)
        pick = pick_matrix(dst_ref[:, here], CNODE)
        pick_t[here, :] = pick
        right = dot(pick, table[...]).astype(BF)
        preact = dot(left, w1_ref[0:feature, :]) + dot(right, w1_ref[feature:, :])
        hidden, slope[here, :] = activations(preact)
        adds = sum_matrix(dst_ref[:, here], CNODE)
        sum_t[:, here] = adds
        part = dot(adds, hidden)
        if at == 0:
            acc[...] = part
        else:
            acc[...] += part
    high, low = halves(acc[...])
    summed = dot(high, w2_ref[...]) + dot(low, w2_ref[...])
    grad_c1 = (g0[0:CNODE, :].astype(F32) + g1[0:CNODE, :].astype(F32)) + (
        g2[0:CNODE, :].astype(F32) + g3[0:CNODE, :].astype(F32)
    )
    grad_summed = summed_grad(grad_c1, gain_ref[...], summed)
    for at in range(0, edges, CHUNK):
        here = slice(at, at + CHUNK)
        grad_message = dot(pick_t[here, :], grad_summed).astype(BF)
        grad_preact = (dot_rt(grad_message, w2_ref[...]) * slope[here, :]).astype(BF)
        part_src = dot(sum_matrix(src_ref[:, here], CNODE), grad_preact)
        part_dst = dot(sum_t[:, here], grad_preact)
        if at == 0:
            by_src[...] = part_src
            by_dst[...] = part_dst
        else:
            by_src[...] += part_src
            by_dst[...] += part_dst
    grad_c0 = (
        grad_c1
        + dot_rt(by_src[...].astype(BF), w1_ref[0:feature, :])
        + dot_rt(by_dst[...].astype(BF), w1_ref[feature:, :])
    )
    high, low = halves(grad_c0 * weight)
    spread = pick_matrix(assign_ref[...], CNODE)
    grad_fine_ref[...] = cot_ref[...].astype(F32) + dot(spread, high) + dot(spread, low)
    own = pl.ds(pl.multiple_of(col_ref[0] * 128, 128), 128)
    for half, rows in enumerate((by_src, by_dst)):
        first = dot_lt(table[...], rows[:, own].astype(BF))
        pack_ref[half, 0:128, 0:128] = first[0:128, :]
        pack_ref[half, 0:128, 128:256] = first[128:256, :]
    second = dot_lt(acc[:, own].astype(BF), grad_summed)
    pack_ref[0, 128:192, :] = second[0:64, :]
    pack_ref[1, 128:192, :] = second[64:128, :]


def fine_backward_kernel(
    grad_fine_ref, summed_ref, slope_ref, acc_ref, table_ref, src_ref, dst_ref,
    live_ref, core_ref, w1_ref, w2_ref, gain_ref, coarse_ref,
    local_ref, give_ref, keep_ref, ghost_b, ghost_w, ghost_e, by_src, by_dst, ghost,
):
    nodes, feature = grad_fine_ref.shape
    rim = ghost_b.shape[0]
    core = core_ref[0]
    grad_fine = grad_fine_ref[...]
    grad_summed = summed_grad(grad_fine, gain_ref[...], summed_ref[...])
    for at in range(0, src_ref.shape[1], CHUNK):
        here = slice(at, at + CHUNK)
        target = receivers_of(dst_ref, live_ref, at)
        grad_message = dot(pick_matrix(target, nodes), grad_summed).astype(BF)
        grad_preact = (dot_rt(grad_message, w2_ref[...]) * slope_ref[here, :]).astype(BF)
        part_src = dot(sum_matrix(src_ref[:, here], table_ref.shape[0]), grad_preact)
        part_dst = dot(sum_matrix(target, nodes), grad_preact)
        if at == 0:
            by_src[...] = part_src
            by_dst[...] = part_dst
        else:
            by_src[...] += part_src
            by_dst[...] += part_dst
    grad_table = dot_rt(by_src[...].astype(BF), w1_ref[0:feature, :])
    local_ref[...] = (
        grad_fine
        + grad_table[0:nodes, :]
        + dot_rt(by_dst[...].astype(BF), w1_ref[feature:, :])
    )
    ghost[...] = grad_table[nodes:, :].astype(BF)
    give_ref[960:, :] = ghost[pl.ds(pl.multiple_of(rim * (1 - core), rim), rim), :]
    ghost_b[...] = ghost[pl.ds(pl.multiple_of(rim * core, rim), rim), :]
    ghost_w[...] = ghost[2 * rim : 3 * rim, :]
    ghost_e[...] = ghost[3 * rim :, :]
    for out, half in ((give_ref, 1 - core), (keep_ref, core)):
        part = pl.ds(pl.multiple_of(half * 256, 256), 256)
        out[0:256, :] = dot_lt(table_ref[...], by_src[:, part].astype(BF)).astype(out.dtype)
        out[256:512, :] = dot_lt(table_ref[0:nodes, :], by_dst[:, part].astype(BF)).astype(
            out.dtype
        )
        out[512:768, :] = dot_lt(acc_ref[:, part], grad_summed).astype(out.dtype)
        out[768:960, :] = coarse_ref[half].astype(out.dtype)


def return_kernel(local_ref, from_core, from_b, from_west, from_east, export_ref, col_ref, out_ref):
    rim = export_ref.shape[1]
    adds = sum_matrix(export_ref[...], local_ref.shape[0])
    col = col_ref[0]
    west = from_west[192:, :].astype(F32) * jnp.where(col > 0, 1.0, 0.0)
    east = from_east[192:, :].astype(F32) * jnp.where(col < 3, 1.0, 0.0)
    arrived = (from_core[960:, :].astype(F32) + from_b[...].astype(F32)) + (west + east)
    high, low = halves(arrived)
    out_ref[...] = local_ref[...] + dot(adds, high) + dot(adds, low)


def unpack_kernel(
    mine_ref, other_ref, core_ref, fine1_ref, fine2_ref, coarse1_ref, coarse2_ref,
    *, fine_scale, coarse_scale,
):
    for ref, half in ((mine_ref, core_ref[0]), (other_ref, 1 - core_ref[0])):
        for x in range(4):
            for y in range(4):
                for lo, hi in ((0, 32), (32, 48)):
                    row = x * 192 + y * 48 + lo
                    values = ref[x, y, lo:hi, :].astype(F32) * fine_scale
                    if row < 512:
                        lanes = pl.ds(pl.multiple_of(half * 256, 256), 256)
                        fine1_ref[row : row + hi - lo, lanes] = values
                    else:
                        start = pl.multiple_of(half * 256 + row - 512, 16)
                        fine2_ref[pl.ds(start, hi - lo), :] = values
                    row = y * 48 + lo
                    values = ref[x, y, 48 + lo : 48 + hi, :].astype(F32) * coarse_scale
                    if row < 128:
                        lanes = slice(x * 128, x * 128 + 128)
                        for k in range(2):
                            start = pl.multiple_of(half * 256 + k * 128 + row, 16)
                            coarse1_ref[pl.ds(start, hi - lo), lanes] = values[
                                :, k * 128 : k * 128 + 128
                            ]
                    else:
                        start = pl.multiple_of(half * 64 + x * 128 + row - 128, 16)
                        coarse2_ref[pl.ds(start, hi - lo), :] = values


class Late:
    def __init__(self, source, held, sem):
        self.held = held
        self.shape = held.shape
        self.copy = pltpu.make_async_copy(source, held, sem)
        self.copy.start()

    def __getitem__(self, index):
        if self.copy is not None:
            self.copy.wait()
            self.copy = None
        return self.held[index]

    def finish(self):
        if self.copy is not None:
            self.copy.wait()
            self.copy = None


def run(kernel, outs, operands, scratch=(), scalars=(), late=(), inner=(), limit=16):
    shapes = [
        (pltpu.VMEM if i in inner else jax.ShapeDtypeStruct)(shape, kind)
        for i, (shape, kind) in enumerate(outs)
    ]
    operands = [
        pltpu.with_memory_space_constraint(x, pltpu.HBM) if i in late else x
        for i, x in enumerate(operands)
    ]

    def space(i):
        return pltpu.SMEM if i in scalars else pltpu.HBM if i in late else pltpu.VMEM

    first_out = len(operands)
    first_scratch = first_out + len(shapes)
    first_held = first_scratch + len(scratch)

    def body(*refs):
        sems = refs[-1]
        inputs = list(refs[:first_out])
        for k, i in enumerate(late):
            inputs[i] = Late(refs[i], refs[first_held + k], sems.at[k])
        kernel(*inputs, *refs[first_out:first_held])
        for i in late:
            inputs[i].finish()

    size = sum(math.prod(x.shape) * x.dtype.itemsize for x in operands) + sum(
        math.prod(shape) * jnp.dtype(kind).itemsize for shape, kind in outs
    )
    return pl.pallas_call(
        body if late else kernel,
        out_shape=shapes,
        in_specs=[pl.BlockSpec(memory_space=space(i)) for i in range(len(operands))],
        out_specs=[pl.BlockSpec(memory_space=pltpu.VMEM)] * len(shapes),
        scratch_shapes=[pltpu.VMEM(shape, kind) for shape, kind in scratch]
        + [pltpu.VMEM(operands[i].shape, operands[i].dtype) for i in late]
        + ([pltpu.SemaphoreType.DMA((len(late),))] if late else []),
        compiler_params=pltpu.CompilerParams(vmem_limit_bytes=limit * 1024 * 1024),
        cost_estimate=pl.CostEstimate(flops=0, bytes_accessed=size, transcendentals=0),
    )(*operands)


def ring_pairs(kind, step):
    if kind == "x":
        return "col", [(i, (i + step) % 4) for i in range(4)]
    pairs = []
    for row in range(32):
        z, y, core = row // 8, (row // 2) % 4, row % 2
        if kind == "core":
            core = (core + step) % 2
        elif kind == "y":
            y = (y + step) % 4
        else:
            z = (z + step) % 4
        pairs.append((row, z * 8 + y * 2 + core))
    return "row", pairs


SIZES = {"x": 4, "y": 4, "z": 4, "core": 2}


def place(kind):
    row = lax.axis_index("row")
    return {
        "x": lax.axis_index("col"),
        "y": (row // 2) % 4,
        "z": row // 8,
        "core": row % 2,
    }[kind]


def send(value, kind, step):
    axis, pairs = ring_pairs(kind, step)
    return lax.ppermute(value, axis, pairs)


def scatter_blocks(value, size, me):
    part = value.shape[0] // size

    def block(step):
        return lax.dynamic_slice_in_dim(value, lax.rem(me + step, size) * part, part, 0)

    return block(0), [block(step).astype(BF) for step in range(1, size)]


def all_sum(value, kind):
    size = SIZES[kind]
    me = place(kind)
    value = value.astype(BF)
    held = [value] + [send(value, kind, step) for step in range(1, size)]
    total = None
    for owner in range(size):
        away = lax.rem(me - owner + size, size)
        term = held[size - 1]
        for step in range(size - 2, -1, -1):
            term = jnp.where(away == step, held[step], term)
        term = term.astype(F32)
        total = term if total is None else total + term
    return total.astype(BF)


def collect(value, kind):
    size = SIZES[kind]
    me = place(kind)
    full = jnp.zeros((size,) + value.shape, value.dtype)
    full = lax.dynamic_update_index_in_dim(full, value, me, 0)
    for step in range(1, size):
        got = send(value, kind, step)
        full = lax.dynamic_update_index_in_dim(full, got, lax.rem(me - step + size, size), 0)
    return full


def shards(
    latent, cotangent, fine_w1, fine_w2, fine_gain, coarse_w1, coarse_w2, coarse_gain,
    fine_src, fine_dst, live_blocks, export_rows, pool_assign, coarse_src, coarse_dst,
):
    own = latent[0, 0]
    cot = cotangent[0, 0]
    nodes, feature = own.shape
    export = export_rows[0]
    assign = pool_assign[0]
    src, dst = fine_src[0], fine_dst[0]
    rim_count = export.shape[1]
    hidden = fine_w1.shape[1]
    edges, coarse_edges = src.shape[1], coarse_src.shape[1]
    rows, cols = lax.axis_size("row"), lax.axis_size("col")
    fine_gain = fine_gain[None, :]
    coarse_gain = coarse_gain[None, :]

    east = [(i, i + 1) for i in range(cols - 1)]
    west = [(i + 1, i) for i in range(cols - 1)]
    between = [(i, i + 1) for i in range(1, rows - 1, 2)]
    between = between + [(target, source) for source, target in between]
    column = lax.axis_index("col").astype(jnp.int32)[None]
    core = place("core").astype(jnp.int32)[None]

    (rim,) = run(rim_kernel, [((rim_count, feature), BF)], [own, export], late=(0, 1))
    rims = [
        send(rim, "core", 1),
        lax.ppermute(rim, "row", between),
        lax.ppermute(rim, "col", east),
        lax.ppermute(rim, "col", west),
    ]
    cot_later, _ = lax.optimization_barrier((cot, rim))
    (pool_grad,) = run(
        pool_grad_kernel, [((CNODE + 32, feature), BF)], [cot_later, assign], late=(0, 1)
    )
    pool_grads = [pool_grad] + [send(pool_grad, "x", step) for step in (1, 2, 3)]

    slope, acc, summed, pooled, table = run(
        fine_forward_kernel,
        [
            ((edges, hidden), F32),
            ((nodes, hidden), BF),
            ((nodes, feature), F32),
            ((CNODE, feature), BF),
            ((nodes + 4 * rim_count, feature), BF),
        ],
        [own, *rims, src, dst, live_blocks, core, fine_w1, fine_w2, fine_gain, assign],
        [((nodes, hidden), F32)],
        scalars=(7, 8),
        late=(0, 5, 6, 9, 10, 11, 12),
        inner=(0, 1, 2, 3, 4),
        limit=LIMITS[0],
    )
    pooleds = [pooled] + [send(pooled, "x", step) for step in (1, 2, 3)]

    grad_fine, coarse_pack = run(
        coarse_kernel,
        [((nodes, feature), F32), ((2, 192, 256), F32)],
        [
            *pooleds, *pool_grads, coarse_src, coarse_dst, coarse_w1, coarse_w2, coarse_gain,
            cot, assign, column,
        ],
        [
            ((CNODE, feature), BF),
            ((coarse_edges, hidden), F32),
            ((coarse_edges, CNODE), BF),
            ((CNODE, coarse_edges), BF),
            ((CNODE, hidden), F32),
            ((CNODE, hidden), F32),
            ((CNODE, hidden), F32),
        ],
        scalars=(15,),
        late=(8, 9, 10, 11, 12, 13, 14),
        inner=(0, 1),
        limit=LIMITS[1],
    )

    local, give, keep, ghost_b, ghost_w, ghost_e = run(
        fine_backward_kernel,
        [
            ((nodes, feature), F32),
            ((960 + rim_count, 256), BF),
            ((960, 256), F32),
            ((rim_count, feature), BF),
            ((rim_count, feature), BF),
            ((rim_count, feature), BF),
        ],
        [
            grad_fine, summed, slope, acc, table, src, dst, live_blocks, core,
            fine_w1, fine_w2, fine_gain, coarse_pack,
        ],
        [
            ((nodes + 4 * rim_count, hidden), F32),
            ((nodes, hidden), F32),
            ((4 * rim_count, feature), BF),
        ],
        scalars=(7, 8),
        late=(5, 6, 9, 10, 11),
        inner=(0, 1, 2, 3, 4, 5),
        limit=LIMITS[2],
    )
    from_core = send(give, "core", 1)
    from_b = lax.ppermute(ghost_b, "row", between)
    half = keep + from_core[0:960].astype(F32)
    total, away = scatter_blocks(half[0:768], 4, place("x"))
    to_east = jnp.concatenate([away[0], ghost_e], axis=0)
    to_west = jnp.concatenate([away[2], ghost_w], axis=0)
    from_west = send(to_east, "x", 1)
    from_cross = send(away[1], "x", 2)
    from_east = send(to_west, "x", 3)
    total = (
        total
        + from_west[0:192].astype(F32)
        + from_cross.astype(F32)
        + from_east[0:192].astype(F32)
    )
    both = jnp.concatenate([total.reshape(4, 48, 256), half[768:].reshape(4, 48, 256)], axis=1)
    total, away = scatter_blocks(both.reshape(384, 256), 4, place("y"))
    for got in [send(block, "y", step) for step, block in enumerate(away, 1)]:
        total = total + got.astype(F32)
    (grad_latent,) = run(
        return_kernel,
        [((nodes, feature), F32)],
        [local, from_core, from_b, from_west, from_east, export, column],
        scalars=(6,),
        late=(5,),
    )
    total, grad_latent = lax.optimization_barrier((total, grad_latent))
    part = all_sum(total, "z")
    part = collect(part, "y")
    part = collect(part, "x")
    other = send(part, "core", 1)
    unpack = functools.partial(
        unpack_kernel,
        fine_scale=1.0 / math.sqrt(edges * rows * cols),
        coarse_scale=1.0 / math.sqrt(coarse_edges * rows),
    )
    weight_grads = run(
        unpack,
        [
            ((2 * feature, hidden), F32),
            ((hidden, feature), F32),
            ((2 * feature, hidden), F32),
            ((hidden, feature), F32),
        ],
        [part, other, core],
        scalars=(2,),
    )
    return (grad_latent[None, None], *weight_grads)


def solution(mesh):
    placed = (
        P("row", "col", None, None),
        P("row", "col", None, None),
        P(),
        P(),
        P(),
        P(),
        P(),
        P(),
        P("row", "col", None),
        P("row", "col", None),
        P("row", "col"),
        P("row", "col", None),
        P("row", "col", None),
        P("row", None),
        P("row", None),
    )
    return jax.shard_map(
        shards,
        mesh=mesh,
        in_specs=placed,
        out_specs=(P("row", "col", None, None), P(), P(), P(), P()),
        check_vma=False,
    )
```

```python
import functools
import math

import jax
import jax.numpy as jnp
from jax import lax
from jax.experimental import pallas as pl
from jax.experimental.pallas import tpu as pltpu
from jax.sharding import Mesh
from jax.sharding import PartitionSpec as P

EPS = 1e-05
CNODE = 512
CHUNK = 1024
LIMITS = (20, 20, 36, 22)
BF = jnp.bfloat16
F32 = jnp.float32


def dot(left, right):
    return lax.dot_general(left, right, (((1,), (0,)), ((), ())), preferred_element_type=F32)


def dot_rt(left, right):
    return lax.dot_general(left, right, (((1,), (1,)), ((), ())), preferred_element_type=F32)


def dot_lt(left, right):
    return lax.dot_general(left, right, (((0,), (0,)), ((), ())), preferred_element_type=F32)


def halves(value):
    high = value.astype(BF)
    return high, (value - high.astype(F32)).astype(BF)


def spread_row(row):
    count = row.shape[1]
    return jnp.concatenate(
        [
            jnp.broadcast_to(row[:, at : at + 128], (128, 128)).T
            for at in range(0, count, 128)
        ],
        axis=0,
    )


def pick_matrix(row, width):
    column = spread_row(row)
    wide = jnp.concatenate([column] * (width // 128), axis=1)
    hit = wide == lax.broadcasted_iota(jnp.int32, wide.shape, 1)
    return jnp.where(hit, 1.0, 0.0).astype(BF)


def sum_matrix(row, width):
    shape = (width, row.shape[1])
    hit = lax.broadcasted_iota(jnp.int32, shape, 0) == row
    return jnp.where(hit, 1.0, 0.0).astype(BF)


def receivers_of(dst_ref, live_ref, at):
    row = dst_ref[:, at : at + CHUNK]
    slot = lax.broadcasted_iota(jnp.int32, row.shape, 1) + at
    return jnp.where(slot < 128 * live_ref[0, 0], row, -1)


def norm_of(summed):
    inverse = lax.rsqrt(jnp.mean(summed * summed, axis=-1, keepdims=True) + EPS)
    return inverse, summed * inverse


def summed_grad(grad_new, gain, summed):
    inverse, normed = norm_of(summed)
    grad_normed = grad_new * gain
    mean = jnp.mean(grad_normed * normed, axis=-1, keepdims=True)
    return (inverse * (grad_normed - normed * mean)).astype(BF)


def activations(preact):
    sig = jax.nn.sigmoid(preact)
    return (preact * sig).astype(BF), sig * (1.0 + preact * (1.0 - sig))


def start_kernel(own_ref, export_ref, cot_ref, assign_ref, rim_ref, pack_ref):
    rim_count = export_ref.shape[1]
    rim = dot(pick_matrix(export_ref[...], own_ref.shape[0]), own_ref[...]).astype(BF)
    rim_ref[...] = rim
    pack_ref[0:rim_count, :] = rim
    pool = sum_matrix(assign_ref[...], CNODE)
    pack_ref[rim_count : rim_count + CNODE, :] = dot(pool, cot_ref[...]).astype(BF)
    count = dot_rt(jnp.ones((16, pool.shape[1]), BF), pool)
    coarse_part = jnp.floor(count * (1.0 / 256.0)) * 256.0
    upper = lax.broadcasted_iota(jnp.int32, count.shape, 0) < 8
    packed = jnp.where(upper, coarse_part, count - coarse_part).astype(BF)
    at = rim_count + CNODE
    pack_ref[at : at + 16, :] = packed[:, :256]
    pack_ref[at + 16 : at + 32, :] = packed[:, 256:]


def own_kernel(own_ref, src_ref, dst_ref, live_ref, w1_ref, part_ref):
    nodes, feature = own_ref.shape
    for at in range(0, src_ref.shape[1], CHUNK):
        here = slice(at, at + CHUNK)
        left = dot(pick_matrix(src_ref[:, here], nodes), own_ref[...]).astype(BF)
        target = receivers_of(dst_ref, live_ref, at)
        right = dot(pick_matrix(target, nodes), own_ref[...]).astype(BF)
        part_ref[here, :] = dot(left, w1_ref[0:feature, :]) + dot(right, w1_ref[feature:, :])


def fine_forward_kernel(
    part_ref, own_ref, ra, rb, rw, re, src_ref, dst_ref, live_ref, core_ref, col_ref,
    w1_ref, w2_ref, gain_ref, assign_ref, slope_ref, acc_out, summed_ref, pooled_ref, table, acc,
):
    nodes, feature = own_ref.shape
    rim = ra.shape[0]
    core, col = core_ref[0], col_ref[0]
    table[0:nodes, :] = own_ref[...]
    table[pl.ds(pl.multiple_of(nodes + rim * (1 - core), rim), rim), :] = ra[...]
    table[pl.ds(pl.multiple_of(nodes + rim * core, rim), rim), :] = rb[...]
    west = rw[0:rim, :].astype(F32) * jnp.where(col > 0, 1.0, 0.0)
    east = re[0:rim, :].astype(F32) * jnp.where(col < 3, 1.0, 0.0)
    table[nodes + 2 * rim : nodes + 3 * rim, :] = west.astype(BF)
    table[nodes + 3 * rim :, :] = east.astype(BF)
    for at in range(0, src_ref.shape[1], CHUNK):
        here = slice(at, at + CHUNK)
        picks = pick_matrix(src_ref[:, here] - nodes, 4 * rim)
        left = dot(picks, table[nodes:, :]).astype(BF)
        preact = part_ref[here, :] + dot(left, w1_ref[0:feature, :])
        hidden, slope = activations(preact)
        slope_ref[here, :] = slope
        part = dot(sum_matrix(receivers_of(dst_ref, live_ref, at), nodes), hidden)
        if at == 0:
            acc[...] = part
        else:
            acc[...] += part
    high, low = halves(acc[...])
    acc_out[...] = high
    summed = dot(high, w2_ref[...]) + dot(low, w2_ref[...])
    summed_ref[...] = summed
    _, normed = norm_of(summed)
    fine_new = own_ref[...].astype(F32) + normed * gain_ref[...]
    high, low = halves(fine_new)
    pool = sum_matrix(assign_ref[...], CNODE)
    pooled_ref[...] = (dot(pool, high) + dot(pool, low)).astype(BF)


def coarse_kernel(
    p0, p1, p2, p3, p4, g0, g1, g2, g3, src_ref, dst_ref, w1_ref, w2_ref, gain_ref, cot_ref,
    assign_ref, col_ref, grad_fine_ref, pack_ref,
    table, slope, pick_t, sum_t, acc, by_src, by_dst,
):
    feature = p0.shape[1]
    edges = src_ref.shape[1]
    grads = []
    count = None
    for ref in (g0, g1, g2, g3):
        skip = ref.shape[0] - CNODE - 32
        grads.append(ref[skip : skip + CNODE, :].astype(F32))
        tail = ref[skip + CNODE :, :].astype(F32)
        tail = [tail[at : at + 1, :] + tail[at + 8 : at + 9, :] for at in (0, 16)]
        tail = jnp.concatenate(tail, axis=1)
        count = tail if count is None else count + tail
    grad_c1 = (grads[0] + grads[1]) + (grads[2] + grads[3])
    weight = spread_row(1.0 / jnp.maximum(count, 1.0))
    weight = jnp.concatenate([weight] * (feature // 128), axis=1)
    across = jnp.concatenate([p3[...].astype(F32), p4[...].astype(F32)], axis=0)
    pooled = (p0[...].astype(F32) + p1[...].astype(F32)) + (p2[...].astype(F32) + across)
    table[...] = (pooled * weight).astype(BF)
    for at in range(0, edges, CHUNK):
        here = slice(at, at + CHUNK)
        left = dot(pick_matrix(src_ref[:, here], CNODE), table[...]).astype(BF)
        pick = pick_matrix(dst_ref[:, here], CNODE)
        pick_t[here, :] = pick
        right = dot(pick, table[...]).astype(BF)
        preact = dot(left, w1_ref[0:feature, :]) + dot(right, w1_ref[feature:, :])
        hidden, slope[here, :] = activations(preact)
        adds = sum_matrix(dst_ref[:, here], CNODE)
        sum_t[:, here] = adds
        part = dot(adds, hidden)
        if at == 0:
            acc[...] = part
        else:
            acc[...] += part
    high, low = halves(acc[...])
    summed = dot(high, w2_ref[...]) + dot(low, w2_ref[...])
    grad_summed = summed_grad(grad_c1, gain_ref[...], summed)
    for at in range(0, edges, CHUNK):
        here = slice(at, at + CHUNK)
        grad_message = dot(pick_t[here, :], grad_summed).astype(BF)
        grad_preact = (dot_rt(grad_message, w2_ref[...]) * slope[here, :]).astype(BF)
        part_src = dot(sum_matrix(src_ref[:, here], CNODE), grad_preact)
        part_dst = dot(sum_t[:, here], grad_preact)
        if at == 0:
            by_src[...] = part_src
            by_dst[...] = part_dst
        else:
            by_src[...] += part_src
            by_dst[...] += part_dst
    grad_c0 = (
        grad_c1
        + dot_rt(by_src[...].astype(BF), w1_ref[0:feature, :])
        + dot_rt(by_dst[...].astype(BF), w1_ref[feature:, :])
    )
    high, low = halves(grad_c0 * weight)
    spread = pick_matrix(assign_ref[...], CNODE)
    grad_fine_ref[...] = cot_ref[...].astype(F32) + dot(spread, high) + dot(spread, low)
    own = pl.ds(pl.multiple_of(col_ref[0] * 128, 128), 128)
    for half, rows in enumerate((by_src, by_dst)):
        pack_ref[half, 0:256, :] = dot_lt(table[...], rows[:, own].astype(BF))
    second = dot_lt(acc[:, own].astype(BF), grad_summed)
    for half in range(2):
        for k in range(2):
            pack_ref[half, 256 + 64 * k : 320 + 64 * k, :] = second[
                64 * half : 64 * half + 64, 128 * k : 128 * k + 128
            ]


def fine_backward_kernel(
    grad_fine_ref, summed_ref, slope_ref, acc_ref, table_ref, src_ref, dst_ref,
    live_ref, core_ref, w1_ref, w2_ref, gain_ref, coarse_ref,
    local_ref, give_ref, keep_ref, ghost_b, ghost_w, ghost_e, by_src, by_dst, ghost,
):
    nodes, feature = grad_fine_ref.shape
    rim = ghost_b.shape[0]
    core = core_ref[0]
    grad_fine = grad_fine_ref[...]
    grad_summed = summed_grad(grad_fine, gain_ref[...], summed_ref[...])
    for at in range(0, src_ref.shape[1], CHUNK):
        here = slice(at, at + CHUNK)
        target = receivers_of(dst_ref, live_ref, at)
        grad_message = dot(pick_matrix(target, nodes), grad_summed).astype(BF)
        grad_preact = (dot_rt(grad_message, w2_ref[...]) * slope_ref[here, :]).astype(BF)
        part_src = dot(sum_matrix(src_ref[:, here], table_ref.shape[0]), grad_preact)
        part_dst = dot(sum_matrix(target, nodes), grad_preact)
        if at == 0:
            by_src[...] = part_src
            by_dst[...] = part_dst
        else:
            by_src[...] += part_src
            by_dst[...] += part_dst
    grad_table = dot_rt(by_src[...].astype(BF), w1_ref[0:feature, :])
    local_ref[...] = (
        grad_fine
        + grad_table[0:nodes, :]
        + dot_rt(by_dst[...].astype(BF), w1_ref[feature:, :])
    )
    ghost[...] = grad_table[nodes:, :].astype(BF)
    to_core = ghost[pl.ds(pl.multiple_of(rim * (1 - core), rim), rim), :]
    give_ref[1920 : 1920 + rim, :] = to_core[:, 0:128]
    give_ref[1920 + rim :, :] = to_core[:, 128:256]
    ghost_b[...] = ghost[pl.ds(pl.multiple_of(rim * core, rim), rim), :]
    for out, at in ((ghost_w, 2 * rim), (ghost_e, 3 * rim)):
        out[0:rim, :] = ghost[at : at + rim, 0:128]
        out[rim:, :] = ghost[at : at + rim, 128:256]
    for out, half in ((give_ref, 1 - core), (keep_ref, core)):
        part = pl.ds(pl.multiple_of(half * 256, 256), 256)
        first = dot_lt(table_ref[...], by_src[:, part].astype(BF)).astype(out.dtype)
        second = dot_lt(table_ref[0:nodes, :], by_dst[:, part].astype(BF)).astype(out.dtype)
        third = dot_lt(acc_ref[:, part], grad_summed).astype(out.dtype)
        for k in range(2):
            lanes = slice(128 * k, 128 * k + 128)
            out[512 * k : 512 * k + 256, :] = first[:, lanes]
            out[512 * k + 256 : 512 * k + 512, :] = second[:, lanes]
            out[1024 + 256 * k : 1280 + 256 * k, :] = third[:, lanes]
        out[1536:1920, :] = coarse_ref[half].astype(out.dtype)


def split_kernel(keep_ref, got_ref, ghost_w, ghost_e, col_ref, total_ref, coarse_ref, *sends):
    col = col_ref[0]

    def block(step):
        rows = pl.ds(pl.multiple_of(lax.rem(col + step, 4) * 384, 384), 384)
        return keep_ref[rows, :] + got_ref[rows, :].astype(F32)

    total_ref[...] = block(0)
    coarse_ref[...] = keep_ref[1536:1920, :] + got_ref[1536:1920, :].astype(F32)
    for step, out in enumerate(sends, 1):
        out[0:384, :] = block(step).astype(BF)
    sends[0][384:, :] = ghost_e[...]
    sends[2][384:, :] = ghost_w[...]


def return_kernel(local_ref, from_core, from_b, from_west, from_east, export_ref, col_ref, out_ref):
    rim = export_ref.shape[1]
    adds = sum_matrix(export_ref[...], local_ref.shape[0])
    col = col_ref[0]

    def wide(ref):
        at = ref.shape[0] - 2 * rim
        rows = ref[at:, :].astype(F32)
        return jnp.concatenate([rows[0:rim, :], rows[rim:, :]], axis=1)

    west = wide(from_west) * jnp.where(col > 0, 1.0, 0.0)
    east = wide(from_east) * jnp.where(col < 3, 1.0, 0.0)
    arrived = (wide(from_core) + from_b[...].astype(F32)) + (west + east)
    high, low = halves(arrived)
    out_ref[...] = local_ref[...] + dot(adds, high) + dot(adds, low)


def unpack_kernel(
    mine_ref, other_ref, core_ref, fine1_ref, fine2_ref, coarse1_ref, coarse2_ref,
    *, fine_scale, coarse_scale,
):
    for ref, half in ((mine_ref, core_ref[0]), (other_ref, 1 - core_ref[0])):
        for plane in range(16):
            for x in range(4):
                values = ref[plane * 4 + x].astype(F32)
                for at in range(0, 24, 8):
                    row = x * 384 + plane * 24 + at
                    piece = values[at : at + 8, :] * fine_scale
                    if row < 1024:
                        lanes = pl.ds(pl.multiple_of(half * 256 + row // 512 * 128, 128), 128)
                        fine1_ref[row % 512 : row % 512 + 8, lanes] = piece
                    else:
                        start = pl.multiple_of(half * 256 + row % 256, 8)
                        lane = (row - 1024) // 256 * 128
                        fine2_ref[pl.ds(start, 8), lane : lane + 128] = piece
                    row = plane * 24 + at
                    piece = values[24 + at : 32 + at, :] * coarse_scale
                    if row < 256:
                        start = pl.multiple_of(half * 256 + row, 8)
                        coarse1_ref[pl.ds(start, 8), x * 128 : x * 128 + 128] = piece
                    else:
                        start = pl.multiple_of(half * 64 + x * 128 + row % 64, 8)
                        lane = (row - 256) // 64 * 128
                        coarse2_ref[pl.ds(start, 8), lane : lane + 128] = piece


class Late:
    def __init__(self, source, held, sem):
        self.held = held
        self.shape = held.shape
        self.copy = pltpu.make_async_copy(source, held, sem)
        self.copy.start()

    def __getitem__(self, index):
        if self.copy is not None:
            self.copy.wait()
            self.copy = None
        return self.held[index]

    def finish(self):
        if self.copy is not None:
            self.copy.wait()
            self.copy = None


def run(kernel, outs, operands, scratch=(), scalars=(), late=(), inner=(), ahead=(), limit=16):
    size = sum(math.prod(x.shape) * x.dtype.itemsize for x in [*operands, *ahead]) + sum(
        math.prod(shape) * jnp.dtype(kind).itemsize for shape, kind in outs
    )
    shapes = [
        (pltpu.VMEM if i in inner else jax.ShapeDtypeStruct)(shape, kind)
        for i, (shape, kind) in enumerate(outs)
    ] + [pltpu.VMEM(x.shape, x.dtype) for x in ahead]
    operands = [
        pltpu.with_memory_space_constraint(x, pltpu.HBM) if i in late else x
        for i, x in enumerate(operands)
    ] + [pltpu.with_memory_space_constraint(x, pltpu.HBM) for x in ahead]
    count = len(operands) - len(ahead)
    first_out = len(operands)
    first_ahead = first_out + len(outs)
    first_scratch = first_ahead + len(ahead)
    first_held = first_scratch + len(scratch)

    def space(i):
        return pltpu.SMEM if i in scalars else pltpu.HBM if i in late or i >= count else pltpu.VMEM

    def body(*refs):
        sems = refs[-1]
        inputs = list(refs[:count])
        for k, i in enumerate(late):
            inputs[i] = Late(refs[i], refs[first_held + k], sems.at[k])
        fetched = [
            Late(refs[count + k], refs[first_ahead + k], sems.at[len(late) + k])
            for k in range(len(ahead))
        ]
        kernel(*inputs, *refs[first_out:first_ahead], *refs[first_scratch:first_held])
        for copy in [inputs[i] for i in late] + fetched:
            copy.finish()

    copies = len(late) + len(ahead)
    return pl.pallas_call(
        body if copies else kernel,
        out_shape=shapes,
        in_specs=[pl.BlockSpec(memory_space=space(i)) for i in range(first_out)],
        out_specs=[pl.BlockSpec(memory_space=pltpu.VMEM)] * len(shapes),
        scratch_shapes=[pltpu.VMEM(shape, kind) for shape, kind in scratch]
        + [pltpu.VMEM(operands[i].shape, operands[i].dtype) for i in late]
        + ([pltpu.SemaphoreType.DMA((copies,))] if copies else []),
        compiler_params=pltpu.CompilerParams(vmem_limit_bytes=limit * 1024 * 1024),
        cost_estimate=pl.CostEstimate(flops=0, bytes_accessed=size, transcendentals=0),
    )(*operands)


ROW = ("z", "y", "core")
PLANE = ("z", "y")
CHIPS = ("z", "y", "x")


def send(value, axis, step):
    size = lax.axis_size(axis)
    return lax.ppermute(value, axis, [(i, (i + step) % size) for i in range(size)])


def shards(
    latent, cotangent, fine_w1, fine_w2, fine_gain, coarse_w1, coarse_w2, coarse_gain,
    fine_src, fine_dst, live_blocks, export_rows, pool_assign, coarse_src, coarse_dst,
):
    own = latent[0, 0]
    cot = cotangent[0, 0]
    nodes, feature = own.shape
    export = export_rows[0]
    assign = pool_assign[0]
    src, dst = fine_src[0], fine_dst[0]
    rim_count = export.shape[1]
    hidden = fine_w1.shape[1]
    edges, coarse_edges = src.shape[1], coarse_src.shape[1]
    rows, cols = lax.axis_size(ROW), lax.axis_size("x")
    fine_gain = fine_gain[None, :]
    coarse_gain = coarse_gain[None, :]
    between = [(i, i + 1) for i in range(1, rows - 1, 2)]
    between = between + [(target, source) for source, target in between]
    column = lax.axis_index("x").astype(jnp.int32)[None]
    core = lax.axis_index("core").astype(jnp.int32)[None]
    own, column, core = lax.optimization_barrier((own, column, core))
    wide = 2 * feature

    rim, pack, own_in, src_in, dst_in, w1_in, w2_in, gain_in, assign_in, export_in = run(
        start_kernel,
        [((rim_count, feature), BF), ((rim_count + CNODE + 32, feature), BF)],
        [own, export, cot, assign],
        late=(0, 1, 2, 3),
        inner=(0, 1),
        ahead=[own, src, dst, fine_w1, fine_w2, fine_gain, assign, export],
    )
    from_a = send(rim, "core", 1)
    from_b = lax.ppermute(rim, ROW, between)
    packs = [pack, send(pack, "x", 1), send(pack, "x", 3), send(pack[rim_count:], "x", 2)]
    part, csrc_in, cdst_in, cw1_in, cw2_in, cgain_in, cot_in = run(
        own_kernel,
        [((edges, hidden), F32)],
        [own_in, src_in, dst_in, live_blocks, w1_in],
        scalars=(3,),
        inner=(0,),
        ahead=[coarse_src, coarse_dst, coarse_w1, coarse_w2, coarse_gain, cot],
        limit=LIMITS[0],
    )
    slope, acc, summed, pooled, table = run(
        fine_forward_kernel,
        [
            ((edges, hidden), F32),
            ((nodes, hidden), BF),
            ((nodes, feature), F32),
            ((CNODE, feature), BF),
            ((nodes + 4 * rim_count, feature), BF),
        ],
        [
            part, own_in, from_a, from_b, packs[1], packs[2], src_in, dst_in, live_blocks, core,
            column, w1_in, w2_in, gain_in, assign_in,
        ],
        [((nodes, hidden), F32)],
        scalars=(8, 9, 10),
        inner=(0, 1, 2, 3, 4),
        limit=LIMITS[1],
    )
    half_rows = CNODE // 2
    left, right = send(pooled, "x", 1), send(pooled, "x", 3)
    across = [send(left[:half_rows], "x", 1), send(right[half_rows:], "x", 3)]

    grad_fine, coarse_pack = run(
        coarse_kernel,
        [((nodes, feature), F32), ((2, 384, 128), F32)],
        [
            pooled, left, right, *across, *packs, csrc_in, cdst_in, cw1_in, cw2_in, cgain_in,
            cot_in, assign_in, column,
        ],
        [
            ((CNODE, feature), BF),
            ((coarse_edges, hidden), F32),
            ((coarse_edges, CNODE), BF),
            ((CNODE, coarse_edges), BF),
            ((CNODE, hidden), F32),
            ((CNODE, hidden), F32),
            ((CNODE, hidden), F32),
        ],
        scalars=(16,),
        inner=(0, 1),
        limit=LIMITS[2],
    )

    local, give, keep, ghost_b, ghost_w, ghost_e = run(
        fine_backward_kernel,
        [
            ((nodes, feature), F32),
            ((1920 + 2 * rim_count, 128), BF),
            ((1920, 128), F32),
            ((rim_count, feature), BF),
            ((2 * rim_count, 128), BF),
            ((2 * rim_count, 128), BF),
        ],
        [
            grad_fine, summed, slope, acc, table, src_in, dst_in, live_blocks, core,
            w1_in, w2_in, gain_in, coarse_pack,
        ],
        [
            ((nodes + 4 * rim_count, hidden), F32),
            ((nodes, hidden), F32),
            ((4 * rim_count, feature), BF),
        ],
        scalars=(7, 8),
        inner=(0, 1, 2, 3, 4, 5),
        limit=LIMITS[3],
    )
    from_core = send(give, "core", 1)
    from_b = lax.ppermute(ghost_b, ROW, between)
    total, coarse_total, to_east, to_cross, to_west = run(
        split_kernel,
        [
            ((384, 128), F32),
            ((384, 128), F32),
            ((384 + 2 * rim_count, 128), BF),
            ((384, 128), BF),
            ((384 + 2 * rim_count, 128), BF),
        ],
        [keep, from_core, ghost_w, ghost_e, column],
        scalars=(4,),
        inner=(0, 1, 2, 3, 4),
    )
    from_west = send(to_east, "x", 1)
    from_cross = send(to_cross, "x", 2)
    from_east = send(to_west, "x", 3)
    total = (
        total
        + from_west[0:384].astype(F32)
        + from_cross.astype(F32)
        + from_east[0:384].astype(F32)
    )
    both = jnp.concatenate(
        [total.reshape(16, 24, 128), coarse_total.reshape(16, 24, 128)], axis=1
    ).astype(BF)
    both = lax.all_to_all(both, PLANE, 0, 0, tiled=True)
    both = jnp.sum(both.astype(F32), axis=0).astype(BF)
    copies = jnp.broadcast_to(both[None], (64,) + both.shape)
    mine = lax.all_to_all(copies, CHIPS, 0, 0, tiled=True)
    mine, local = lax.optimization_barrier((mine, local))
    other = send(mine, "core", 1)
    (grad_latent,) = run(
        return_kernel,
        [((nodes, feature), F32)],
        [local, from_core, from_b, from_west, from_east, export_in, column],
        scalars=(6,),
    )
    unpack = functools.partial(
        unpack_kernel,
        fine_scale=1.0 / math.sqrt(edges * rows * cols),
        coarse_scale=1.0 / math.sqrt(coarse_edges * rows),
    )
    weight_grads = run(
        unpack,
        [
            ((2 * feature, hidden), F32),
            ((hidden, feature), F32),
            ((2 * feature, hidden), F32),
            ((hidden, feature), F32),
        ],
        [mine, other, core],
        scalars=(2,),
    )
    return (grad_latent[None, None], *weight_grads)


def solution(mesh):
    shape = (4, 4, 2, 4)
    inner = Mesh(mesh.devices.reshape(shape), ("z", "y", "core", "x"))
    node_sharded = P(ROW, "x", None, None)
    index_sharded = P(ROW, "x", None)
    placed = (
        node_sharded,
        node_sharded,
        P(),
        P(),
        P(),
        P(),
        P(),
        P(),
        index_sharded,
        index_sharded,
        P(ROW, "x"),
        index_sharded,
        index_sharded,
        P(ROW, None),
        P(ROW, None),
    )
    return jax.shard_map(
        shards,
        mesh=inner,
        in_specs=placed,
        out_specs=(node_sharded, P(), P(), P(), P()),
        check_vma=False,
    )
```

```python
import functools
import math

import jax
import jax.numpy as jnp
from jax import lax
from jax.experimental import pallas as pl
from jax.experimental.pallas import tpu as pltpu
from jax.sharding import Mesh
from jax.sharding import PartitionSpec as P

EPS = 1e-05
CNODE = 512
CHUNK = 1024
LIMITS = (20, 20, 36, 22)
BF = jnp.bfloat16
F32 = jnp.float32


def dot(left, right):
    return lax.dot_general(left, right, (((1,), (0,)), ((), ())), preferred_element_type=F32)


def dot_rt(left, right):
    return lax.dot_general(left, right, (((1,), (1,)), ((), ())), preferred_element_type=F32)


def dot_lt(left, right):
    return lax.dot_general(left, right, (((0,), (0,)), ((), ())), preferred_element_type=F32)


def halves(value):
    high = value.astype(BF)
    return high, (value - high.astype(F32)).astype(BF)


def spread_row(row):
    count = row.shape[1]
    return jnp.concatenate(
        [
            jnp.broadcast_to(row[:, at : at + 128], (128, 128)).T
            for at in range(0, count, 128)
        ],
        axis=0,
    )


def pick_matrix(row, width):
    column = spread_row(row)
    wide = jnp.concatenate([column] * (width // 128), axis=1)
    hit = wide == lax.broadcasted_iota(jnp.int32, wide.shape, 1)
    return jnp.where(hit, 1.0, 0.0).astype(BF)


def sum_matrix(row, width):
    shape = (width, row.shape[1])
    hit = lax.broadcasted_iota(jnp.int32, shape, 0) == row
    return jnp.where(hit, 1.0, 0.0).astype(BF)


def norm_of(summed):
    inverse = lax.rsqrt(jnp.mean(summed * summed, axis=-1, keepdims=True) + EPS)
    return inverse, summed * inverse


def summed_grad(grad_new, gain, summed):
    inverse, normed = norm_of(summed)
    grad_normed = grad_new * gain
    mean = jnp.mean(grad_normed * normed, axis=-1, keepdims=True)
    return (inverse * (grad_normed - normed * mean)).astype(BF)


def activations(preact):
    sig = jax.nn.sigmoid(preact)
    return (preact * sig).astype(BF), sig * (1.0 + preact * (1.0 - sig))


def start_kernel(
    own_ref, export_ref, cot_ref, assign_ref, dst_ref, place_ref, rim_ref, pack_ref, target_ref
):
    rim_count = export_ref.shape[1]
    rim = dot(pick_matrix(export_ref[...], own_ref.shape[0]), own_ref[...]).astype(BF)
    rim_ref[...] = rim
    pack_ref[0:rim_count, :] = rim
    pool = sum_matrix(assign_ref[...], CNODE)
    pack_ref[rim_count : rim_count + CNODE, :] = dot(pool, cot_ref[...]).astype(BF)
    count = dot_rt(jnp.ones((16, pool.shape[1]), BF), pool)
    coarse_part = jnp.floor(count * (1.0 / 256.0)) * 256.0
    upper = lax.broadcasted_iota(jnp.int32, count.shape, 0) < 8
    packed = jnp.where(upper, coarse_part, count - coarse_part).astype(BF)
    at = rim_count + CNODE
    pack_ref[at : at + 16, :] = packed[:, :256]
    pack_ref[at + 16 : at + 32, :] = packed[:, 256:]
    slot = lax.broadcasted_iota(jnp.int32, dst_ref.shape, 1)
    target_ref[...] = jnp.where(slot < place_ref[2], dst_ref[...], -1)


def own_kernel(own_ref, src_ref, target_ref, w1_ref, part_ref):
    nodes, feature = own_ref.shape
    for at in range(0, src_ref.shape[1], CHUNK):
        here = slice(at, at + CHUNK)
        left = dot(pick_matrix(src_ref[:, here], nodes), own_ref[...]).astype(BF)
        right = dot(pick_matrix(target_ref[:, here], nodes), own_ref[...]).astype(BF)
        part_ref[here, :] = dot(left, w1_ref[0:feature, :]) + dot(right, w1_ref[feature:, :])


def fine_forward_kernel(
    part_ref, own_ref, ra, rb, rw, re, src_ref, target_ref, place_ref,
    w1_ref, w2_ref, gain_ref, assign_ref, slope_ref, acc_out, summed_ref, pooled_ref, table, acc,
):
    nodes, feature = own_ref.shape
    rim = ra.shape[0]
    col, core = place_ref[0], place_ref[1]
    table[0:nodes, :] = own_ref[...]
    table[pl.ds(pl.multiple_of(nodes + rim * (1 - core), rim), rim), :] = ra[...]
    table[pl.ds(pl.multiple_of(nodes + rim * core, rim), rim), :] = rb[...]
    west = rw[0:rim, :].astype(F32) * jnp.where(col > 0, 1.0, 0.0)
    east = re[0:rim, :].astype(F32) * jnp.where(col < 3, 1.0, 0.0)
    table[nodes + 2 * rim : nodes + 3 * rim, :] = west.astype(BF)
    table[nodes + 3 * rim :, :] = east.astype(BF)
    for at in range(0, src_ref.shape[1], CHUNK):
        here = slice(at, at + CHUNK)
        picks = pick_matrix(src_ref[:, here] - nodes, 4 * rim)
        left = dot(picks, table[nodes:, :]).astype(BF)
        preact = part_ref[here, :] + dot(left, w1_ref[0:feature, :])
        hidden, slope = activations(preact)
        slope_ref[here, :] = slope
        part = dot(sum_matrix(target_ref[:, here], nodes), hidden)
        if at == 0:
            acc[...] = part
        else:
            acc[...] += part
    high, low = halves(acc[...])
    acc_out[...] = high
    summed = dot(high, w2_ref[...]) + dot(low, w2_ref[...])
    summed_ref[...] = summed
    _, normed = norm_of(summed)
    fine_new = own_ref[...].astype(F32) + normed * gain_ref[...]
    high, low = halves(fine_new)
    pool = sum_matrix(assign_ref[...], CNODE)
    pooled_ref[...] = (dot(pool, high) + dot(pool, low)).astype(BF)


def coarse_kernel(
    p0, p1, p2, p3, p4, g0, g1, g2, g3, src_ref, dst_ref, w1_ref, w2_ref, gain_ref, cot_ref,
    assign_ref, place_ref, grad_fine_ref, pack_ref,
    table, slope, pick_t, sum_t, acc, by_src, by_dst,
):
    feature = p0.shape[1]
    edges = src_ref.shape[1]
    grads = []
    count = None
    for ref in (g0, g1, g2, g3):
        skip = ref.shape[0] - CNODE - 32
        grads.append(ref[skip : skip + CNODE, :].astype(F32))
        tail = ref[skip + CNODE :, :].astype(F32)
        tail = [tail[at : at + 1, :] + tail[at + 8 : at + 9, :] for at in (0, 16)]
        tail = jnp.concatenate(tail, axis=1)
        count = tail if count is None else count + tail
    grad_c1 = (grads[0] + grads[1]) + (grads[2] + grads[3])
    weight = spread_row(1.0 / jnp.maximum(count, 1.0))
    weight = jnp.concatenate([weight] * (feature // 128), axis=1)
    across = jnp.concatenate([p3[...].astype(F32), p4[...].astype(F32)], axis=0)
    pooled = (p0[...].astype(F32) + p1[...].astype(F32)) + (p2[...].astype(F32) + across)
    table[...] = (pooled * weight).astype(BF)
    for at in range(0, edges, CHUNK):
        here = slice(at, at + CHUNK)
        left = dot(pick_matrix(src_ref[:, here], CNODE), table[...]).astype(BF)
        pick = pick_matrix(dst_ref[:, here], CNODE)
        pick_t[here, :] = pick
        right = dot(pick, table[...]).astype(BF)
        preact = dot(left, w1_ref[0:feature, :]) + dot(right, w1_ref[feature:, :])
        hidden, slope[here, :] = activations(preact)
        adds = sum_matrix(dst_ref[:, here], CNODE)
        sum_t[:, here] = adds
        part = dot(adds, hidden)
        if at == 0:
            acc[...] = part
        else:
            acc[...] += part
    high, low = halves(acc[...])
    summed = dot(high, w2_ref[...]) + dot(low, w2_ref[...])
    grad_summed = summed_grad(grad_c1, gain_ref[...], summed)
    for at in range(0, edges, CHUNK):
        here = slice(at, at + CHUNK)
        grad_message = dot(pick_t[here, :], grad_summed).astype(BF)
        grad_preact = (dot_rt(grad_message, w2_ref[...]) * slope[here, :]).astype(BF)
        part_src = dot(sum_matrix(src_ref[:, here], CNODE), grad_preact)
        part_dst = dot(sum_t[:, here], grad_preact)
        if at == 0:
            by_src[...] = part_src
            by_dst[...] = part_dst
        else:
            by_src[...] += part_src
            by_dst[...] += part_dst
    grad_c0 = (
        grad_c1
        + dot_rt(by_src[...].astype(BF), w1_ref[0:feature, :])
        + dot_rt(by_dst[...].astype(BF), w1_ref[feature:, :])
    )
    high, low = halves(grad_c0 * weight)
    spread = pick_matrix(assign_ref[...], CNODE)
    grad_fine_ref[...] = cot_ref[...].astype(F32) + dot(spread, high) + dot(spread, low)
    own = pl.ds(pl.multiple_of(place_ref[0] * 128, 128), 128)
    for half, rows in enumerate((by_src, by_dst)):
        pack_ref[half, 0:256, :] = dot_lt(table[...], rows[:, own].astype(BF))
    second = dot_lt(acc[:, own].astype(BF), grad_summed)
    for half in range(2):
        for k in range(2):
            pack_ref[half, 256 + 64 * k : 320 + 64 * k, :] = second[
                64 * half : 64 * half + 64, 128 * k : 128 * k + 128
            ]


def fine_backward_kernel(
    grad_fine_ref, summed_ref, slope_ref, acc_ref, table_ref, src_ref, target_ref,
    place_ref, w1_ref, w2_ref, gain_ref, coarse_ref,
    local_ref, give_ref, keep_ref, ghost_b, ghost_w, ghost_e, by_src, by_dst, ghost,
):
    nodes, feature = grad_fine_ref.shape
    rim = ghost_b.shape[0]
    core = place_ref[1]
    grad_fine = grad_fine_ref[...]
    grad_summed = summed_grad(grad_fine, gain_ref[...], summed_ref[...])
    for at in range(0, src_ref.shape[1], CHUNK):
        here = slice(at, at + CHUNK)
        target = target_ref[:, here]
        grad_message = dot(pick_matrix(target, nodes), grad_summed).astype(BF)
        grad_preact = (dot_rt(grad_message, w2_ref[...]) * slope_ref[here, :]).astype(BF)
        part_src = dot(sum_matrix(src_ref[:, here], table_ref.shape[0]), grad_preact)
        part_dst = dot(sum_matrix(target, nodes), grad_preact)
        if at == 0:
            by_src[...] = part_src
            by_dst[...] = part_dst
        else:
            by_src[...] += part_src
            by_dst[...] += part_dst
    grad_table = dot_rt(by_src[...].astype(BF), w1_ref[0:feature, :])
    local_ref[...] = (
        grad_fine
        + grad_table[0:nodes, :]
        + dot_rt(by_dst[...].astype(BF), w1_ref[feature:, :])
    )
    ghost[...] = grad_table[nodes:, :].astype(BF)
    to_core = ghost[pl.ds(pl.multiple_of(rim * (1 - core), rim), rim), :]
    give_ref[1920 : 1920 + rim, :] = to_core[:, 0:128]
    give_ref[1920 + rim :, :] = to_core[:, 128:256]
    ghost_b[...] = ghost[pl.ds(pl.multiple_of(rim * core, rim), rim), :]
    for out, at in ((ghost_w, 2 * rim), (ghost_e, 3 * rim)):
        out[0:rim, :] = ghost[at : at + rim, 0:128]
        out[rim:, :] = ghost[at : at + rim, 128:256]
    for out, half in ((give_ref, 1 - core), (keep_ref, core)):
        part = pl.ds(pl.multiple_of(half * 256, 256), 256)
        first = dot_lt(table_ref[...], by_src[:, part].astype(BF)).astype(out.dtype)
        second = dot_lt(table_ref[0:nodes, :], by_dst[:, part].astype(BF)).astype(out.dtype)
        third = dot_lt(acc_ref[:, part], grad_summed).astype(out.dtype)
        for k in range(2):
            lanes = slice(128 * k, 128 * k + 128)
            out[512 * k : 512 * k + 256, :] = first[:, lanes]
            out[512 * k + 256 : 512 * k + 512, :] = second[:, lanes]
            out[1024 + 256 * k : 1280 + 256 * k, :] = third[:, lanes]
        out[1536:1920, :] = coarse_ref[half].astype(out.dtype)


def split_kernel(keep_ref, got_ref, ghost_w, ghost_e, place_ref, total_ref, coarse_ref, *sends):
    col = place_ref[0]

    def block(step):
        rows = pl.ds(pl.multiple_of(lax.rem(col + step, 4) * 384, 384), 384)
        return keep_ref[rows, :] + got_ref[rows, :].astype(F32)

    total_ref[...] = block(0)
    coarse_ref[...] = keep_ref[1536:1920, :] + got_ref[1536:1920, :].astype(F32)
    for step, out in enumerate(sends, 1):
        out[0:384, :] = block(step).astype(BF)
    sends[0][384:, :] = ghost_e[...]
    sends[2][384:, :] = ghost_w[...]


def return_kernel(local_ref, from_core, from_b, from_west, from_east, export_ref, place_ref, out_ref):
    rim = export_ref.shape[1]
    adds = sum_matrix(export_ref[...], local_ref.shape[0])
    col = place_ref[0]

    def wide(ref):
        at = ref.shape[0] - 2 * rim
        rows = ref[at:, :].astype(F32)
        return jnp.concatenate([rows[0:rim, :], rows[rim:, :]], axis=1)

    west = wide(from_west) * jnp.where(col > 0, 1.0, 0.0)
    east = wide(from_east) * jnp.where(col < 3, 1.0, 0.0)
    arrived = (wide(from_core) + from_b[...].astype(F32)) + (west + east)
    high, low = halves(arrived)
    out_ref[...] = local_ref[...] + dot(adds, high) + dot(adds, low)


def unpack_kernel(
    mine_ref, other_ref, place_ref, fine1_ref, fine2_ref, coarse1_ref, coarse2_ref,
    *, fine_scale, coarse_scale,
):
    for ref, half in ((mine_ref, place_ref[1]), (other_ref, 1 - place_ref[1])):
        for plane in range(16):
            for x in range(4):
                values = ref[plane * 4 + x].astype(F32)
                for at in range(0, 24, 8):
                    row = x * 384 + plane * 24 + at
                    piece = values[at : at + 8, :] * fine_scale
                    if row < 1024:
                        lanes = pl.ds(pl.multiple_of(half * 256 + row // 512 * 128, 128), 128)
                        fine1_ref[row % 512 : row % 512 + 8, lanes] = piece
                    else:
                        start = pl.multiple_of(half * 256 + row % 256, 8)
                        lane = (row - 1024) // 256 * 128
                        fine2_ref[pl.ds(start, 8), lane : lane + 128] = piece
                    row = plane * 24 + at
                    piece = values[24 + at : 32 + at, :] * coarse_scale
                    if row < 256:
                        start = pl.multiple_of(half * 256 + row, 8)
                        coarse1_ref[pl.ds(start, 8), x * 128 : x * 128 + 128] = piece
                    else:
                        start = pl.multiple_of(half * 64 + x * 128 + row % 64, 8)
                        lane = (row - 256) // 64 * 128
                        coarse2_ref[pl.ds(start, 8), lane : lane + 128] = piece


class Late:
    def __init__(self, source, held, sem):
        self.held = held
        self.shape = held.shape
        self.copy = pltpu.make_async_copy(source, held, sem)
        self.copy.start()

    def __getitem__(self, index):
        if self.copy is not None:
            self.copy.wait()
            self.copy = None
        return self.held[index]

    def finish(self):
        if self.copy is not None:
            self.copy.wait()
            self.copy = None


def run(kernel, outs, operands, scratch=(), scalars=(), late=(), inner=(), ahead=(), limit=16):
    size = sum(math.prod(x.shape) * x.dtype.itemsize for x in [*operands, *ahead]) + sum(
        math.prod(shape) * jnp.dtype(kind).itemsize for shape, kind in outs
    )
    shapes = [
        (pltpu.VMEM if i in inner else jax.ShapeDtypeStruct)(shape, kind)
        for i, (shape, kind) in enumerate(outs)
    ] + [pltpu.VMEM(x.shape, x.dtype) for x in ahead]
    operands = [
        pltpu.with_memory_space_constraint(x, pltpu.HBM) if i in late else x
        for i, x in enumerate(operands)
    ] + [pltpu.with_memory_space_constraint(x, pltpu.HBM) for x in ahead]
    count = len(operands) - len(ahead)
    first_out = len(operands)
    first_ahead = first_out + len(outs)
    first_scratch = first_ahead + len(ahead)
    first_held = first_scratch + len(scratch)

    def space(i):
        return pltpu.SMEM if i in scalars else pltpu.HBM if i in late or i >= count else pltpu.VMEM

    def body(*refs):
        sems = refs[-1]
        inputs = list(refs[:count])
        for k, i in enumerate(late):
            inputs[i] = Late(refs[i], refs[first_held + k], sems.at[k])
        fetched = [
            Late(refs[count + k], refs[first_ahead + k], sems.at[len(late) + k])
            for k in range(len(ahead))
        ]
        kernel(*inputs, *refs[first_out:first_ahead], *refs[first_scratch:first_held])
        for copy in [inputs[i] for i in late] + fetched:
            copy.finish()

    copies = len(late) + len(ahead)
    return pl.pallas_call(
        body if copies else kernel,
        out_shape=shapes,
        in_specs=[pl.BlockSpec(memory_space=space(i)) for i in range(first_out)],
        out_specs=[pl.BlockSpec(memory_space=pltpu.VMEM)] * len(shapes),
        scratch_shapes=[pltpu.VMEM(shape, kind) for shape, kind in scratch]
        + [pltpu.VMEM(operands[i].shape, operands[i].dtype) for i in late]
        + ([pltpu.SemaphoreType.DMA((copies,))] if copies else []),
        compiler_params=pltpu.CompilerParams(vmem_limit_bytes=limit * 1024 * 1024),
        cost_estimate=pl.CostEstimate(flops=0, bytes_accessed=size, transcendentals=0),
    )(*operands)


ROW = ("z", "y", "core")
PLANE = ("z", "y")
CHIPS = ("z", "y", "x")


def send(value, axis, step):
    size = lax.axis_size(axis)
    return lax.ppermute(value, axis, [(i, (i + step) % size) for i in range(size)])


def shards(
    latent, cotangent, fine_w1, fine_w2, fine_gain, coarse_w1, coarse_w2, coarse_gain,
    fine_src, fine_dst, live_blocks, export_rows, pool_assign, coarse_src, coarse_dst,
):
    own = latent[0, 0]
    cot = cotangent[0, 0]
    nodes, feature = own.shape
    export = export_rows[0]
    assign = pool_assign[0]
    src, dst = fine_src[0], fine_dst[0]
    rim_count = export.shape[1]
    hidden = fine_w1.shape[1]
    edges, coarse_edges = src.shape[1], coarse_src.shape[1]
    rows, cols = lax.axis_size(ROW), lax.axis_size("x")
    fine_gain = fine_gain[None, :]
    coarse_gain = coarse_gain[None, :]
    between = [(i, i + 1) for i in range(1, rows - 1, 2)]
    between = between + [(target, source) for source, target in between]
    place = jnp.stack([lax.axis_index("x"), lax.axis_index("core"), 128 * live_blocks[0, 0]])
    own, place = lax.optimization_barrier((own, place.astype(jnp.int32)))
    wide = 2 * feature

    rim, pack, target, own_in, src_in, w1_in, w2_in, gain_in, assign_in, export_in = run(
        start_kernel,
        [
            ((rim_count, feature), BF),
            ((rim_count + CNODE + 32, feature), BF),
            ((1, edges), jnp.int32),
        ],
        [own, export, cot, assign, dst, place],
        scalars=(5,),
        late=(0, 1, 2, 3, 4),
        inner=(0, 1, 2),
        ahead=[own, src, fine_w1, fine_w2, fine_gain, assign, export],
    )
    from_a = send(rim, "core", 1)
    from_b = lax.ppermute(rim, ROW, between)
    packs = [pack, send(pack, "x", 1), send(pack, "x", 3), send(pack[rim_count:], "x", 2)]
    part, csrc_in, cdst_in, cw1_in, cw2_in, cgain_in, cot_in = run(
        own_kernel,
        [((edges, hidden), F32)],
        [own_in, src_in, target, w1_in],
        inner=(0,),
        ahead=[coarse_src, coarse_dst, coarse_w1, coarse_w2, coarse_gain, cot],
        limit=LIMITS[0],
    )
    slope, acc, summed, pooled, table = run(
        fine_forward_kernel,
        [
            ((edges, hidden), F32),
            ((nodes, hidden), BF),
            ((nodes, feature), F32),
            ((CNODE, feature), BF),
            ((nodes + 4 * rim_count, feature), BF),
        ],
        [
            part, own_in, from_a, from_b, packs[1], packs[2], src_in, target, place,
            w1_in, w2_in, gain_in, assign_in,
        ],
        [((nodes, hidden), F32)],
        scalars=(8,),
        inner=(0, 1, 2, 3, 4),
        limit=LIMITS[1],
    )
    half_rows = CNODE // 2
    pooled, packs[3] = lax.optimization_barrier((pooled, packs[3]))
    left, right = send(pooled, "x", 1), send(pooled, "x", 3)
    across = [send(left[:half_rows], "x", 1), send(right[half_rows:], "x", 3)]

    grad_fine, coarse_pack = run(
        coarse_kernel,
        [((nodes, feature), F32), ((2, 384, 128), F32)],
        [
            pooled, left, right, *across, *packs, csrc_in, cdst_in, cw1_in, cw2_in, cgain_in,
            cot_in, assign_in, place,
        ],
        [
            ((CNODE, feature), BF),
            ((coarse_edges, hidden), F32),
            ((coarse_edges, CNODE), BF),
            ((CNODE, coarse_edges), BF),
            ((CNODE, hidden), F32),
            ((CNODE, hidden), F32),
            ((CNODE, hidden), F32),
        ],
        scalars=(16,),
        inner=(0, 1),
        limit=LIMITS[2],
    )

    local, give, keep, ghost_b, ghost_w, ghost_e = run(
        fine_backward_kernel,
        [
            ((nodes, feature), F32),
            ((1920 + 2 * rim_count, 128), BF),
            ((1920, 128), F32),
            ((rim_count, feature), BF),
            ((2 * rim_count, 128), BF),
            ((2 * rim_count, 128), BF),
        ],
        [
            grad_fine, summed, slope, acc, table, src_in, target, place,
            w1_in, w2_in, gain_in, coarse_pack,
        ],
        [
            ((nodes + 4 * rim_count, hidden), F32),
            ((nodes, hidden), F32),
            ((4 * rim_count, feature), BF),
        ],
        scalars=(7,),
        inner=(0, 1, 2, 3, 4, 5),
        limit=LIMITS[3],
    )
    from_core = send(give, "core", 1)
    from_b = lax.ppermute(ghost_b, ROW, between)
    total, coarse_total, to_east, to_cross, to_west = run(
        split_kernel,
        [
            ((384, 128), F32),
            ((384, 128), F32),
            ((384 + 2 * rim_count, 128), BF),
            ((384, 128), BF),
            ((384 + 2 * rim_count, 128), BF),
        ],
        [keep, from_core, ghost_w, ghost_e, place],
        scalars=(4,),
        inner=(0, 1, 2, 3, 4),
    )
    from_west = send(to_east, "x", 1)
    from_cross = send(to_cross, "x", 2)
    from_east = send(to_west, "x", 3)
    total = (
        total
        + from_west[0:384].astype(F32)
        + from_cross.astype(F32)
        + from_east[0:384].astype(F32)
    )
    both = jnp.concatenate(
        [total.reshape(16, 24, 128), coarse_total.reshape(16, 24, 128)], axis=1
    ).astype(BF)
    both, from_b = lax.optimization_barrier((both, from_b))
    both = lax.all_to_all(both, PLANE, 0, 0, tiled=True)
    both = jnp.sum(both.astype(F32), axis=0).astype(BF)
    copies = jnp.broadcast_to(both[None], (64,) + both.shape)
    mine = lax.all_to_all(copies, CHIPS, 0, 0, tiled=True)
    mine, local = lax.optimization_barrier((mine, local))
    other = send(mine, "core", 1)
    (grad_latent,) = run(
        return_kernel,
        [((nodes, feature), F32)],
        [local, from_core, from_b, from_west, from_east, export_in, place],
        scalars=(6,),
    )
    unpack = functools.partial(
        unpack_kernel,
        fine_scale=1.0 / math.sqrt(edges * rows * cols),
        coarse_scale=1.0 / math.sqrt(coarse_edges * rows),
    )
    weight_grads = run(
        unpack,
        [
            ((2 * feature, hidden), F32),
            ((hidden, feature), F32),
            ((2 * feature, hidden), F32),
            ((hidden, feature), F32),
        ],
        [mine, other, place],
        scalars=(2,),
    )
    return (grad_latent[None, None], *weight_grads)


def solution(mesh):
    shape = (4, 4, 2, 4)
    inner = Mesh(mesh.devices.reshape(shape), ("z", "y", "core", "x"))
    node_sharded = P(ROW, "x", None, None)
    index_sharded = P(ROW, "x", None)
    placed = (
        node_sharded,
        node_sharded,
        P(),
        P(),
        P(),
        P(),
        P(),
        P(),
        index_sharded,
        index_sharded,
        P(ROW, "x"),
        index_sharded,
        index_sharded,
        P(ROW, None),
        P(ROW, None),
    )
    return jax.shard_map(
        shards,
        mesh=inner,
        in_specs=placed,
        out_specs=(node_sharded, P(), P(), P(), P()),
        check_vma=False,
    )
```

```python
import functools
import math

import jax
import jax.numpy as jnp
from jax import lax
from jax.experimental import pallas as pl
from jax.experimental.pallas import tpu as pltpu
from jax.sharding import Mesh
from jax.sharding import PartitionSpec as P

EPS = 1e-05
CNODE = 512
CHUNK = 1024
LIMITS = (16, 16, 18, 18, 18)
BF = jnp.bfloat16
F32 = jnp.float32


def dot(left, right):
    return lax.dot_general(left, right, (((1,), (0,)), ((), ())), preferred_element_type=F32)


def dot_rt(left, right):
    return lax.dot_general(left, right, (((1,), (1,)), ((), ())), preferred_element_type=F32)


def dot_lt(left, right):
    return lax.dot_general(left, right, (((0,), (0,)), ((), ())), preferred_element_type=F32)


def halves(value):
    high = value.astype(BF)
    return high, (value - high.astype(F32)).astype(BF)


def spread_row(row):
    count = row.shape[1]
    return jnp.concatenate(
        [
            jnp.broadcast_to(row[:, at : at + 128], (128, 128)).T
            for at in range(0, count, 128)
        ],
        axis=0,
    )


def pick_matrix(row, width):
    column = spread_row(row)
    wide = jnp.concatenate([column] * (width // 128), axis=1)
    hit = wide == lax.broadcasted_iota(jnp.int32, wide.shape, 1)
    return jnp.where(hit, 1.0, 0.0).astype(BF)


def sum_matrix(row, width):
    shape = (width, row.shape[1])
    hit = lax.broadcasted_iota(jnp.int32, shape, 0) == row
    return jnp.where(hit, 1.0, 0.0).astype(BF)


def norm_of(summed):
    inverse = lax.rsqrt(jnp.mean(summed * summed, axis=-1, keepdims=True) + EPS)
    return inverse, summed * inverse


def summed_grad(grad_new, gain, summed):
    inverse, normed = norm_of(summed)
    grad_normed = grad_new * gain
    mean = jnp.mean(grad_normed * normed, axis=-1, keepdims=True)
    return (inverse * (grad_normed - normed * mean)).astype(BF)


def activations(preact):
    sig = jax.nn.sigmoid(preact)
    return (preact * sig).astype(BF), sig * (1.0 + preact * (1.0 - sig))


def rim_kernel(own_ref, export_ref, rim_ref):
    rim_ref[...] = dot(pick_matrix(export_ref[...], own_ref.shape[0]), own_ref[...]).astype(BF)


def pool_kernel(cot_ref, assign_ref, pack_ref, count_ref):
    pool = sum_matrix(assign_ref[...], CNODE)
    pack_ref[...] = dot(pool, cot_ref[...]).astype(BF)
    count = dot_rt(jnp.ones((16, pool.shape[1]), BF), pool)
    coarse_part = jnp.floor(count * (1.0 / 256.0)) * 256.0
    upper = lax.broadcasted_iota(jnp.int32, count.shape, 0) < 8
    packed = jnp.where(upper, coarse_part, count - coarse_part).astype(BF)
    count_ref[0:16, :] = packed[:, :256]
    count_ref[16:32, :] = packed[:, 256:]


def own_kernel(own_ref, src_ref, dst_ref, w1_ref, place_ref, target_ref, part_ref):
    nodes, feature = own_ref.shape
    slot = lax.broadcasted_iota(jnp.int32, dst_ref.shape, 1)
    target_ref[...] = jnp.where(slot < place_ref[2], dst_ref[...], -1)
    for at in range(0, src_ref.shape[1], CHUNK):
        here = slice(at, at + CHUNK)
        left = dot(pick_matrix(src_ref[:, here], nodes), own_ref[...]).astype(BF)
        right = dot(pick_matrix(target_ref[:, here], nodes), own_ref[...]).astype(BF)
        part_ref[here, :] = dot(left, w1_ref[0:feature, :]) + dot(right, w1_ref[feature:, :])


def fine_forward_kernel(
    part_ref, own_ref, ra, rb, rw, re, src_ref, target_ref, place_ref,
    w1_ref, w2_ref, gain_ref, assign_ref, count_ref, slope_ref, acc_out, summed_ref, pooled_ref, table,
    acc,
):
    nodes, feature = own_ref.shape
    rim = ra.shape[0]
    core = place_ref[1]
    table[0:nodes, :] = own_ref[...]
    table[pl.ds(pl.multiple_of(nodes + rim * (1 - core), rim), rim), :] = ra[...]
    table[pl.ds(pl.multiple_of(nodes + rim * core, rim), rim), :] = rb[...]
    table[nodes + 2 * rim : nodes + 3 * rim, :] = rw[...]
    table[nodes + 3 * rim :, :] = re[...]
    for at in range(0, src_ref.shape[1], CHUNK):
        here = slice(at, at + CHUNK)
        picks = pick_matrix(src_ref[:, here] - nodes, 4 * rim)
        left = dot(picks, table[nodes:, :]).astype(BF)
        preact = part_ref[here, :] + dot(left, w1_ref[0:feature, :])
        hidden, slope = activations(preact)
        slope_ref[here, :] = slope
        part = dot(sum_matrix(target_ref[:, here], nodes), hidden)
        if at == 0:
            acc[...] = part
        else:
            acc[...] += part
    high, low = halves(acc[...])
    acc_out[...] = high
    summed = dot(high, w2_ref[...]) + dot(low, w2_ref[...])
    summed_ref[...] = summed
    _, normed = norm_of(summed)
    fine_new = own_ref[...].astype(F32) + normed * gain_ref[...]
    high, low = halves(fine_new)
    pool = sum_matrix(assign_ref[...], CNODE)
    pooled_ref[0:CNODE, :] = (dot(pool, high) + dot(pool, low)).astype(BF)
    pooled_ref[CNODE:, :] = count_ref[...]


def coarse_forward_kernel(
    p0, p1, p2, p3, p4, src_ref, dst_ref, w1_ref, w2_ref,
    table, weight_ref, slope, pick_t, sum_t, acc, summed_ref,
):
    feature = p0.shape[1]
    edges = src_ref.shape[1]
    count = None
    for ref in (p0, p1, p2, p4):
        tail = ref[ref.shape[0] - 32 :, :].astype(F32)
        tail = [tail[at : at + 1, :] + tail[at + 8 : at + 9, :] for at in (0, 16)]
        tail = jnp.concatenate(tail, axis=1)
        count = tail if count is None else count + tail
    weight = spread_row(1.0 / jnp.maximum(count, 1.0))
    weight = jnp.concatenate([weight] * (feature // 128), axis=1)
    weight_ref[...] = weight
    across = jnp.concatenate([p3[...].astype(F32), p4[0 : CNODE // 2, :].astype(F32)], axis=0)
    near = [ref[0:CNODE, :].astype(F32) for ref in (p0, p1, p2)]
    pooled = (near[0] + near[1]) + (near[2] + across)
    table[...] = (pooled * weight).astype(BF)
    for at in range(0, edges, CHUNK):
        here = slice(at, at + CHUNK)
        left = dot(pick_matrix(src_ref[:, here], CNODE), table[...]).astype(BF)
        pick = pick_matrix(dst_ref[:, here], CNODE)
        pick_t[here, :] = pick
        right = dot(pick, table[...]).astype(BF)
        preact = dot(left, w1_ref[0:feature, :]) + dot(right, w1_ref[feature:, :])
        hidden, slope[here, :] = activations(preact)
        adds = sum_matrix(dst_ref[:, here], CNODE)
        sum_t[:, here] = adds
        part = dot(adds, hidden)
        if at == 0:
            acc[...] = part
        else:
            acc[...] += part
    high, low = halves(acc[...])
    summed_ref[...] = dot(high, w2_ref[...]) + dot(low, w2_ref[...])


def coarse_backward_kernel(
    g0, g1, g2, g3, table, weight_ref, slope, pick_t, sum_t, acc, summed_ref,
    src_ref, w1_ref, w2_ref, gain_ref, cot_ref, assign_ref, place_ref, grad_fine_ref, pack_ref,
    by_src, by_dst,
):
    feature = g0.shape[1]
    edges = src_ref.shape[1]
    weight = weight_ref[...]
    grads = [ref[...].astype(F32) for ref in (g0, g1, g2, g3)]
    grad_c1 = (grads[0] + grads[1]) + (grads[2] + grads[3])
    grad_summed = summed_grad(grad_c1, gain_ref[...], summed_ref[...])
    for at in range(0, edges, CHUNK):
        here = slice(at, at + CHUNK)
        grad_message = dot(pick_t[here, :], grad_summed).astype(BF)
        grad_preact = (dot_rt(grad_message, w2_ref[...]) * slope[here, :]).astype(BF)
        part_src = dot(sum_matrix(src_ref[:, here], CNODE), grad_preact)
        part_dst = dot(sum_t[:, here], grad_preact)
        if at == 0:
            by_src[...] = part_src
            by_dst[...] = part_dst
        else:
            by_src[...] += part_src
            by_dst[...] += part_dst
    grad_c0 = (
        grad_c1
        + dot_rt(by_src[...].astype(BF), w1_ref[0:feature, :])
        + dot_rt(by_dst[...].astype(BF), w1_ref[feature:, :])
    )
    high, low = halves(grad_c0 * weight)
    spread = pick_matrix(assign_ref[...], CNODE)
    grad_fine_ref[...] = cot_ref[...].astype(F32) + dot(spread, high) + dot(spread, low)
    own = pl.ds(pl.multiple_of(place_ref[0] * 128, 128), 128)
    for half, rows in enumerate((by_src, by_dst)):
        pack_ref[half, 0:256, :] = dot_lt(table[...], rows[:, own].astype(BF))
    second = dot_lt(acc[:, own].astype(BF), grad_summed)
    for half in range(2):
        for k in range(2):
            pack_ref[half, 256 + 64 * k : 320 + 64 * k, :] = second[
                64 * half : 64 * half + 64, 128 * k : 128 * k + 128
            ]


def fine_backward_kernel(
    grad_fine_ref, summed_ref, slope_ref, acc_ref, table_ref, src_ref, target_ref,
    place_ref, w1_ref, w2_ref, gain_ref, coarse_ref,
    local_ref, give_ref, keep_ref, ghost_b, ghost_w, ghost_e, by_src, by_dst, ghost,
):
    nodes, feature = grad_fine_ref.shape
    rim = ghost_b.shape[0]
    core = place_ref[1]
    grad_fine = grad_fine_ref[...]
    grad_summed = summed_grad(grad_fine, gain_ref[...], summed_ref[...])
    for at in range(0, src_ref.shape[1], CHUNK):
        here = slice(at, at + CHUNK)
        target = target_ref[:, here]
        grad_message = dot(pick_matrix(target, nodes), grad_summed).astype(BF)
        grad_preact = (dot_rt(grad_message, w2_ref[...]) * slope_ref[here, :]).astype(BF)
        part_src = dot(sum_matrix(src_ref[:, here], table_ref.shape[0]), grad_preact)
        part_dst = dot(sum_matrix(target, nodes), grad_preact)
        if at == 0:
            by_src[...] = part_src
            by_dst[...] = part_dst
        else:
            by_src[...] += part_src
            by_dst[...] += part_dst
    grad_table = dot_rt(by_src[...].astype(BF), w1_ref[0:feature, :])
    local_ref[...] = (
        grad_fine
        + grad_table[0:nodes, :]
        + dot_rt(by_dst[...].astype(BF), w1_ref[feature:, :])
    )
    ghost[...] = grad_table[nodes:, :].astype(BF)
    to_core = ghost[pl.ds(pl.multiple_of(rim * (1 - core), rim), rim), :]
    give_ref[1920 : 1920 + rim, :] = to_core[:, 0:128]
    give_ref[1920 + rim :, :] = to_core[:, 128:256]
    ghost_b[...] = ghost[pl.ds(pl.multiple_of(rim * core, rim), rim), :]
    for out, at in ((ghost_w, 2 * rim), (ghost_e, 3 * rim)):
        out[0:rim, :] = ghost[at : at + rim, 0:128]
        out[rim:, :] = ghost[at : at + rim, 128:256]
    for out, half in ((give_ref, 1 - core), (keep_ref, core)):
        part = pl.ds(pl.multiple_of(half * 256, 256), 256)
        first = dot_lt(table_ref[...], by_src[:, part].astype(BF)).astype(out.dtype)
        second = dot_lt(table_ref[0:nodes, :], by_dst[:, part].astype(BF)).astype(out.dtype)
        third = dot_lt(acc_ref[:, part], grad_summed).astype(out.dtype)
        for k in range(2):
            lanes = slice(128 * k, 128 * k + 128)
            out[512 * k : 512 * k + 256, :] = first[:, lanes]
            out[512 * k + 256 : 512 * k + 512, :] = second[:, lanes]
            out[1024 + 256 * k : 1280 + 256 * k, :] = third[:, lanes]
        out[1536:1920, :] = coarse_ref[half].astype(out.dtype)


def split_kernel(keep_ref, got_ref, ghost_w, ghost_e, place_ref, total_ref, coarse_ref, *sends):
    col = place_ref[0]

    def block(step):
        rows = pl.ds(pl.multiple_of(lax.rem(col + step, 4) * 384, 384), 384)
        return keep_ref[rows, :] + got_ref[rows, :].astype(F32)

    total_ref[...] = block(0)
    coarse_ref[...] = keep_ref[1536:1920, :] + got_ref[1536:1920, :].astype(F32)
    for step, out in enumerate(sends, 1):
        out[0:384, :] = block(step).astype(BF)
    sends[0][384:, :] = ghost_e[...]
    sends[2][384:, :] = ghost_w[...]


def return_kernel(local_ref, from_core, from_b, from_west, from_east, export_ref, place_ref, out_ref):
    rim = export_ref.shape[1]
    adds = sum_matrix(export_ref[...], local_ref.shape[0])
    col = place_ref[0]

    def wide(ref):
        at = ref.shape[0] - 2 * rim
        rows = ref[at:, :].astype(F32)
        return jnp.concatenate([rows[0:rim, :], rows[rim:, :]], axis=1)

    west = wide(from_west) * jnp.where(col > 0, 1.0, 0.0)
    east = wide(from_east) * jnp.where(col < 3, 1.0, 0.0)
    arrived = (wide(from_core) + from_b[...].astype(F32)) + (west + east)
    high, low = halves(arrived)
    out_ref[...] = local_ref[...] + dot(adds, high) + dot(adds, low)


def unpack_kernel(ref, place_ref, *rest, other, fine_scale, coarse_scale):
    outs, (fine1, fine2, coarse1, coarse2, sems) = rest[-9:-5], rest[-5:]
    half = 1 - place_ref[1] if other else place_ref[1]
    start = pl.multiple_of(half * 256, 256)
    for x in range(4):
        for plane in range(16):
            values = ref[plane * 4 + x].astype(F32)
            for at in range(0, 24, 8):
                row = x * 384 + plane * 24 + at
                piece = values[at : at + 8, :] * fine_scale
                if row < 1024:
                    lane = row // 512 * 128
                    fine1[row % 512 : row % 512 + 8, lane : lane + 128] = piece
                else:
                    lane = (row - 1024) // 256 * 128
                    fine2[row % 256 : row % 256 + 8, lane : lane + 128] = piece
                row = plane * 24 + at
                piece = values[24 + at : 32 + at, :] * coarse_scale
                if row < 256:
                    coarse1[row : row + 8, x * 128 : x * 128 + 128] = piece
                else:
                    lane = (row - 256) // 64 * 128
                    row = row % 64
                    coarse2[x, row : row + 8, lane : lane + 128] = piece
    copies = [
        pltpu.make_async_copy(fine1, outs[0].at[:, pl.ds(start, 256)], sems.at[0]),
        pltpu.make_async_copy(fine2, outs[1].at[pl.ds(start, 256), :], sems.at[1]),
        pltpu.make_async_copy(coarse1, outs[2].at[pl.ds(start, 256), :], sems.at[2]),
    ]
    for x in range(4):
        rows = pl.ds(pl.multiple_of(x * 128 + half * 64, 64), 64)
        copies.append(pltpu.make_async_copy(coarse2.at[x], outs[3].at[rows, :], sems.at[3 + x]))
    for copy in copies:
        copy.start()
    for copy in copies:
        copy.wait()


def unpack(part, place, earlier, shapes, fine_scale, coarse_scale):
    body = functools.partial(
        unpack_kernel, other=bool(earlier), fine_scale=fine_scale, coarse_scale=coarse_scale
    )
    return pl.pallas_call(
        body,
        out_shape=[pltpu.HBM(shape, F32) for shape in shapes],
        in_specs=[
            pl.BlockSpec(memory_space=pltpu.VMEM),
            pl.BlockSpec(memory_space=pltpu.SMEM),
        ]
        + [pl.BlockSpec(memory_space=pltpu.HBM)] * len(earlier),
        out_specs=[pl.BlockSpec(memory_space=pltpu.HBM)] * len(shapes),
        scratch_shapes=[
            pltpu.VMEM((512, 256), F32),
            pltpu.VMEM((256, 256), F32),
            pltpu.VMEM((256, 512), F32),
            pltpu.VMEM((4, 64, 256), F32),
            pltpu.SemaphoreType.DMA((7,)),
        ],
        input_output_aliases={2 + i: i for i in range(len(earlier))},
        compiler_params=pltpu.CompilerParams(vmem_limit_bytes=16 * 1024 * 1024),
        cost_estimate=pl.CostEstimate(flops=0, bytes_accessed=3 * 2**20, transcendentals=0),
    )(part, place, *earlier)


class Late:
    def __init__(self, source, held, sem):
        self.held = held
        self.shape = held.shape
        self.copy = pltpu.make_async_copy(source, held, sem)
        self.copy.start()

    def __getitem__(self, index):
        if self.copy is not None:
            self.copy.wait()
            self.copy = None
        return self.held[index]

    def finish(self):
        if self.copy is not None:
            self.copy.wait()
            self.copy = None


def run(kernel, outs, operands, scratch=(), scalars=(), late=(), inner=(), ahead=(), limit=16, work=0.1):
    size = sum(math.prod(x.shape) * x.dtype.itemsize for x in [*operands, *ahead]) + sum(
        math.prod(shape) * jnp.dtype(kind).itemsize for shape, kind in outs
    )
    shapes = [
        (pltpu.VMEM if i in inner else jax.ShapeDtypeStruct)(shape, kind)
        for i, (shape, kind) in enumerate(outs)
    ] + [pltpu.VMEM(x.shape, x.dtype) for x in ahead]
    operands = [
        pltpu.with_memory_space_constraint(x, pltpu.HBM) if i in late else x
        for i, x in enumerate(operands)
    ] + [pltpu.with_memory_space_constraint(x, pltpu.HBM) for x in ahead]
    count = len(operands) - len(ahead)
    first_out = len(operands)
    first_ahead = first_out + len(outs)
    first_scratch = first_ahead + len(ahead)
    first_held = first_scratch + len(scratch)

    def space(i):
        return pltpu.SMEM if i in scalars else pltpu.HBM if i in late or i >= count else pltpu.VMEM

    def body(*refs):
        sems = refs[-1]
        inputs = list(refs[:count])
        for k, i in enumerate(late):
            inputs[i] = Late(refs[i], refs[first_held + k], sems.at[k])
        fetched = [
            Late(refs[count + k], refs[first_ahead + k], sems.at[len(late) + k])
            for k in range(len(ahead))
        ]
        kernel(*inputs, *refs[first_out:first_ahead], *refs[first_scratch:first_held])
        for copy in [inputs[i] for i in late] + fetched:
            copy.finish()

    copies = len(late) + len(ahead)
    return pl.pallas_call(
        body if copies else kernel,
        out_shape=shapes,
        in_specs=[pl.BlockSpec(memory_space=space(i)) for i in range(first_out)],
        out_specs=[pl.BlockSpec(memory_space=pltpu.VMEM)] * len(shapes),
        scratch_shapes=[pltpu.VMEM(shape, kind) for shape, kind in scratch]
        + [pltpu.VMEM(operands[i].shape, operands[i].dtype) for i in late]
        + ([pltpu.SemaphoreType.DMA((copies,))] if copies else []),
        compiler_params=pltpu.CompilerParams(vmem_limit_bytes=limit * 1024 * 1024),
        cost_estimate=pl.CostEstimate(
            flops=int(2e9 * work), bytes_accessed=size, transcendentals=0
        ),
    )(*operands)


ROW = ("z", "y", "core")
PLANE = ("z", "y")
CHIPS = ("z", "y", "x")


def send(value, axis, step):
    size = lax.axis_size(axis)
    return lax.ppermute(value, axis, [(i, (i + step) % size) for i in range(size)])


def shards(
    latent, cotangent, fine_w1, fine_w2, fine_gain, coarse_w1, coarse_w2, coarse_gain,
    fine_src, fine_dst, live_blocks, export_rows, pool_assign, coarse_src, coarse_dst,
):
    own = latent[0, 0]
    cot = cotangent[0, 0]
    nodes, feature = own.shape
    export = export_rows[0]
    assign = pool_assign[0]
    src, dst = fine_src[0], fine_dst[0]
    rim_count = export.shape[1]
    hidden = fine_w1.shape[1]
    edges, coarse_edges = src.shape[1], coarse_src.shape[1]
    rows, cols = lax.axis_size(ROW), lax.axis_size("x")
    fine_gain = fine_gain[None, :]
    coarse_gain = coarse_gain[None, :]
    between = [(i, i + 1) for i in range(1, rows - 1, 2)]
    between = between + [(target, source) for source, target in between]
    place = jnp.stack([lax.axis_index("x"), lax.axis_index("core"), 128 * live_blocks[0, 0]])
    own, place = lax.optimization_barrier((own, place.astype(jnp.int32)))
    wide = 2 * feature

    east = [(i, i + 1) for i in range(cols - 1)]
    west = [(i + 1, i) for i in range(cols - 1)]
    rim, own_in, src_in, w1_in, export_in = run(
        rim_kernel,
        [((rim_count, feature), BF)],
        [own, export],
        late=(0, 1),
        inner=(0,),
        ahead=[own, src, fine_w1, export],
    )
    from_west = lax.ppermute(rim, "x", east)
    from_east = lax.ppermute(rim, "x", west)
    from_b = lax.ppermute(rim, ROW, between)
    from_a = send(rim, "core", 1)
    target, part, csrc_in, cdst_in, cw1_in, cw2_in, cgain_in, cot_in = run(
        own_kernel,
        [((1, edges), jnp.int32), ((edges, hidden), F32)],
        [own_in, src_in, dst, w1_in, place],
        scalars=(4,),
        late=(2,),
        inner=(0, 1),
        ahead=[coarse_src, coarse_dst, coarse_w1, coarse_w2, coarse_gain, cot],
        limit=LIMITS[0],
        work=1.1,
    )
    cot_in, part = lax.optimization_barrier((cot_in, part))
    pack, count, w2_in, gain_in, assign_in = run(
        pool_kernel,
        [((CNODE, feature), BF), ((32, feature), BF)],
        [cot_in, assign],
        late=(1,),
        inner=(0, 1),
        ahead=[fine_w2, fine_gain, assign],
    )
    packs = [pack, send(pack, "x", 1), send(pack, "x", 3)]
    slope, acc, summed, pooled, table = run(
        fine_forward_kernel,
        [
            ((edges, hidden), F32),
            ((nodes, hidden), BF),
            ((nodes, feature), F32),
            ((CNODE + 32, feature), BF),
            ((nodes + 4 * rim_count, feature), BF),
        ],
        [
            part, own_in, from_a, from_b, from_west, from_east, src_in, target, place,
            w1_in, w2_in, gain_in, assign_in, count,
        ],
        [((nodes, hidden), F32)],
        scalars=(8,),
        inner=(0, 1, 2, 3, 4),
        limit=LIMITS[1],
        work=1.6,
    )
    half_rows = CNODE // 2
    pooled, packs = lax.optimization_barrier((pooled, packs))
    left, right = send(pooled, "x", 1), send(pooled, "x", 3)
    across = [send(left[:half_rows], "x", 1), send(right[half_rows:], "x", 3)]
    pack, left, right, across = lax.optimization_barrier((packs[0], left, right, across))
    packs.append(send(pack, "x", 2))

    ctable, weight, cslope, pick, adds, cacc, csummed = run(
        coarse_forward_kernel,
        [
            ((CNODE, feature), BF),
            ((CNODE, feature), F32),
            ((coarse_edges, hidden), F32),
            ((coarse_edges, CNODE), BF),
            ((CNODE, coarse_edges), BF),
            ((CNODE, hidden), F32),
            ((CNODE, feature), F32),
        ],
        [pooled, left, right, *across, csrc_in, cdst_in, cw1_in, cw2_in],
        inner=(0, 1, 2, 3, 4, 5, 6),
        limit=LIMITS[2],
        work=2.6,
    )
    grad_fine, coarse_pack = run(
        coarse_backward_kernel,
        [((nodes, feature), F32), ((2, 384, 128), F32)],
        [
            *packs, ctable, weight, cslope, pick, adds, cacc, csummed,
            csrc_in, cw1_in, cw2_in, cgain_in, cot_in, assign_in, place,
        ],
        [((CNODE, hidden), F32), ((CNODE, hidden), F32)],
        scalars=(17,),
        inner=(0, 1),
        limit=LIMITS[3],
        work=2.8,
    )

    local, give, keep, ghost_b, ghost_w, ghost_e = run(
        fine_backward_kernel,
        [
            ((nodes, feature), F32),
            ((1920 + 2 * rim_count, 128), BF),
            ((1920, 128), F32),
            ((rim_count, feature), BF),
            ((2 * rim_count, 128), BF),
            ((2 * rim_count, 128), BF),
        ],
        [
            grad_fine, summed, slope, acc, table, src_in, target, place,
            w1_in, w2_in, gain_in, coarse_pack,
        ],
        [
            ((nodes + 4 * rim_count, hidden), F32),
            ((nodes, hidden), F32),
            ((4 * rim_count, feature), BF),
        ],
        scalars=(7,),
        inner=(0, 1, 2, 3, 4, 5),
        limit=LIMITS[4],
        work=2.8,
    )
    from_core = send(give, "core", 1)
    from_b = lax.ppermute(ghost_b, ROW, between)
    total, coarse_total, to_east, to_cross, to_west = run(
        split_kernel,
        [
            ((384, 128), F32),
            ((384, 128), F32),
            ((384 + 2 * rim_count, 128), BF),
            ((384, 128), BF),
            ((384 + 2 * rim_count, 128), BF),
        ],
        [keep, from_core, ghost_w, ghost_e, place],
        scalars=(4,),
        inner=(0, 1, 2, 3, 4),
    )
    from_west = send(to_east, "x", 1)
    from_cross = send(to_cross, "x", 2)
    from_east = send(to_west, "x", 3)
    total = (
        total
        + from_west[0:384].astype(F32)
        + from_cross.astype(F32)
        + from_east[0:384].astype(F32)
    )
    both = jnp.concatenate(
        [total.reshape(16, 24, 128), coarse_total.reshape(16, 24, 128)], axis=1
    ).astype(BF)
    both, from_b = lax.optimization_barrier((both, from_b))
    both = lax.all_to_all(both, PLANE, 0, 0, tiled=True)
    both = jnp.sum(both.astype(F32), axis=0).astype(BF)
    copies = jnp.broadcast_to(both[None], (64,) + both.shape)
    mine = lax.all_to_all(copies, CHIPS, 0, 0, tiled=True)
    mine, local = lax.optimization_barrier((mine, local))
    other = send(mine, "core", 1)
    (grad_latent,) = run(
        return_kernel,
        [((nodes, feature), F32)],
        [local, from_core, from_b, from_west, from_east, export_in, place],
        scalars=(6,),
    )
    shapes = [(wide, hidden), (hidden, feature), (wide, hidden), (hidden, feature)]
    scales = (1.0 / math.sqrt(edges * rows * cols), 1.0 / math.sqrt(coarse_edges * rows))
    grads = unpack(mine, place, [], shapes, *scales)
    grads = unpack(other, place, list(grads), shapes, *scales)
    return (grad_latent[None, None], *grads)


def solution(mesh):
    shape = (4, 4, 2, 4)
    inner = Mesh(mesh.devices.reshape(shape), ("z", "y", "core", "x"))
    node_sharded = P(ROW, "x", None, None)
    index_sharded = P(ROW, "x", None)
    placed = (
        node_sharded,
        node_sharded,
        P(),
        P(),
        P(),
        P(),
        P(),
        P(),
        index_sharded,
        index_sharded,
        P(ROW, "x"),
        index_sharded,
        index_sharded,
        P(ROW, None),
        P(ROW, None),
    )
    return jax.shard_map(
        shards,
        mesh=inner,
        in_specs=placed,
        out_specs=(node_sharded, P(), P(), P(), P()),
        check_vma=False,
    )
```

```python
import functools
import math

import jax
import jax.numpy as jnp
from jax import lax
from jax.experimental import pallas as pl
from jax.experimental.pallas import tpu as pltpu
from jax.sharding import Mesh
from jax.sharding import PartitionSpec as P

EPS = 1e-05
CNODE = 512
CHUNK = 1024
LIMITS = (20, 20, 36, 22)
BF = jnp.bfloat16
F32 = jnp.float32


def dot(left, right):
    return lax.dot_general(left, right, (((1,), (0,)), ((), ())), preferred_element_type=F32)


def dot_rt(left, right):
    return lax.dot_general(left, right, (((1,), (1,)), ((), ())), preferred_element_type=F32)


def dot_lt(left, right):
    return lax.dot_general(left, right, (((0,), (0,)), ((), ())), preferred_element_type=F32)


def halves(value):
    high = value.astype(BF)
    return high, (value - high.astype(F32)).astype(BF)


def spread_row(row):
    count = row.shape[1]
    return jnp.concatenate(
        [
            jnp.broadcast_to(row[:, at : at + 128], (128, 128)).T
            for at in range(0, count, 128)
        ],
        axis=0,
    )


def pick_matrix(row, width):
    column = spread_row(row)
    wide = jnp.concatenate([column] * (width // 128), axis=1)
    hit = wide == lax.broadcasted_iota(jnp.int32, wide.shape, 1)
    return jnp.where(hit, 1.0, 0.0).astype(BF)


def sum_matrix(row, width):
    shape = (width, row.shape[1])
    hit = lax.broadcasted_iota(jnp.int32, shape, 0) == row
    return jnp.where(hit, 1.0, 0.0).astype(BF)


def norm_of(summed):
    inverse = lax.rsqrt(jnp.mean(summed * summed, axis=-1, keepdims=True) + EPS)
    return inverse, summed * inverse


def summed_grad(grad_new, gain, summed):
    inverse, normed = norm_of(summed)
    grad_normed = grad_new * gain
    mean = jnp.mean(grad_normed * normed, axis=-1, keepdims=True)
    return (inverse * (grad_normed - normed * mean)).astype(BF)


def activations(preact):
    sig = jax.nn.sigmoid(preact)
    return (preact * sig).astype(BF), sig * (1.0 + preact * (1.0 - sig))


def start_kernel(
    own_ref, export_ref, cot_ref, assign_ref, dst_ref, place_ref, rim_ref, pack_ref, target_ref
):
    rim_count = export_ref.shape[1]
    rim = dot(pick_matrix(export_ref[...], own_ref.shape[0]), own_ref[...]).astype(BF)
    rim_ref[...] = rim
    pack_ref[0:rim_count, :] = rim
    pool = sum_matrix(assign_ref[...], CNODE)
    pack_ref[rim_count : rim_count + CNODE, :] = dot(pool, cot_ref[...]).astype(BF)
    count = dot_rt(jnp.ones((16, pool.shape[1]), BF), pool)
    coarse_part = jnp.floor(count * (1.0 / 256.0)) * 256.0
    upper = lax.broadcasted_iota(jnp.int32, count.shape, 0) < 8
    packed = jnp.where(upper, coarse_part, count - coarse_part).astype(BF)
    at = rim_count + CNODE
    pack_ref[at : at + 16, :] = packed[:, :256]
    pack_ref[at + 16 : at + 32, :] = packed[:, 256:]
    slot = lax.broadcasted_iota(jnp.int32, dst_ref.shape, 1)
    target_ref[...] = jnp.where(slot < place_ref[2], dst_ref[...], -1)


def own_kernel(own_ref, src_ref, target_ref, w1_ref, part_ref):
    nodes, feature = own_ref.shape
    for at in range(0, src_ref.shape[1], CHUNK):
        here = slice(at, at + CHUNK)
        left = dot(pick_matrix(src_ref[:, here], nodes), own_ref[...]).astype(BF)
        right = dot(pick_matrix(target_ref[:, here], nodes), own_ref[...]).astype(BF)
        part_ref[here, :] = dot(left, w1_ref[0:feature, :]) + dot(right, w1_ref[feature:, :])


def fine_forward_kernel(
    part_ref, own_ref, ra, rb, rw, re, src_ref, target_ref, place_ref,
    w1_ref, w2_ref, gain_ref, assign_ref, slope_ref, acc_out, summed_ref, pooled_ref, table, acc,
):
    nodes, feature = own_ref.shape
    rim = ra.shape[0]
    col, core = place_ref[0], place_ref[1]
    table[0:nodes, :] = own_ref[...]
    table[pl.ds(pl.multiple_of(nodes + rim * (1 - core), rim), rim), :] = ra[...]
    beyond = rb[...].astype(F32) * jnp.where(place_ref[3] > 0, 1.0, 0.0)
    table[pl.ds(pl.multiple_of(nodes + rim * core, rim), rim), :] = beyond.astype(BF)
    west = rw[0:rim, :].astype(F32) * jnp.where(col > 0, 1.0, 0.0)
    east = re[0:rim, :].astype(F32) * jnp.where(col < 3, 1.0, 0.0)
    table[nodes + 2 * rim : nodes + 3 * rim, :] = west.astype(BF)
    table[nodes + 3 * rim :, :] = east.astype(BF)
    for at in range(0, src_ref.shape[1], CHUNK):
        here = slice(at, at + CHUNK)
        picks = pick_matrix(src_ref[:, here] - nodes, 4 * rim)
        left = dot(picks, table[nodes:, :]).astype(BF)
        preact = part_ref[here, :] + dot(left, w1_ref[0:feature, :])
        hidden, slope = activations(preact)
        slope_ref[here, :] = slope
        part = dot(sum_matrix(target_ref[:, here], nodes), hidden)
        if at == 0:
            acc[...] = part
        else:
            acc[...] += part
    high, low = halves(acc[...])
    acc_out[...] = high
    summed = dot(high, w2_ref[...]) + dot(low, w2_ref[...])
    summed_ref[...] = summed
    _, normed = norm_of(summed)
    fine_new = own_ref[...].astype(F32) + normed * gain_ref[...]
    high, low = halves(fine_new)
    pool = sum_matrix(assign_ref[...], CNODE)
    pooled_ref[...] = (dot(pool, high) + dot(pool, low)).astype(BF)


def coarse_kernel(
    p0, p1, p2, p3, p4, g0, g1, g2, g3, src_ref, dst_ref, w1_ref, w2_ref, gain_ref, cot_ref,
    assign_ref, place_ref, grad_fine_ref, pack_ref,
    table, slope, pick_t, sum_t, acc, by_src, by_dst,
):
    feature = p0.shape[1]
    edges = src_ref.shape[1]
    grads = []
    count = None
    for ref in (g0, g1, g2, g3):
        skip = ref.shape[0] - CNODE - 32
        grads.append(ref[skip : skip + CNODE, :].astype(F32))
        tail = ref[skip + CNODE :, :].astype(F32)
        tail = [tail[at : at + 1, :] + tail[at + 8 : at + 9, :] for at in (0, 16)]
        tail = jnp.concatenate(tail, axis=1)
        count = tail if count is None else count + tail
    grad_c1 = (grads[0] + grads[1]) + (grads[2] + grads[3])
    weight = spread_row(1.0 / jnp.maximum(count, 1.0))
    weight = jnp.concatenate([weight] * (feature // 128), axis=1)
    across = jnp.concatenate([p3[...].astype(F32), p4[...].astype(F32)], axis=0)
    pooled = (p0[...].astype(F32) + p1[...].astype(F32)) + (p2[...].astype(F32) + across)
    table[...] = (pooled * weight).astype(BF)
    for at in range(0, edges, CHUNK):
        here = slice(at, at + CHUNK)
        left = dot(pick_matrix(src_ref[:, here], CNODE), table[...]).astype(BF)
        pick = pick_matrix(dst_ref[:, here], CNODE)
        pick_t[here, :] = pick
        right = dot(pick, table[...]).astype(BF)
        preact = dot(left, w1_ref[0:feature, :]) + dot(right, w1_ref[feature:, :])
        hidden, slope[here, :] = activations(preact)
        adds = sum_matrix(dst_ref[:, here], CNODE)
        sum_t[:, here] = adds
        part = dot(adds, hidden)
        if at == 0:
            acc[...] = part
        else:
            acc[...] += part
    high, low = halves(acc[...])
    summed = dot(high, w2_ref[...]) + dot(low, w2_ref[...])
    grad_summed = summed_grad(grad_c1, gain_ref[...], summed)
    for at in range(0, edges, CHUNK):
        here = slice(at, at + CHUNK)
        grad_message = dot(pick_t[here, :], grad_summed).astype(BF)
        grad_preact = (dot_rt(grad_message, w2_ref[...]) * slope[here, :]).astype(BF)
        part_src = dot(sum_matrix(src_ref[:, here], CNODE), grad_preact)
        part_dst = dot(sum_t[:, here], grad_preact)
        if at == 0:
            by_src[...] = part_src
            by_dst[...] = part_dst
        else:
            by_src[...] += part_src
            by_dst[...] += part_dst
    grad_c0 = (
        grad_c1
        + dot_rt(by_src[...].astype(BF), w1_ref[0:feature, :])
        + dot_rt(by_dst[...].astype(BF), w1_ref[feature:, :])
    )
    high, low = halves(grad_c0 * weight)
    spread = pick_matrix(assign_ref[...], CNODE)
    grad_fine_ref[...] = cot_ref[...].astype(F32) + dot(spread, high) + dot(spread, low)
    own = pl.ds(pl.multiple_of(place_ref[0] * 128, 128), 128)
    for half, rows in enumerate((by_src, by_dst)):
        pack_ref[half, 0:256, :] = dot_lt(table[...], rows[:, own].astype(BF))
    second = dot_lt(acc[:, own].astype(BF), grad_summed)
    for half in range(2):
        for k in range(2):
            pack_ref[half, 256 + 64 * k : 320 + 64 * k, :] = second[
                64 * half : 64 * half + 64, 128 * k : 128 * k + 128
            ]


def fine_backward_kernel(
    grad_fine_ref, summed_ref, slope_ref, acc_ref, table_ref, src_ref, target_ref,
    place_ref, w1_ref, w2_ref, gain_ref, coarse_ref,
    local_ref, give_ref, keep_ref, ghost_b, ghost_w, ghost_e, by_src, by_dst, ghost,
):
    nodes, feature = grad_fine_ref.shape
    rim = ghost_b.shape[0]
    core = place_ref[1]
    grad_fine = grad_fine_ref[...]
    grad_summed = summed_grad(grad_fine, gain_ref[...], summed_ref[...])
    for at in range(0, src_ref.shape[1], CHUNK):
        here = slice(at, at + CHUNK)
        target = target_ref[:, here]
        grad_message = dot(pick_matrix(target, nodes), grad_summed).astype(BF)
        grad_preact = (dot_rt(grad_message, w2_ref[...]) * slope_ref[here, :]).astype(BF)
        part_src = dot(sum_matrix(src_ref[:, here], table_ref.shape[0]), grad_preact)
        part_dst = dot(sum_matrix(target, nodes), grad_preact)
        if at == 0:
            by_src[...] = part_src
            by_dst[...] = part_dst
        else:
            by_src[...] += part_src
            by_dst[...] += part_dst
    grad_table = dot_rt(by_src[...].astype(BF), w1_ref[0:feature, :])
    local_ref[...] = (
        grad_fine
        + grad_table[0:nodes, :]
        + dot_rt(by_dst[...].astype(BF), w1_ref[feature:, :])
    )
    ghost[...] = grad_table[nodes:, :].astype(BF)
    to_core = ghost[pl.ds(pl.multiple_of(rim * (1 - core), rim), rim), :]
    give_ref[1920 : 1920 + rim, :] = to_core[:, 0:128]
    give_ref[1920 + rim :, :] = to_core[:, 128:256]
    ghost_b[...] = ghost[pl.ds(pl.multiple_of(rim * core, rim), rim), :]
    for out, at in ((ghost_w, 2 * rim), (ghost_e, 3 * rim)):
        out[0:rim, :] = ghost[at : at + rim, 0:128]
        out[rim:, :] = ghost[at : at + rim, 128:256]
    for out, half in ((give_ref, 1 - core), (keep_ref, core)):
        part = pl.ds(pl.multiple_of(half * 256, 256), 256)
        first = dot_lt(table_ref[...], by_src[:, part].astype(BF)).astype(out.dtype)
        second = dot_lt(table_ref[0:nodes, :], by_dst[:, part].astype(BF)).astype(out.dtype)
        third = dot_lt(acc_ref[:, part], grad_summed).astype(out.dtype)
        for k in range(2):
            lanes = slice(128 * k, 128 * k + 128)
            out[512 * k : 512 * k + 256, :] = first[:, lanes]
            out[512 * k + 256 : 512 * k + 512, :] = second[:, lanes]
            out[1024 + 256 * k : 1280 + 256 * k, :] = third[:, lanes]
        out[1536:1920, :] = coarse_ref[half].astype(out.dtype)


def split_kernel(keep_ref, got_ref, ghost_w, ghost_e, place_ref, total_ref, coarse_ref, *sends):
    col = place_ref[0]

    def block(step):
        rows = pl.ds(pl.multiple_of(lax.rem(col + step, 4) * 384, 384), 384)
        return keep_ref[rows, :] + got_ref[rows, :].astype(F32)

    total_ref[...] = block(0)
    coarse_ref[...] = keep_ref[1536:1920, :] + got_ref[1536:1920, :].astype(F32)
    for step, out in enumerate(sends, 1):
        out[0:384, :] = block(step).astype(BF)
    sends[0][384:, :] = ghost_e[...]
    sends[2][384:, :] = ghost_w[...]


def return_kernel(local_ref, from_core, from_b, from_west, from_east, export_ref, place_ref, out_ref):
    rim = export_ref.shape[1]
    adds = sum_matrix(export_ref[...], local_ref.shape[0])
    col = place_ref[0]

    def wide(ref):
        at = ref.shape[0] - 2 * rim
        rows = ref[at:, :].astype(F32)
        return jnp.concatenate([rows[0:rim, :], rows[rim:, :]], axis=1)

    west = wide(from_west) * jnp.where(col > 0, 1.0, 0.0)
    east = wide(from_east) * jnp.where(col < 3, 1.0, 0.0)
    beyond = from_b[...].astype(F32) * jnp.where(place_ref[3] > 0, 1.0, 0.0)
    arrived = (wide(from_core) + beyond) + (west + east)
    high, low = halves(arrived)
    out_ref[...] = local_ref[...] + dot(adds, high) + dot(adds, low)


def unpack_kernel(
    mine_ref, other_ref, place_ref, fine1_ref, fine2_ref, coarse1_ref, coarse2_ref,
    *, fine_scale, coarse_scale,
):
    for ref, half in ((mine_ref, place_ref[1]), (other_ref, 1 - place_ref[1])):
        for plane in range(16):
            for x in range(4):
                values = ref[plane * 4 + x].astype(F32)
                for at in range(0, 24, 8):
                    row = x * 384 + plane * 24 + at
                    piece = values[at : at + 8, :] * fine_scale
                    if row < 1024:
                        lanes = pl.ds(pl.multiple_of(half * 256 + row // 512 * 128, 128), 128)
                        fine1_ref[row % 512 : row % 512 + 8, lanes] = piece
                    else:
                        start = pl.multiple_of(half * 256 + row % 256, 8)
                        lane = (row - 1024) // 256 * 128
                        fine2_ref[pl.ds(start, 8), lane : lane + 128] = piece
                    row = plane * 24 + at
                    piece = values[24 + at : 32 + at, :] * coarse_scale
                    if row < 256:
                        start = pl.multiple_of(half * 256 + row, 8)
                        coarse1_ref[pl.ds(start, 8), x * 128 : x * 128 + 128] = piece
                    else:
                        start = pl.multiple_of(half * 64 + x * 128 + row % 64, 8)
                        lane = (row - 256) // 64 * 128
                        coarse2_ref[pl.ds(start, 8), lane : lane + 128] = piece


class Late:
    def __init__(self, source, held, sem):
        self.held = held
        self.shape = held.shape
        self.copy = pltpu.make_async_copy(source, held, sem)
        self.copy.start()

    def __getitem__(self, index):
        if self.copy is not None:
            self.copy.wait()
            self.copy = None
        return self.held[index]

    def finish(self):
        if self.copy is not None:
            self.copy.wait()
            self.copy = None


def run(kernel, outs, operands, scratch=(), scalars=(), late=(), inner=(), ahead=(), limit=16):
    size = sum(math.prod(x.shape) * x.dtype.itemsize for x in [*operands, *ahead]) + sum(
        math.prod(shape) * jnp.dtype(kind).itemsize for shape, kind in outs
    )
    shapes = [
        (pltpu.VMEM if i in inner else jax.ShapeDtypeStruct)(shape, kind)
        for i, (shape, kind) in enumerate(outs)
    ] + [pltpu.VMEM(x.shape, x.dtype) for x in ahead]
    operands = [
        pltpu.with_memory_space_constraint(x, pltpu.HBM) if i in late else x
        for i, x in enumerate(operands)
    ] + [pltpu.with_memory_space_constraint(x, pltpu.HBM) for x in ahead]
    count = len(operands) - len(ahead)
    first_out = len(operands)
    first_ahead = first_out + len(outs)
    first_scratch = first_ahead + len(ahead)
    first_held = first_scratch + len(scratch)

    def space(i):
        return pltpu.SMEM if i in scalars else pltpu.HBM if i in late or i >= count else pltpu.VMEM

    def body(*refs):
        sems = refs[-1]
        inputs = list(refs[:count])
        for k, i in enumerate(late):
            inputs[i] = Late(refs[i], refs[first_held + k], sems.at[k])
        fetched = [
            Late(refs[count + k], refs[first_ahead + k], sems.at[len(late) + k])
            for k in range(len(ahead))
        ]
        kernel(*inputs, *refs[first_out:first_ahead], *refs[first_scratch:first_held])
        for copy in [inputs[i] for i in late] + fetched:
            copy.finish()

    copies = len(late) + len(ahead)
    return pl.pallas_call(
        body if copies else kernel,
        out_shape=shapes,
        in_specs=[pl.BlockSpec(memory_space=space(i)) for i in range(first_out)],
        out_specs=[pl.BlockSpec(memory_space=pltpu.VMEM)] * len(shapes),
        scratch_shapes=[pltpu.VMEM(shape, kind) for shape, kind in scratch]
        + [pltpu.VMEM(operands[i].shape, operands[i].dtype) for i in late]
        + ([pltpu.SemaphoreType.DMA((copies,))] if copies else []),
        compiler_params=pltpu.CompilerParams(vmem_limit_bytes=limit * 1024 * 1024),
        cost_estimate=pl.CostEstimate(flops=0, bytes_accessed=size, transcendentals=0),
    )(*operands)


ROW = ("z", "y", "core")
PLANE = ("z", "y")
CHIPS = ("z", "y", "x")


def send(value, axis, step):
    size = lax.axis_size(axis)
    return lax.ppermute(value, axis, [(i, (i + step) % size) for i in range(size)])


def shards(
    latent, cotangent, fine_w1, fine_w2, fine_gain, coarse_w1, coarse_w2, coarse_gain,
    fine_src, fine_dst, live_blocks, export_rows, pool_assign, coarse_src, coarse_dst,
):
    own = latent[0, 0]
    cot = cotangent[0, 0]
    nodes, feature = own.shape
    export = export_rows[0]
    assign = pool_assign[0]
    src, dst = fine_src[0], fine_dst[0]
    rim_count = export.shape[1]
    hidden = fine_w1.shape[1]
    edges, coarse_edges = src.shape[1], coarse_src.shape[1]
    rows, cols = lax.axis_size(ROW), lax.axis_size("x")
    fine_gain = fine_gain[None, :]
    coarse_gain = coarse_gain[None, :]
    between = [(i, i + 1) for i in range(1, rows - 1, 2)]
    between = between + [(target, source) for source, target in between]
    between = between + [(rows - 1, 0), (0, rows - 1)]
    row = lax.axis_index(ROW)
    inside = jnp.logical_and(row > 0, row < rows - 1)
    place = jnp.stack(
        [lax.axis_index("x"), lax.axis_index("core"), 128 * live_blocks[0, 0], inside]
    )
    own, place = lax.optimization_barrier((own, place.astype(jnp.int32)))
    wide = 2 * feature

    rim, pack, target, own_in, src_in, w1_in, w2_in, gain_in, assign_in, export_in = run(
        start_kernel,
        [
            ((rim_count, feature), BF),
            ((rim_count + CNODE + 32, feature), BF),
            ((1, edges), jnp.int32),
        ],
        [own, export, cot, assign, dst, place],
        scalars=(5,),
        late=(0, 1, 2, 3, 4),
        inner=(0, 1, 2),
        ahead=[own, src, fine_w1, fine_w2, fine_gain, assign, export],
    )
    from_a = send(rim, "core", 1)
    from_b = lax.ppermute(rim, ROW, between)
    packs = [pack, send(pack, "x", 1), send(pack, "x", 3), send(pack[rim_count:], "x", 2)]
    part, csrc_in, cdst_in, cw1_in, cw2_in, cgain_in, cot_in = run(
        own_kernel,
        [((edges, hidden), F32)],
        [own_in, src_in, target, w1_in],
        inner=(0,),
        ahead=[coarse_src, coarse_dst, coarse_w1, coarse_w2, coarse_gain, cot],
        limit=LIMITS[0],
    )
    slope, acc, summed, pooled, table = run(
        fine_forward_kernel,
        [
            ((edges, hidden), F32),
            ((nodes, hidden), BF),
            ((nodes, feature), F32),
            ((CNODE, feature), BF),
            ((nodes + 4 * rim_count, feature), BF),
        ],
        [
            part, own_in, from_a, from_b, packs[1], packs[2], src_in, target, place,
            w1_in, w2_in, gain_in, assign_in,
        ],
        [((nodes, hidden), F32)],
        scalars=(8,),
        inner=(0, 1, 2, 3, 4),
        limit=LIMITS[1],
    )
    half_rows = CNODE // 2
    pooled, packs[3] = lax.optimization_barrier((pooled, packs[3]))
    left, right = send(pooled, "x", 1), send(pooled, "x", 3)
    across = [send(left[:half_rows], "x", 1), send(right[half_rows:], "x", 3)]

    grad_fine, coarse_pack = run(
        coarse_kernel,
        [((nodes, feature), F32), ((2, 384, 128), F32)],
        [
            pooled, left, right, *across, *packs, csrc_in, cdst_in, cw1_in, cw2_in, cgain_in,
            cot_in, assign_in, place,
        ],
        [
            ((CNODE, feature), BF),
            ((coarse_edges, hidden), F32),
            ((coarse_edges, CNODE), BF),
            ((CNODE, coarse_edges), BF),
            ((CNODE, hidden), F32),
            ((CNODE, hidden), F32),
            ((CNODE, hidden), F32),
        ],
        scalars=(16,),
        inner=(0, 1),
        limit=LIMITS[2],
    )

    local, give, keep, ghost_b, ghost_w, ghost_e = run(
        fine_backward_kernel,
        [
            ((nodes, feature), F32),
            ((1920 + 2 * rim_count, 128), BF),
            ((1920, 128), F32),
            ((rim_count, feature), BF),
            ((2 * rim_count, 128), BF),
            ((2 * rim_count, 128), BF),
        ],
        [
            grad_fine, summed, slope, acc, table, src_in, target, place,
            w1_in, w2_in, gain_in, coarse_pack,
        ],
        [
            ((nodes + 4 * rim_count, hidden), F32),
            ((nodes, hidden), F32),
            ((4 * rim_count, feature), BF),
        ],
        scalars=(7,),
        inner=(0, 1, 2, 3, 4, 5),
        limit=LIMITS[3],
    )
    from_core = send(give, "core", 1)
    from_b = lax.ppermute(ghost_b, ROW, between)
    total, coarse_total, to_east, to_cross, to_west = run(
        split_kernel,
        [
            ((384, 128), F32),
            ((384, 128), F32),
            ((384 + 2 * rim_count, 128), BF),
            ((384, 128), BF),
            ((384 + 2 * rim_count, 128), BF),
        ],
        [keep, from_core, ghost_w, ghost_e, place],
        scalars=(4,),
        inner=(0, 1, 2, 3, 4),
    )
    from_west = send(to_east, "x", 1)
    from_cross = send(to_cross, "x", 2)
    from_east = send(to_west, "x", 3)
    total = (
        total
        + from_west[0:384].astype(F32)
        + from_cross.astype(F32)
        + from_east[0:384].astype(F32)
    )
    both = jnp.concatenate(
        [total.reshape(16, 24, 128), coarse_total.reshape(16, 24, 128)], axis=1
    ).astype(BF)
    both, from_b = lax.optimization_barrier((both, from_b))
    both = lax.all_to_all(both, PLANE, 0, 0, tiled=True)
    both = jnp.sum(both.astype(F32), axis=0).astype(BF)
    copies = jnp.broadcast_to(both[None], (64,) + both.shape)
    mine = lax.all_to_all(copies, CHIPS, 0, 0, tiled=True)
    mine, local = lax.optimization_barrier((mine, local))
    other = send(mine, "core", 1)
    (grad_latent,) = run(
        return_kernel,
        [((nodes, feature), F32)],
        [local, from_core, from_b, from_west, from_east, export_in, place],
        scalars=(6,),
    )
    unpack = functools.partial(
        unpack_kernel,
        fine_scale=1.0 / math.sqrt(edges * rows * cols),
        coarse_scale=1.0 / math.sqrt(coarse_edges * rows),
    )
    weight_grads = run(
        unpack,
        [
            ((2 * feature, hidden), F32),
            ((hidden, feature), F32),
            ((2 * feature, hidden), F32),
            ((hidden, feature), F32),
        ],
        [mine, other, place],
        scalars=(2,),
    )
    return (grad_latent[None, None], *weight_grads)


def solution(mesh):
    shape = (4, 4, 2, 4)
    inner = Mesh(mesh.devices.reshape(shape), ("z", "y", "core", "x"))
    node_sharded = P(ROW, "x", None, None)
    index_sharded = P(ROW, "x", None)
    placed = (
        node_sharded,
        node_sharded,
        P(),
        P(),
        P(),
        P(),
        P(),
        P(),
        index_sharded,
        index_sharded,
        P(ROW, "x"),
        index_sharded,
        index_sharded,
        P(ROW, None),
        P(ROW, None),
    )
    return jax.shard_map(
        shards,
        mesh=inner,
        in_specs=placed,
        out_specs=(node_sharded, P(), P(), P(), P()),
        check_vma=False,
    )
```

```python
import functools
import math

import jax
import jax.numpy as jnp
from jax import lax
from jax.experimental import pallas as pl
from jax.experimental.pallas import tpu as pltpu
from jax.sharding import Mesh
from jax.sharding import PartitionSpec as P

EPS = 1e-05
CNODE = 512
CHUNK = 1024
LIMITS = (20, 20, 36, 22)
BF = jnp.bfloat16
F32 = jnp.float32


def dot(left, right):
    return lax.dot_general(left, right, (((1,), (0,)), ((), ())), preferred_element_type=F32)


def dot_rt(left, right):
    return lax.dot_general(left, right, (((1,), (1,)), ((), ())), preferred_element_type=F32)


def dot_lt(left, right):
    return lax.dot_general(left, right, (((0,), (0,)), ((), ())), preferred_element_type=F32)


def halves(value):
    high = value.astype(BF)
    return high, (value - high.astype(F32)).astype(BF)


def spread_row(row):
    count = row.shape[1]
    return jnp.concatenate(
        [
            jnp.broadcast_to(row[:, at : at + 128], (128, 128)).T
            for at in range(0, count, 128)
        ],
        axis=0,
    )


def pick_matrix(row, width):
    column = spread_row(row)
    wide = jnp.concatenate([column] * (width // 128), axis=1)
    hit = wide == lax.broadcasted_iota(jnp.int32, wide.shape, 1)
    return jnp.where(hit, 1.0, 0.0).astype(BF)


def sum_matrix(row, width):
    shape = (width, row.shape[1])
    hit = lax.broadcasted_iota(jnp.int32, shape, 0) == row
    return jnp.where(hit, 1.0, 0.0).astype(BF)


def norm_of(summed):
    inverse = lax.rsqrt(jnp.mean(summed * summed, axis=-1, keepdims=True) + EPS)
    return inverse, summed * inverse


def summed_grad(grad_new, gain, summed):
    inverse, normed = norm_of(summed)
    grad_normed = grad_new * gain
    mean = jnp.mean(grad_normed * normed, axis=-1, keepdims=True)
    return (inverse * (grad_normed - normed * mean)).astype(BF)


def activations(preact):
    sig = jax.nn.sigmoid(preact)
    return (preact * sig).astype(BF), sig * (1.0 + preact * (1.0 - sig))


def split_count(count):
    many = jnp.floor(count * (1.0 / 256.0)) * 256.0
    upper = lax.broadcasted_iota(jnp.int32, count.shape, 0) < 8
    return jnp.where(upper, many, count - many).astype(BF)


def whole_count(rows):
    rows = rows.astype(F32)
    parts = [rows[at : at + 1, :] + rows[at + 8 : at + 9, :] for at in (0, 16)]
    return jnp.concatenate(parts, axis=1)


def start_kernel(
    own_ref, export_ref, cot_ref, assign_ref, dst_ref, place_ref, rim_ref, pack_ref, target_ref
):
    rim_ref[...] = dot(pick_matrix(export_ref[...], own_ref.shape[0]), own_ref[...]).astype(BF)
    pool = sum_matrix(assign_ref[...], CNODE)
    pack_ref[0:CNODE, :] = dot(pool, cot_ref[...]).astype(BF)
    packed = split_count(dot_rt(jnp.ones((16, pool.shape[1]), BF), pool))
    pack_ref[CNODE : CNODE + 16, :] = packed[:, :256]
    pack_ref[CNODE + 16 : CNODE + 32, :] = packed[:, 256:]
    slot = lax.broadcasted_iota(jnp.int32, dst_ref.shape, 1)
    target_ref[...] = jnp.where(slot < place_ref[2], dst_ref[...], -1)


def add_kernel(mine_ref, got_ref, out_ref):
    out_ref[0:CNODE, :] = (
        mine_ref[0:CNODE, :].astype(F32) + got_ref[0:CNODE, :].astype(F32)
    ).astype(BF)
    count = whole_count(mine_ref[CNODE:, :]) + whole_count(got_ref[CNODE:, :])
    packed = split_count(jnp.broadcast_to(count, (16, CNODE)))
    out_ref[CNODE : CNODE + 16, :] = packed[:, :256]
    out_ref[CNODE + 16 : CNODE + 32, :] = packed[:, 256:]


def own_kernel(own_ref, src_ref, target_ref, w1_ref, part_ref):
    nodes, feature = own_ref.shape
    for at in range(0, src_ref.shape[1], CHUNK):
        here = slice(at, at + CHUNK)
        left = dot(pick_matrix(src_ref[:, here], nodes), own_ref[...]).astype(BF)
        right = dot(pick_matrix(target_ref[:, here], nodes), own_ref[...]).astype(BF)
        part_ref[here, :] = dot(left, w1_ref[0:feature, :]) + dot(right, w1_ref[feature:, :])


def fine_forward_kernel(
    part_ref, own_ref, ra, rb, rw, re, src_ref, target_ref, place_ref,
    w1_ref, w2_ref, gain_ref, assign_ref, slope_ref, acc_out, summed_ref, pooled_ref, table, acc,
):
    nodes, feature = own_ref.shape
    rim = ra.shape[0]
    col, core = place_ref[0], place_ref[1]
    table[0:nodes, :] = own_ref[...]
    table[pl.ds(pl.multiple_of(nodes + rim * (1 - core), rim), rim), :] = ra[...]
    beyond = rb[...].astype(F32) * jnp.where(place_ref[3] > 0, 1.0, 0.0)
    table[pl.ds(pl.multiple_of(nodes + rim * core, rim), rim), :] = beyond.astype(BF)
    west = rw[...].astype(F32) * jnp.where(col > 0, 1.0, 0.0)
    east = re[...].astype(F32) * jnp.where(col < 3, 1.0, 0.0)
    table[nodes + 2 * rim : nodes + 3 * rim, :] = west.astype(BF)
    table[nodes + 3 * rim :, :] = east.astype(BF)
    for at in range(0, src_ref.shape[1], CHUNK):
        here = slice(at, at + CHUNK)
        picks = pick_matrix(src_ref[:, here] - nodes, 4 * rim)
        left = dot(picks, table[nodes:, :]).astype(BF)
        preact = part_ref[here, :] + dot(left, w1_ref[0:feature, :])
        hidden, slope = activations(preact)
        slope_ref[here, :] = slope
        part = dot(sum_matrix(target_ref[:, here], nodes), hidden)
        if at == 0:
            acc[...] = part
        else:
            acc[...] += part
    high, low = halves(acc[...])
    acc_out[...] = high
    summed = dot(high, w2_ref[...]) + dot(low, w2_ref[...])
    summed_ref[...] = summed
    _, normed = norm_of(summed)
    fine_new = own_ref[...].astype(F32) + normed * gain_ref[...]
    high, low = halves(fine_new)
    pool = sum_matrix(assign_ref[...], CNODE)
    pooled_ref[...] = (dot(pool, high) + dot(pool, low)).astype(BF)


def coarse_kernel(
    p0, p1, p2, p3, p4, g0, g1, src_ref, dst_ref, w1_ref, w2_ref, gain_ref, cot_ref,
    assign_ref, place_ref, grad_fine_ref, pack_ref,
    table, slope, pick_t, sum_t, acc, by_src, by_dst,
):
    feature = p0.shape[1]
    edges = src_ref.shape[1]
    grad_c1 = g0[0:CNODE, :].astype(F32) + g1[0:CNODE, :].astype(F32)
    count = whole_count(g0[CNODE:, :]) + whole_count(g1[CNODE:, :])
    weight = spread_row(1.0 / jnp.maximum(count, 1.0))
    weight = jnp.concatenate([weight] * (feature // 128), axis=1)
    across = jnp.concatenate([p3[...].astype(F32), p4[...].astype(F32)], axis=0)
    pooled = (p0[...].astype(F32) + p1[...].astype(F32)) + (p2[...].astype(F32) + across)
    table[...] = (pooled * weight).astype(BF)
    for at in range(0, edges, CHUNK):
        here = slice(at, at + CHUNK)
        left = dot(pick_matrix(src_ref[:, here], CNODE), table[...]).astype(BF)
        pick = pick_matrix(dst_ref[:, here], CNODE)
        pick_t[here, :] = pick
        right = dot(pick, table[...]).astype(BF)
        preact = dot(left, w1_ref[0:feature, :]) + dot(right, w1_ref[feature:, :])
        hidden, slope[here, :] = activations(preact)
        adds = sum_matrix(dst_ref[:, here], CNODE)
        sum_t[:, here] = adds
        part = dot(adds, hidden)
        if at == 0:
            acc[...] = part
        else:
            acc[...] += part
    high, low = halves(acc[...])
    summed = dot(high, w2_ref[...]) + dot(low, w2_ref[...])
    grad_summed = summed_grad(grad_c1, gain_ref[...], summed)
    for at in range(0, edges, CHUNK):
        here = slice(at, at + CHUNK)
        grad_message = dot(pick_t[here, :], grad_summed).astype(BF)
        grad_preact = (dot_rt(grad_message, w2_ref[...]) * slope[here, :]).astype(BF)
        part_src = dot(sum_matrix(src_ref[:, here], CNODE), grad_preact)
        part_dst = dot(sum_t[:, here], grad_preact)
        if at == 0:
            by_src[...] = part_src
            by_dst[...] = part_dst
        else:
            by_src[...] += part_src
            by_dst[...] += part_dst
    grad_c0 = (
        grad_c1
        + dot_rt(by_src[...].astype(BF), w1_ref[0:feature, :])
        + dot_rt(by_dst[...].astype(BF), w1_ref[feature:, :])
    )
    high, low = halves(grad_c0 * weight)
    spread = pick_matrix(assign_ref[...], CNODE)
    grad_fine_ref[...] = cot_ref[...].astype(F32) + dot(spread, high) + dot(spread, low)
    own = pl.ds(pl.multiple_of(place_ref[0] * 128, 128), 128)
    for half, rows in enumerate((by_src, by_dst)):
        pack_ref[half, 0:256, :] = dot_lt(table[...], rows[:, own].astype(BF))
    second = dot_lt(acc[:, own].astype(BF), grad_summed)
    for half in range(2):
        for k in range(2):
            pack_ref[half, 256 + 64 * k : 320 + 64 * k, :] = second[
                64 * half : 64 * half + 64, 128 * k : 128 * k + 128
            ]


def fine_backward_kernel(
    grad_fine_ref, summed_ref, slope_ref, acc_ref, table_ref, src_ref, target_ref,
    place_ref, w1_ref, w2_ref, gain_ref, coarse_ref,
    local_ref, give_ref, keep_ref, ghost_b, ghost_w, ghost_e, by_src, by_dst, ghost,
):
    nodes, feature = grad_fine_ref.shape
    rim = ghost_b.shape[0]
    core = place_ref[1]
    grad_fine = grad_fine_ref[...]
    grad_summed = summed_grad(grad_fine, gain_ref[...], summed_ref[...])
    for at in range(0, src_ref.shape[1], CHUNK):
        here = slice(at, at + CHUNK)
        target = target_ref[:, here]
        grad_message = dot(pick_matrix(target, nodes), grad_summed).astype(BF)
        grad_preact = (dot_rt(grad_message, w2_ref[...]) * slope_ref[here, :]).astype(BF)
        part_src = dot(sum_matrix(src_ref[:, here], table_ref.shape[0]), grad_preact)
        part_dst = dot(sum_matrix(target, nodes), grad_preact)
        if at == 0:
            by_src[...] = part_src
            by_dst[...] = part_dst
        else:
            by_src[...] += part_src
            by_dst[...] += part_dst
    grad_table = dot_rt(by_src[...].astype(BF), w1_ref[0:feature, :])
    local_ref[...] = (
        grad_fine
        + grad_table[0:nodes, :]
        + dot_rt(by_dst[...].astype(BF), w1_ref[feature:, :])
    )
    ghost[...] = grad_table[nodes:, :].astype(BF)
    to_core = ghost[pl.ds(pl.multiple_of(rim * (1 - core), rim), rim), :]
    give_ref[1920 : 1920 + rim, :] = to_core[:, 0:128]
    give_ref[1920 + rim :, :] = to_core[:, 128:256]
    ghost_b[...] = ghost[pl.ds(pl.multiple_of(rim * core, rim), rim), :]
    for out, at in ((ghost_w, 2 * rim), (ghost_e, 3 * rim)):
        out[0:rim, :] = ghost[at : at + rim, 0:128]
        out[rim:, :] = ghost[at : at + rim, 128:256]
    for out, half in ((give_ref, 1 - core), (keep_ref, core)):
        part = pl.ds(pl.multiple_of(half * 256, 256), 256)
        first = dot_lt(table_ref[...], by_src[:, part].astype(BF)).astype(out.dtype)
        second = dot_lt(table_ref[0:nodes, :], by_dst[:, part].astype(BF)).astype(out.dtype)
        third = dot_lt(acc_ref[:, part], grad_summed).astype(out.dtype)
        for k in range(2):
            lanes = slice(128 * k, 128 * k + 128)
            out[512 * k : 512 * k + 256, :] = first[:, lanes]
            out[512 * k + 256 : 512 * k + 512, :] = second[:, lanes]
            out[1024 + 256 * k : 1280 + 256 * k, :] = third[:, lanes]
        out[1536:1920, :] = coarse_ref[half].astype(out.dtype)


def split_kernel(keep_ref, got_ref, ghost_w, ghost_e, place_ref, total_ref, coarse_ref, *sends):
    col = place_ref[0]

    def block(step):
        rows = pl.ds(pl.multiple_of(lax.rem(col + step, 4) * 384, 384), 384)
        return keep_ref[rows, :] + got_ref[rows, :].astype(F32)

    total_ref[...] = block(0)
    coarse_ref[...] = keep_ref[1536:1920, :] + got_ref[1536:1920, :].astype(F32)
    for step, out in enumerate(sends, 1):
        out[0:384, :] = block(step).astype(BF)
    sends[0][384:, :] = ghost_e[...]
    sends[2][384:, :] = ghost_w[...]


def return_kernel(local_ref, from_core, from_b, from_west, from_east, export_ref, place_ref, out_ref):
    rim = export_ref.shape[1]
    adds = sum_matrix(export_ref[...], local_ref.shape[0])
    col = place_ref[0]

    def wide(ref):
        at = ref.shape[0] - 2 * rim
        rows = ref[at:, :].astype(F32)
        return jnp.concatenate([rows[0:rim, :], rows[rim:, :]], axis=1)

    west = wide(from_west) * jnp.where(col > 0, 1.0, 0.0)
    east = wide(from_east) * jnp.where(col < 3, 1.0, 0.0)
    beyond = from_b[...].astype(F32) * jnp.where(place_ref[3] > 0, 1.0, 0.0)
    arrived = (wide(from_core) + beyond) + (west + east)
    high, low = halves(arrived)
    out_ref[...] = local_ref[...] + dot(adds, high) + dot(adds, low)


def unpack_kernel(
    mine_ref, other_ref, place_ref, fine1_ref, fine2_ref, coarse1_ref, coarse2_ref,
    *, fine_scale, coarse_scale,
):
    for ref, half in ((mine_ref, place_ref[1]), (other_ref, 1 - place_ref[1])):
        for plane in range(16):
            for x in range(4):
                values = ref[plane * 4 + x].astype(F32)
                for at in range(0, 24, 8):
                    row = x * 384 + plane * 24 + at
                    piece = values[at : at + 8, :] * fine_scale
                    if row < 1024:
                        lanes = pl.ds(pl.multiple_of(half * 256 + row // 512 * 128, 128), 128)
                        fine1_ref[row % 512 : row % 512 + 8, lanes] = piece
                    else:
                        start = pl.multiple_of(half * 256 + row % 256, 8)
                        lane = (row - 1024) // 256 * 128
                        fine2_ref[pl.ds(start, 8), lane : lane + 128] = piece
                    row = plane * 24 + at
                    piece = values[24 + at : 32 + at, :] * coarse_scale
                    if row < 256:
                        start = pl.multiple_of(half * 256 + row, 8)
                        coarse1_ref[pl.ds(start, 8), x * 128 : x * 128 + 128] = piece
                    else:
                        start = pl.multiple_of(half * 64 + x * 128 + row % 64, 8)
                        lane = (row - 256) // 64 * 128
                        coarse2_ref[pl.ds(start, 8), lane : lane + 128] = piece


class Late:
    def __init__(self, source, held, sem):
        self.held = held
        self.shape = held.shape
        self.copy = pltpu.make_async_copy(source, held, sem)
        self.copy.start()

    def __getitem__(self, index):
        if self.copy is not None:
            self.copy.wait()
            self.copy = None
        return self.held[index]

    def finish(self):
        if self.copy is not None:
            self.copy.wait()
            self.copy = None


def run(kernel, outs, operands, scratch=(), scalars=(), late=(), inner=(), ahead=(), limit=16, work=0.1):
    size = sum(math.prod(x.shape) * x.dtype.itemsize for x in [*operands, *ahead]) + sum(
        math.prod(shape) * jnp.dtype(kind).itemsize for shape, kind in outs
    )
    shapes = [
        (pltpu.VMEM if i in inner else jax.ShapeDtypeStruct)(shape, kind)
        for i, (shape, kind) in enumerate(outs)
    ] + [pltpu.VMEM(x.shape, x.dtype) for x in ahead]
    operands = [
        pltpu.with_memory_space_constraint(x, pltpu.HBM) if i in late else x
        for i, x in enumerate(operands)
    ] + [pltpu.with_memory_space_constraint(x, pltpu.HBM) for x in ahead]
    count = len(operands) - len(ahead)
    first_out = len(operands)
    first_ahead = first_out + len(outs)
    first_scratch = first_ahead + len(ahead)
    first_held = first_scratch + len(scratch)

    def space(i):
        return pltpu.SMEM if i in scalars else pltpu.HBM if i in late or i >= count else pltpu.VMEM

    def body(*refs):
        sems = refs[-1]
        inputs = list(refs[:count])
        for k, i in enumerate(late):
            inputs[i] = Late(refs[i], refs[first_held + k], sems.at[k])
        fetched = [
            Late(refs[count + k], refs[first_ahead + k], sems.at[len(late) + k])
            for k in range(len(ahead))
        ]
        kernel(*inputs, *refs[first_out:first_ahead], *refs[first_scratch:first_held])
        for copy in [inputs[i] for i in late] + fetched:
            copy.finish()

    copies = len(late) + len(ahead)
    return pl.pallas_call(
        body if copies else kernel,
        out_shape=shapes,
        in_specs=[pl.BlockSpec(memory_space=space(i)) for i in range(first_out)],
        out_specs=[pl.BlockSpec(memory_space=pltpu.VMEM)] * len(shapes),
        scratch_shapes=[pltpu.VMEM(shape, kind) for shape, kind in scratch]
        + [pltpu.VMEM(operands[i].shape, operands[i].dtype) for i in late]
        + ([pltpu.SemaphoreType.DMA((copies,))] if copies else []),
        compiler_params=pltpu.CompilerParams(vmem_limit_bytes=limit * 1024 * 1024),
        cost_estimate=pl.CostEstimate(
            flops=int(2e9 * work), bytes_accessed=size, transcendentals=0
        ),
    )(*operands)


ROW = ("z", "y", "core")
PLANE = ("z", "y")
CHIPS = ("z", "y", "x")


def send(value, axis, step):
    size = lax.axis_size(axis)
    return lax.ppermute(value, axis, [(i, (i + step) % size) for i in range(size)])


def shards(
    latent, cotangent, fine_w1, fine_w2, fine_gain, coarse_w1, coarse_w2, coarse_gain,
    fine_src, fine_dst, live_blocks, export_rows, pool_assign, coarse_src, coarse_dst,
):
    own = latent[0, 0]
    cot = cotangent[0, 0]
    nodes, feature = own.shape
    export = export_rows[0]
    assign = pool_assign[0]
    src, dst = fine_src[0], fine_dst[0]
    rim_count = export.shape[1]
    hidden = fine_w1.shape[1]
    edges, coarse_edges = src.shape[1], coarse_src.shape[1]
    rows, cols = lax.axis_size(ROW), lax.axis_size("x")
    fine_gain = fine_gain[None, :]
    coarse_gain = coarse_gain[None, :]
    between = [(i, i + 1) for i in range(1, rows - 1, 2)]
    between = between + [(target, source) for source, target in between]
    between = between + [(rows - 1, 0), (0, rows - 1)]
    row = lax.axis_index(ROW)
    inside = jnp.logical_and(row > 0, row < rows - 1)
    place = jnp.stack(
        [lax.axis_index("x"), lax.axis_index("core"), 128 * live_blocks[0, 0], inside]
    )
    own, place = lax.optimization_barrier((own, place.astype(jnp.int32)))
    wide = 2 * feature

    rim, pack, target, own_in, src_in, w1_in, w2_in, gain_in, assign_in, export_in = run(
        start_kernel,
        [
            ((rim_count, feature), BF),
            ((CNODE + 32, feature), BF),
            ((1, edges), jnp.int32),
        ],
        [own, export, cot, assign, dst, place],
        scalars=(5,),
        late=(0, 1, 2, 3, 4),
        inner=(0, 1, 2),
        ahead=[own, src, fine_w1, fine_w2, fine_gain, assign, export],
    )
    near, far = [(0, 1), (1, 0), (2, 3), (3, 2)], [(1, 2), (2, 1), (3, 0), (0, 3)]
    pack_got = lax.ppermute(pack, "x", near)
    from_west, from_east = send(rim, "x", 1), send(rim, "x", 3)
    from_a = send(rim, "core", 1)
    from_b = lax.ppermute(rim, ROW, between)
    part, csrc_in, cdst_in, cw1_in, cw2_in, cgain_in, cot_in = run(
        own_kernel,
        [((edges, hidden), F32)],
        [own_in, src_in, target, w1_in],
        inner=(0,),
        ahead=[coarse_src, coarse_dst, coarse_w1, coarse_w2, coarse_gain, cot],
        limit=LIMITS[0],
        work=1.1,
    )
    pack, pack_got, part = lax.optimization_barrier((pack, pack_got, part))
    (pair,) = run(add_kernel, [((CNODE + 32, feature), BF)], [pack, pack_got], inner=(0,))
    pair, part = lax.optimization_barrier((pair, part))
    pair_got = lax.ppermute(pair, "x", far)
    slope, acc, summed, pooled, table = run(
        fine_forward_kernel,
        [
            ((edges, hidden), F32),
            ((nodes, hidden), BF),
            ((nodes, feature), F32),
            ((CNODE, feature), BF),
            ((nodes + 4 * rim_count, feature), BF),
        ],
        [
            part, own_in, from_a, from_b, from_west, from_east, src_in, target, place,
            w1_in, w2_in, gain_in, assign_in,
        ],
        [((nodes, hidden), F32)],
        scalars=(8,),
        inner=(0, 1, 2, 3, 4),
        limit=LIMITS[1],
        work=1.6,
    )
    half_rows = CNODE // 2
    pooled, pair_got = lax.optimization_barrier((pooled, pair_got))
    left, right = send(pooled, "x", 1), send(pooled, "x", 3)
    across = [send(left[:half_rows], "x", 1), send(right[half_rows:], "x", 3)]

    grad_fine, coarse_pack = run(
        coarse_kernel,
        [((nodes, feature), F32), ((2, 384, 128), F32)],
        [
            pooled, left, right, *across, pair, pair_got, csrc_in, cdst_in, cw1_in, cw2_in, cgain_in,
            cot_in, assign_in, place,
        ],
        [
            ((CNODE, feature), BF),
            ((coarse_edges, hidden), F32),
            ((coarse_edges, CNODE), BF),
            ((CNODE, coarse_edges), BF),
            ((CNODE, hidden), F32),
            ((CNODE, hidden), F32),
            ((CNODE, hidden), F32),
        ],
        scalars=(14,),
        inner=(0, 1),
        limit=LIMITS[2],
        work=5.0,
    )

    local, give, keep, ghost_b, ghost_w, ghost_e = run(
        fine_backward_kernel,
        [
            ((nodes, feature), F32),
            ((1920 + 2 * rim_count, 128), BF),
            ((1920, 128), F32),
            ((rim_count, feature), BF),
            ((2 * rim_count, 128), BF),
            ((2 * rim_count, 128), BF),
        ],
        [
            grad_fine, summed, slope, acc, table, src_in, target, place,
            w1_in, w2_in, gain_in, coarse_pack,
        ],
        [
            ((nodes + 4 * rim_count, hidden), F32),
            ((nodes, hidden), F32),
            ((4 * rim_count, feature), BF),
        ],
        scalars=(7,),
        inner=(0, 1, 2, 3, 4, 5),
        limit=LIMITS[3],
        work=2.8,
    )
    from_core = send(give, "core", 1)
    from_b = lax.ppermute(ghost_b, ROW, between)
    total, coarse_total, to_east, to_cross, to_west = run(
        split_kernel,
        [
            ((384, 128), F32),
            ((384, 128), F32),
            ((384 + 2 * rim_count, 128), BF),
            ((384, 128), BF),
            ((384 + 2 * rim_count, 128), BF),
        ],
        [keep, from_core, ghost_w, ghost_e, place],
        scalars=(4,),
        inner=(0, 1, 2, 3, 4),
    )
    from_west = send(to_east, "x", 1)
    from_cross = send(to_cross, "x", 2)
    from_east = send(to_west, "x", 3)
    total = (
        total
        + from_west[0:384].astype(F32)
        + from_cross.astype(F32)
        + from_east[0:384].astype(F32)
    )
    both = jnp.concatenate(
        [total.reshape(16, 24, 128), coarse_total.reshape(16, 24, 128)], axis=1
    ).astype(BF)
    both, from_b = lax.optimization_barrier((both, from_b))
    both = lax.all_to_all(both, PLANE, 0, 0, tiled=True)
    both = jnp.sum(both.astype(F32), axis=0).astype(BF)
    copies = jnp.broadcast_to(both[None], (64,) + both.shape)
    mine = lax.all_to_all(copies, CHIPS, 0, 0, tiled=True)
    mine, local = lax.optimization_barrier((mine, local))
    other = send(mine, "core", 1)
    (grad_latent,) = run(
        return_kernel,
        [((nodes, feature), F32)],
        [local, from_core, from_b, from_west, from_east, export_in, place],
        scalars=(6,),
    )
    unpack = functools.partial(
        unpack_kernel,
        fine_scale=1.0 / math.sqrt(edges * rows * cols),
        coarse_scale=1.0 / math.sqrt(coarse_edges * rows),
    )
    weight_grads = run(
        unpack,
        [
            ((2 * feature, hidden), F32),
            ((hidden, feature), F32),
            ((2 * feature, hidden), F32),
            ((hidden, feature), F32),
        ],
        [mine, other, place],
        scalars=(2,),
    )
    return (grad_latent[None, None], *weight_grads)


def solution(mesh):
    shape = (4, 4, 2, 4)
    inner = Mesh(mesh.devices.reshape(shape), ("z", "y", "core", "x"))
    node_sharded = P(ROW, "x", None, None)
    index_sharded = P(ROW, "x", None)
    placed = (
        node_sharded,
        node_sharded,
        P(),
        P(),
        P(),
        P(),
        P(),
        P(),
        index_sharded,
        index_sharded,
        P(ROW, "x"),
        index_sharded,
        index_sharded,
        P(ROW, None),
        P(ROW, None),
    )
    return jax.shard_map(
        shards,
        mesh=inner,
        in_specs=placed,
        out_specs=(node_sharded, P(), P(), P(), P()),
        check_vma=False,
    )
```

```python
import functools
import math

import jax
import jax.numpy as jnp
from jax import lax
from jax.experimental import pallas as pl
from jax.experimental.pallas import tpu as pltpu
from jax.sharding import Mesh
from jax.sharding import PartitionSpec as P

EPS = 1e-05
CNODE = 512
CHUNK = 1024
LIMITS = (20, 20, 36, 22)
BF = jnp.bfloat16
F32 = jnp.float32


def dot(left, right):
    return lax.dot_general(left, right, (((1,), (0,)), ((), ())), preferred_element_type=F32)


def dot_rt(left, right):
    return lax.dot_general(left, right, (((1,), (1,)), ((), ())), preferred_element_type=F32)


def dot_lt(left, right):
    return lax.dot_general(left, right, (((0,), (0,)), ((), ())), preferred_element_type=F32)


def halves(value):
    high = value.astype(BF)
    return high, (value - high.astype(F32)).astype(BF)


def spread_row(row):
    count = row.shape[1]
    return jnp.concatenate(
        [
            jnp.broadcast_to(row[:, at : at + 128], (128, 128)).T
            for at in range(0, count, 128)
        ],
        axis=0,
    )


def pick_matrix(row, width):
    column = spread_row(row)
    wide = jnp.concatenate([column] * (width // 128), axis=1)
    hit = wide == lax.broadcasted_iota(jnp.int32, wide.shape, 1)
    return jnp.where(hit, 1.0, 0.0).astype(BF)


def sum_matrix(row, width):
    shape = (width, row.shape[1])
    hit = lax.broadcasted_iota(jnp.int32, shape, 0) == row
    return jnp.where(hit, 1.0, 0.0).astype(BF)


def norm_of(summed):
    inverse = lax.rsqrt(jnp.mean(summed * summed, axis=-1, keepdims=True) + EPS)
    return inverse, summed * inverse


def summed_grad(grad_new, gain, summed):
    inverse, normed = norm_of(summed)
    grad_normed = grad_new * gain
    mean = jnp.mean(grad_normed * normed, axis=-1, keepdims=True)
    return (inverse * (grad_normed - normed * mean)).astype(BF)


def activations(preact):
    sig = jax.nn.sigmoid(preact)
    return (preact * sig).astype(BF), sig * (1.0 + preact * (1.0 - sig))


def split_count(count):
    many = jnp.floor(count * (1.0 / 256.0)) * 256.0
    upper = lax.broadcasted_iota(jnp.int32, count.shape, 0) < 8
    return jnp.where(upper, many, count - many).astype(BF)


def whole_count(rows):
    rows = rows.astype(F32)
    parts = [rows[at : at + 1, :] + rows[at + 8 : at + 9, :] for at in (0, 16)]
    return jnp.concatenate(parts, axis=1)


def start_kernel(
    own_ref, export_ref, cot_ref, assign_ref, dst_ref, place_ref, rim_ref, pack_ref, target_ref
):
    rim_ref[...] = dot(pick_matrix(export_ref[...], own_ref.shape[0]), own_ref[...]).astype(BF)
    pool = sum_matrix(assign_ref[...], CNODE)
    pack_ref[0:CNODE, :] = dot(pool, cot_ref[...]).astype(BF)
    packed = split_count(dot_rt(jnp.ones((16, pool.shape[1]), BF), pool))
    pack_ref[CNODE : CNODE + 16, :] = packed[:, :256]
    pack_ref[CNODE + 16 : CNODE + 32, :] = packed[:, 256:]
    slot = lax.broadcasted_iota(jnp.int32, dst_ref.shape, 1)
    target_ref[...] = jnp.where(slot < place_ref[2], dst_ref[...], -1)


def add_kernel(mine_ref, got_ref, out_ref):
    out_ref[0:CNODE, :] = (
        mine_ref[0:CNODE, :].astype(F32) + got_ref[0:CNODE, :].astype(F32)
    ).astype(BF)
    count = whole_count(mine_ref[CNODE:, :]) + whole_count(got_ref[CNODE:, :])
    packed = split_count(jnp.broadcast_to(count, (16, CNODE)))
    out_ref[CNODE : CNODE + 16, :] = packed[:, :256]
    out_ref[CNODE + 16 : CNODE + 32, :] = packed[:, 256:]


def pair_kernel(mine_ref, near_ref, far_ref, first_ref, second_ref):
    half = near_ref.shape[0]
    mine = mine_ref[...].astype(F32)
    first_ref[...] = (mine[0:half] + near_ref[...].astype(F32)).astype(BF)
    second_ref[...] = (mine[half:] + far_ref[...].astype(F32)).astype(BF)


def own_kernel(own_ref, src_ref, target_ref, w1_ref, part_ref):
    nodes, feature = own_ref.shape
    for at in range(0, src_ref.shape[1], CHUNK):
        here = slice(at, at + CHUNK)
        left = dot(pick_matrix(src_ref[:, here], nodes), own_ref[...]).astype(BF)
        right = dot(pick_matrix(target_ref[:, here], nodes), own_ref[...]).astype(BF)
        part_ref[here, :] = dot(left, w1_ref[0:feature, :]) + dot(right, w1_ref[feature:, :])


def fine_forward_kernel(
    part_ref, own_ref, ra, rb, rw, re, src_ref, target_ref, place_ref,
    w1_ref, w2_ref, gain_ref, assign_ref, slope_ref, acc_out, summed_ref, pooled_ref, table, acc,
):
    nodes, feature = own_ref.shape
    rim = ra.shape[0]
    col, core = place_ref[0], place_ref[1]
    table[0:nodes, :] = own_ref[...]
    table[pl.ds(pl.multiple_of(nodes + rim * (1 - core), rim), rim), :] = ra[...]
    beyond = rb[...].astype(F32) * jnp.where(place_ref[3] > 0, 1.0, 0.0)
    table[pl.ds(pl.multiple_of(nodes + rim * core, rim), rim), :] = beyond.astype(BF)
    west = rw[...].astype(F32) * jnp.where(col > 0, 1.0, 0.0)
    east = re[...].astype(F32) * jnp.where(col < 3, 1.0, 0.0)
    table[nodes + 2 * rim : nodes + 3 * rim, :] = west.astype(BF)
    table[nodes + 3 * rim :, :] = east.astype(BF)
    for at in range(0, src_ref.shape[1], CHUNK):
        here = slice(at, at + CHUNK)
        picks = pick_matrix(src_ref[:, here] - nodes, 4 * rim)
        left = dot(picks, table[nodes:, :]).astype(BF)
        preact = part_ref[here, :] + dot(left, w1_ref[0:feature, :])
        hidden, slope = activations(preact)
        slope_ref[here, :] = slope
        part = dot(sum_matrix(target_ref[:, here], nodes), hidden)
        if at == 0:
            acc[...] = part
        else:
            acc[...] += part
    high, low = halves(acc[...])
    acc_out[...] = high
    summed = dot(high, w2_ref[...]) + dot(low, w2_ref[...])
    summed_ref[...] = summed
    _, normed = norm_of(summed)
    fine_new = own_ref[...].astype(F32) + normed * gain_ref[...]
    high, low = halves(fine_new)
    pool = sum_matrix(assign_ref[...], CNODE)
    pooled_ref[...] = (dot(pool, high) + dot(pool, low)).astype(BF)


def coarse_kernel(
    p0, p1, q0, q1, g0, g1, src_ref, dst_ref, w1_ref, w2_ref, gain_ref, cot_ref,
    assign_ref, place_ref, grad_fine_ref, pack_ref,
    table, slope, pick_t, sum_t, acc, by_src, by_dst,
):
    feature = p0.shape[1]
    edges = src_ref.shape[1]
    grad_c1 = g0[0:CNODE, :].astype(F32) + g1[0:CNODE, :].astype(F32)
    count = whole_count(g0[CNODE:, :]) + whole_count(g1[CNODE:, :])
    weight = spread_row(1.0 / jnp.maximum(count, 1.0))
    weight = jnp.concatenate([weight] * (feature // 128), axis=1)
    pooled = jnp.concatenate(
        [
            p0[...].astype(F32) + p1[...].astype(F32),
            q0[...].astype(F32) + q1[...].astype(F32),
        ],
        axis=0,
    )
    table[...] = (pooled * weight).astype(BF)
    for at in range(0, edges, CHUNK):
        here = slice(at, at + CHUNK)
        left = dot(pick_matrix(src_ref[:, here], CNODE), table[...]).astype(BF)
        pick = pick_matrix(dst_ref[:, here], CNODE)
        pick_t[here, :] = pick
        right = dot(pick, table[...]).astype(BF)
        preact = dot(left, w1_ref[0:feature, :]) + dot(right, w1_ref[feature:, :])
        hidden, slope[here, :] = activations(preact)
        adds = sum_matrix(dst_ref[:, here], CNODE)
        sum_t[:, here] = adds
        part = dot(adds, hidden)
        if at == 0:
            acc[...] = part
        else:
            acc[...] += part
    high, low = halves(acc[...])
    summed = dot(high, w2_ref[...]) + dot(low, w2_ref[...])
    grad_summed = summed_grad(grad_c1, gain_ref[...], summed)
    for at in range(0, edges, CHUNK):
        here = slice(at, at + CHUNK)
        grad_message = dot(pick_t[here, :], grad_summed).astype(BF)
        grad_preact = (dot_rt(grad_message, w2_ref[...]) * slope[here, :]).astype(BF)
        part_src = dot(sum_matrix(src_ref[:, here], CNODE), grad_preact)
        part_dst = dot(sum_t[:, here], grad_preact)
        if at == 0:
            by_src[...] = part_src
            by_dst[...] = part_dst
        else:
            by_src[...] += part_src
            by_dst[...] += part_dst
    grad_c0 = (
        grad_c1
        + dot_rt(by_src[...].astype(BF), w1_ref[0:feature, :])
        + dot_rt(by_dst[...].astype(BF), w1_ref[feature:, :])
    )
    high, low = halves(grad_c0 * weight)
    spread = pick_matrix(assign_ref[...], CNODE)
    grad_fine_ref[...] = cot_ref[...].astype(F32) + dot(spread, high) + dot(spread, low)
    own = pl.ds(pl.multiple_of(place_ref[0] * 128, 128), 128)
    for half, rows in enumerate((by_src, by_dst)):
        pack_ref[half, 0:256, :] = dot_lt(table[...], rows[:, own].astype(BF))
    second = dot_lt(acc[:, own].astype(BF), grad_summed)
    for half in range(2):
        for k in range(2):
            pack_ref[half, 256 + 64 * k : 320 + 64 * k, :] = second[
                64 * half : 64 * half + 64, 128 * k : 128 * k + 128
            ]


def fine_backward_kernel(
    grad_fine_ref, summed_ref, slope_ref, acc_ref, table_ref, src_ref, target_ref,
    place_ref, w1_ref, w2_ref, gain_ref, coarse_ref,
    local_ref, give_ref, keep_ref, ghost_b, ghost_w, ghost_e, by_src, by_dst, ghost,
):
    nodes, feature = grad_fine_ref.shape
    rim = ghost_b.shape[0]
    core = place_ref[1]
    grad_fine = grad_fine_ref[...]
    grad_summed = summed_grad(grad_fine, gain_ref[...], summed_ref[...])
    for at in range(0, src_ref.shape[1], CHUNK):
        here = slice(at, at + CHUNK)
        target = target_ref[:, here]
        grad_message = dot(pick_matrix(target, nodes), grad_summed).astype(BF)
        grad_preact = (dot_rt(grad_message, w2_ref[...]) * slope_ref[here, :]).astype(BF)
        part_src = dot(sum_matrix(src_ref[:, here], table_ref.shape[0]), grad_preact)
        part_dst = dot(sum_matrix(target, nodes), grad_preact)
        if at == 0:
            by_src[...] = part_src
            by_dst[...] = part_dst
        else:
            by_src[...] += part_src
            by_dst[...] += part_dst
    grad_table = dot_rt(by_src[...].astype(BF), w1_ref[0:feature, :])
    local_ref[...] = (
        grad_fine
        + grad_table[0:nodes, :]
        + dot_rt(by_dst[...].astype(BF), w1_ref[feature:, :])
    )
    ghost[...] = grad_table[nodes:, :].astype(BF)
    to_core = ghost[pl.ds(pl.multiple_of(rim * (1 - core), rim), rim), :]
    give_ref[1920 : 1920 + rim, :] = to_core[:, 0:128]
    give_ref[1920 + rim :, :] = to_core[:, 128:256]
    ghost_b[...] = ghost[pl.ds(pl.multiple_of(rim * core, rim), rim), :]
    for out, at in ((ghost_w, 2 * rim), (ghost_e, 3 * rim)):
        out[0:rim, :] = ghost[at : at + rim, 0:128]
        out[rim:, :] = ghost[at : at + rim, 128:256]
    for out, half in ((give_ref, 1 - core), (keep_ref, core)):
        part = pl.ds(pl.multiple_of(half * 256, 256), 256)
        first = dot_lt(table_ref[...], by_src[:, part].astype(BF)).astype(out.dtype)
        second = dot_lt(table_ref[0:nodes, :], by_dst[:, part].astype(BF)).astype(out.dtype)
        third = dot_lt(acc_ref[:, part], grad_summed).astype(out.dtype)
        for k in range(2):
            lanes = slice(128 * k, 128 * k + 128)
            out[512 * k : 512 * k + 256, :] = first[:, lanes]
            out[512 * k + 256 : 512 * k + 512, :] = second[:, lanes]
            out[1024 + 256 * k : 1280 + 256 * k, :] = third[:, lanes]
        out[1536:1920, :] = coarse_ref[half].astype(out.dtype)


def split_kernel(keep_ref, got_ref, ghost_w, ghost_e, place_ref, total_ref, coarse_ref, *sends):
    col = place_ref[0]

    def block(step):
        rows = pl.ds(pl.multiple_of(lax.rem(col + step, 4) * 384, 384), 384)
        return keep_ref[rows, :] + got_ref[rows, :].astype(F32)

    total_ref[...] = block(0)
    coarse_ref[...] = keep_ref[1536:1920, :] + got_ref[1536:1920, :].astype(F32)
    for step, out in enumerate(sends, 1):
        out[0:384, :] = block(step).astype(BF)
    sends[0][384:, :] = ghost_e[...]
    sends[2][384:, :] = ghost_w[...]


def return_kernel(local_ref, from_core, from_b, from_west, from_east, export_ref, place_ref, out_ref):
    rim = export_ref.shape[1]
    adds = sum_matrix(export_ref[...], local_ref.shape[0])
    col = place_ref[0]

    def wide(ref):
        at = ref.shape[0] - 2 * rim
        rows = ref[at:, :].astype(F32)
        return jnp.concatenate([rows[0:rim, :], rows[rim:, :]], axis=1)

    west = wide(from_west) * jnp.where(col > 0, 1.0, 0.0)
    east = wide(from_east) * jnp.where(col < 3, 1.0, 0.0)
    beyond = from_b[...].astype(F32) * jnp.where(place_ref[3] > 0, 1.0, 0.0)
    arrived = (wide(from_core) + beyond) + (west + east)
    high, low = halves(arrived)
    out_ref[...] = local_ref[...] + dot(adds, high) + dot(adds, low)


def unpack_kernel(
    mine_ref, other_ref, place_ref, fine1_ref, fine2_ref, coarse1_ref, coarse2_ref,
    *, fine_scale, coarse_scale,
):
    for ref, half in ((mine_ref, place_ref[1]), (other_ref, 1 - place_ref[1])):
        for plane in range(16):
            for x in range(4):
                values = ref[plane * 4 + x].astype(F32)
                for at in range(0, 24, 8):
                    row = x * 384 + plane * 24 + at
                    piece = values[at : at + 8, :] * fine_scale
                    if row < 1024:
                        lanes = pl.ds(pl.multiple_of(half * 256 + row // 512 * 128, 128), 128)
                        fine1_ref[row % 512 : row % 512 + 8, lanes] = piece
                    else:
                        start = pl.multiple_of(half * 256 + row % 256, 8)
                        lane = (row - 1024) // 256 * 128
                        fine2_ref[pl.ds(start, 8), lane : lane + 128] = piece
                    row = plane * 24 + at
                    piece = values[24 + at : 32 + at, :] * coarse_scale
                    if row < 256:
                        start = pl.multiple_of(half * 256 + row, 8)
                        coarse1_ref[pl.ds(start, 8), x * 128 : x * 128 + 128] = piece
                    else:
                        start = pl.multiple_of(half * 64 + x * 128 + row % 64, 8)
                        lane = (row - 256) // 64 * 128
                        coarse2_ref[pl.ds(start, 8), lane : lane + 128] = piece


class Late:
    def __init__(self, source, held, sem):
        self.held = held
        self.shape = held.shape
        self.copy = pltpu.make_async_copy(source, held, sem)
        self.copy.start()

    def __getitem__(self, index):
        if self.copy is not None:
            self.copy.wait()
            self.copy = None
        return self.held[index]

    def finish(self):
        if self.copy is not None:
            self.copy.wait()
            self.copy = None


def run(kernel, outs, operands, scratch=(), scalars=(), late=(), inner=(), ahead=(), limit=16, work=0.1):
    size = sum(math.prod(x.shape) * x.dtype.itemsize for x in [*operands, *ahead]) + sum(
        math.prod(shape) * jnp.dtype(kind).itemsize for shape, kind in outs
    )
    shapes = [
        (pltpu.VMEM if i in inner else jax.ShapeDtypeStruct)(shape, kind)
        for i, (shape, kind) in enumerate(outs)
    ] + [pltpu.VMEM(x.shape, x.dtype) for x in ahead]
    operands = [
        pltpu.with_memory_space_constraint(x, pltpu.HBM) if i in late else x
        for i, x in enumerate(operands)
    ] + [pltpu.with_memory_space_constraint(x, pltpu.HBM) for x in ahead]
    count = len(operands) - len(ahead)
    first_out = len(operands)
    first_ahead = first_out + len(outs)
    first_scratch = first_ahead + len(ahead)
    first_held = first_scratch + len(scratch)

    def space(i):
        return pltpu.SMEM if i in scalars else pltpu.HBM if i in late or i >= count else pltpu.VMEM

    def body(*refs):
        sems = refs[-1]
        inputs = list(refs[:count])
        for k, i in enumerate(late):
            inputs[i] = Late(refs[i], refs[first_held + k], sems.at[k])
        fetched = [
            Late(refs[count + k], refs[first_ahead + k], sems.at[len(late) + k])
            for k in range(len(ahead))
        ]
        kernel(*inputs, *refs[first_out:first_ahead], *refs[first_scratch:first_held])
        for copy in [inputs[i] for i in late] + fetched:
            copy.finish()

    copies = len(late) + len(ahead)
    return pl.pallas_call(
        body if copies else kernel,
        out_shape=shapes,
        in_specs=[pl.BlockSpec(memory_space=space(i)) for i in range(first_out)],
        out_specs=[pl.BlockSpec(memory_space=pltpu.VMEM)] * len(shapes),
        scratch_shapes=[pltpu.VMEM(shape, kind) for shape, kind in scratch]
        + [pltpu.VMEM(operands[i].shape, operands[i].dtype) for i in late]
        + ([pltpu.SemaphoreType.DMA((copies,))] if copies else []),
        compiler_params=pltpu.CompilerParams(vmem_limit_bytes=limit * 1024 * 1024),
        cost_estimate=pl.CostEstimate(
            flops=int(2e9 * work), bytes_accessed=size, transcendentals=0
        ),
    )(*operands)


ROW = ("z", "y", "core")
PLANE = ("z", "y")
CHIPS = ("z", "y", "x")


def send(value, axis, step):
    size = lax.axis_size(axis)
    return lax.ppermute(value, axis, [(i, (i + step) % size) for i in range(size)])


def shards(
    latent, cotangent, fine_w1, fine_w2, fine_gain, coarse_w1, coarse_w2, coarse_gain,
    fine_src, fine_dst, live_blocks, export_rows, pool_assign, coarse_src, coarse_dst,
):
    own = latent[0, 0]
    cot = cotangent[0, 0]
    nodes, feature = own.shape
    export = export_rows[0]
    assign = pool_assign[0]
    src, dst = fine_src[0], fine_dst[0]
    rim_count = export.shape[1]
    hidden = fine_w1.shape[1]
    edges, coarse_edges = src.shape[1], coarse_src.shape[1]
    rows, cols = lax.axis_size(ROW), lax.axis_size("x")
    fine_gain = fine_gain[None, :]
    coarse_gain = coarse_gain[None, :]
    between = [(i, i + 1) for i in range(1, rows - 1, 2)]
    between = between + [(target, source) for source, target in between]
    between = between + [(rows - 1, 0), (0, rows - 1)]
    row = lax.axis_index(ROW)
    inside = jnp.logical_and(row > 0, row < rows - 1)
    place = jnp.stack(
        [lax.axis_index("x"), lax.axis_index("core"), 128 * live_blocks[0, 0], inside]
    )
    own, place = lax.optimization_barrier((own, place.astype(jnp.int32)))
    wide = 2 * feature

    rim, pack, target, own_in, src_in, w1_in, w2_in, gain_in, assign_in, export_in = run(
        start_kernel,
        [
            ((rim_count, feature), BF),
            ((CNODE + 32, feature), BF),
            ((1, edges), jnp.int32),
        ],
        [own, export, cot, assign, dst, place],
        scalars=(5,),
        late=(0, 1, 2, 3, 4),
        inner=(0, 1, 2),
        ahead=[own, src, fine_w1, fine_w2, fine_gain, assign, export],
    )
    near, far = [(0, 1), (1, 0), (2, 3), (3, 2)], [(1, 2), (2, 1), (3, 0), (0, 3)]
    pack_got = lax.ppermute(pack, "x", near)
    from_west, from_east = send(rim, "x", 1), send(rim, "x", 3)
    from_a = send(rim, "core", 1)
    from_b = lax.ppermute(rim, ROW, between)
    part, csrc_in, cdst_in, cw1_in, cw2_in, cgain_in, cot_in = run(
        own_kernel,
        [((edges, hidden), F32)],
        [own_in, src_in, target, w1_in],
        inner=(0,),
        ahead=[coarse_src, coarse_dst, coarse_w1, coarse_w2, coarse_gain, cot],
        limit=LIMITS[0],
        work=1.1,
    )
    pack, pack_got, part = lax.optimization_barrier((pack, pack_got, part))
    (pair,) = run(add_kernel, [((CNODE + 32, feature), BF)], [pack, pack_got], inner=(0,))
    pair, part = lax.optimization_barrier((pair, part))
    pair_got = lax.ppermute(pair, "x", far)
    slope, acc, summed, pooled, table = run(
        fine_forward_kernel,
        [
            ((edges, hidden), F32),
            ((nodes, hidden), BF),
            ((nodes, feature), F32),
            ((CNODE, feature), BF),
            ((nodes + 4 * rim_count, feature), BF),
        ],
        [
            part, own_in, from_a, from_b, from_west, from_east, src_in, target, place,
            w1_in, w2_in, gain_in, assign_in,
        ],
        [((nodes, hidden), F32)],
        scalars=(8,),
        inner=(0, 1, 2, 3, 4),
        limit=LIMITS[1],
        work=1.6,
    )
    pooled, pair_got = lax.optimization_barrier((pooled, pair_got))
    half_rows = CNODE // 2
    got = [
        lax.ppermute(pooled[:half_rows], "x", near),
        lax.ppermute(pooled[half_rows:], "x", far),
    ]
    first, second = run(
        pair_kernel, [((half_rows, feature), BF)] * 2, [pooled, *got], inner=(0, 1)
    )
    got = [lax.ppermute(first, "x", far), lax.ppermute(second, "x", near)]

    grad_fine, coarse_pack = run(
        coarse_kernel,
        [((nodes, feature), F32), ((2, 384, 128), F32)],
        [
            first, got[0], second, got[1], pair, pair_got, csrc_in, cdst_in, cw1_in, cw2_in, cgain_in,
            cot_in, assign_in, place,
        ],
        [
            ((CNODE, feature), BF),
            ((coarse_edges, hidden), F32),
            ((coarse_edges, CNODE), BF),
            ((CNODE, coarse_edges), BF),
            ((CNODE, hidden), F32),
            ((CNODE, hidden), F32),
            ((CNODE, hidden), F32),
        ],
        scalars=(13,),
        inner=(0, 1),
        limit=LIMITS[2],
        work=5.0,
    )

    local, give, keep, ghost_b, ghost_w, ghost_e = run(
        fine_backward_kernel,
        [
            ((nodes, feature), F32),
            ((1920 + 2 * rim_count, 128), BF),
            ((1920, 128), F32),
            ((rim_count, feature), BF),
            ((2 * rim_count, 128), BF),
            ((2 * rim_count, 128), BF),
        ],
        [
            grad_fine, summed, slope, acc, table, src_in, target, place,
            w1_in, w2_in, gain_in, coarse_pack,
        ],
        [
            ((nodes + 4 * rim_count, hidden), F32),
            ((nodes, hidden), F32),
            ((4 * rim_count, feature), BF),
        ],
        scalars=(7,),
        inner=(0, 1, 2, 3, 4, 5),
        limit=LIMITS[3],
        work=2.8,
    )
    from_core = send(give, "core", 1)
    from_b = lax.ppermute(ghost_b, ROW, between)
    total, coarse_total, to_east, to_cross, to_west = run(
        split_kernel,
        [
            ((384, 128), F32),
            ((384, 128), F32),
            ((384 + 2 * rim_count, 128), BF),
            ((384, 128), BF),
            ((384 + 2 * rim_count, 128), BF),
        ],
        [keep, from_core, ghost_w, ghost_e, place],
        scalars=(4,),
        inner=(0, 1, 2, 3, 4),
    )
    from_west = send(to_east, "x", 1)
    from_cross = send(to_cross, "x", 2)
    from_east = send(to_west, "x", 3)
    total = (
        total
        + from_west[0:384].astype(F32)
        + from_cross.astype(F32)
        + from_east[0:384].astype(F32)
    )
    both = jnp.concatenate(
        [total.reshape(16, 24, 128), coarse_total.reshape(16, 24, 128)], axis=1
    ).astype(BF)
    both, from_b = lax.optimization_barrier((both, from_b))
    both = lax.all_to_all(both, PLANE, 0, 0, tiled=True)
    both = jnp.sum(both.astype(F32), axis=0).astype(BF)
    copies = jnp.broadcast_to(both[None], (64,) + both.shape)
    mine = lax.all_to_all(copies, CHIPS, 0, 0, tiled=True)
    mine, local = lax.optimization_barrier((mine, local))
    other = send(mine, "core", 1)
    (grad_latent,) = run(
        return_kernel,
        [((nodes, feature), F32)],
        [local, from_core, from_b, from_west, from_east, export_in, place],
        scalars=(6,),
    )
    unpack = functools.partial(
        unpack_kernel,
        fine_scale=1.0 / math.sqrt(edges * rows * cols),
        coarse_scale=1.0 / math.sqrt(coarse_edges * rows),
    )
    weight_grads = run(
        unpack,
        [
            ((2 * feature, hidden), F32),
            ((hidden, feature), F32),
            ((2 * feature, hidden), F32),
            ((hidden, feature), F32),
        ],
        [mine, other, place],
        scalars=(2,),
    )
    return (grad_latent[None, None], *weight_grads)


def solution(mesh):
    shape = (4, 4, 2, 4)
    inner = Mesh(mesh.devices.reshape(shape), ("z", "y", "core", "x"))
    node_sharded = P(ROW, "x", None, None)
    index_sharded = P(ROW, "x", None)
    placed = (
        node_sharded,
        node_sharded,
        P(),
        P(),
        P(),
        P(),
        P(),
        P(),
        index_sharded,
        index_sharded,
        P(ROW, "x"),
        index_sharded,
        index_sharded,
        P(ROW, None),
        P(ROW, None),
    )
    return jax.shard_map(
        shards,
        mesh=inner,
        in_specs=placed,
        out_specs=(node_sharded, P(), P(), P(), P()),
        check_vma=False,
    )
```

```python
import functools
import math

import jax
import jax.numpy as jnp
from jax import lax
from jax.experimental import pallas as pl
from jax.experimental.pallas import tpu as pltpu
from jax.sharding import Mesh
from jax.sharding import PartitionSpec as P

EPS = 1e-05
CNODE = 512
CHUNK = 1024
LIMITS = (20, 20, 36, 22)
BF = jnp.bfloat16
F32 = jnp.float32


def dot(left, right):
    return lax.dot_general(left, right, (((1,), (0,)), ((), ())), preferred_element_type=F32)


def dot_rt(left, right):
    return lax.dot_general(left, right, (((1,), (1,)), ((), ())), preferred_element_type=F32)


def dot_lt(left, right):
    return lax.dot_general(left, right, (((0,), (0,)), ((), ())), preferred_element_type=F32)


def halves(value):
    high = value.astype(BF)
    return high, (value - high.astype(F32)).astype(BF)


def spread_row(row):
    count = row.shape[1]
    return jnp.concatenate(
        [
            jnp.broadcast_to(row[:, at : at + 128], (128, 128)).T
            for at in range(0, count, 128)
        ],
        axis=0,
    )


def pick_matrix(row, width):
    column = spread_row(row)
    wide = jnp.concatenate([column] * (width // 128), axis=1)
    hit = wide == lax.broadcasted_iota(jnp.int32, wide.shape, 1)
    return jnp.where(hit, 1.0, 0.0).astype(BF)


def sum_matrix(row, width):
    shape = (width, row.shape[1])
    hit = lax.broadcasted_iota(jnp.int32, shape, 0) == row
    return jnp.where(hit, 1.0, 0.0).astype(BF)


def norm_of(summed):
    inverse = lax.rsqrt(jnp.mean(summed * summed, axis=-1, keepdims=True) + EPS)
    return inverse, summed * inverse


def summed_grad(grad_new, gain, summed):
    inverse, normed = norm_of(summed)
    grad_normed = grad_new * gain
    mean = jnp.mean(grad_normed * normed, axis=-1, keepdims=True)
    return (inverse * (grad_normed - normed * mean)).astype(BF)


def activations(preact):
    sig = jax.nn.sigmoid(preact)
    return (preact * sig).astype(BF), sig * (1.0 + preact * (1.0 - sig))


def split_count(count):
    many = jnp.floor(count * (1.0 / 256.0)) * 256.0
    upper = lax.broadcasted_iota(jnp.int32, count.shape, 0) < 8
    return jnp.where(upper, many, count - many).astype(BF)


def whole_count(rows):
    rows = rows.astype(F32)
    parts = [rows[at : at + 1, :] + rows[at + 8 : at + 9, :] for at in (0, 16)]
    return jnp.concatenate(parts, axis=1)


def start_kernel(
    own_ref, export_ref, cot_ref, assign_ref, dst_ref, place_ref, rim_ref, pack_ref, target_ref
):
    rim_ref[...] = dot(pick_matrix(export_ref[...], own_ref.shape[0]), own_ref[...]).astype(BF)
    pool = sum_matrix(assign_ref[...], CNODE)
    pack_ref[0:CNODE, :] = dot(pool, cot_ref[...]).astype(BF)
    packed = split_count(dot_rt(jnp.ones((16, pool.shape[1]), BF), pool))
    pack_ref[CNODE : CNODE + 16, :] = packed[:, :256]
    pack_ref[CNODE + 16 : CNODE + 32, :] = packed[:, 256:]
    slot = lax.broadcasted_iota(jnp.int32, dst_ref.shape, 1)
    target_ref[...] = jnp.where(slot < place_ref[2], dst_ref[...], -1)


def add_kernel(mine_ref, got_ref, out_ref):
    out_ref[0:CNODE, :] = (
        mine_ref[0:CNODE, :].astype(F32) + got_ref[0:CNODE, :].astype(F32)
    ).astype(BF)
    count = whole_count(mine_ref[CNODE:, :]) + whole_count(got_ref[CNODE:, :])
    packed = split_count(jnp.broadcast_to(count, (16, CNODE)))
    out_ref[CNODE : CNODE + 16, :] = packed[:, :256]
    out_ref[CNODE + 16 : CNODE + 32, :] = packed[:, 256:]


def pair_kernel(mine_ref, near_ref, far_ref, first_ref, second_ref):
    half = near_ref.shape[0]
    mine = mine_ref[...].astype(F32)
    first_ref[...] = (mine[0:half] + near_ref[...].astype(F32)).astype(BF)
    second_ref[...] = (mine[half:] + far_ref[...].astype(F32)).astype(BF)


def own_kernel(own_ref, src_ref, target_ref, w1_ref, part_ref, left_ref):
    nodes, feature = own_ref.shape
    for at in range(0, src_ref.shape[1], CHUNK):
        here = slice(at, at + CHUNK)
        left = dot(pick_matrix(src_ref[:, here], nodes), own_ref[...]).astype(BF)
        left_ref[here, :] = left
        right = dot(pick_matrix(target_ref[:, here], nodes), own_ref[...]).astype(BF)
        part_ref[here, :] = dot(left, w1_ref[0:feature, :]) + dot(right, w1_ref[feature:, :])


def fine_forward_kernel(
    part_ref, left_ref, own_ref, ra, rb, rw, re, src_ref, target_ref, place_ref,
    w1_ref, w2_ref, gain_ref, assign_ref, slope_ref, acc_out, summed_ref, pooled_ref, pair_ref, table, acc,
):
    nodes, feature = own_ref.shape
    rim = ra.shape[0]
    col, core = place_ref[0], place_ref[1]
    table[0:nodes, :] = own_ref[...]
    table[pl.ds(pl.multiple_of(nodes + rim * (1 - core), rim), rim), :] = ra[...]
    beyond = rb[...].astype(F32) * jnp.where(place_ref[3] > 0, 1.0, 0.0)
    table[pl.ds(pl.multiple_of(nodes + rim * core, rim), rim), :] = beyond.astype(BF)
    west = rw[...].astype(F32) * jnp.where(col > 0, 1.0, 0.0)
    east = re[...].astype(F32) * jnp.where(col < 3, 1.0, 0.0)
    table[nodes + 2 * rim : nodes + 3 * rim, :] = west.astype(BF)
    table[nodes + 3 * rim :, :] = east.astype(BF)
    for at in range(0, src_ref.shape[1], CHUNK):
        here = slice(at, at + CHUNK)
        picks = pick_matrix(src_ref[:, here] - nodes, 4 * rim)
        left = dot(picks, table[nodes:, :]).astype(BF)
        pair_ref[here, :] = left + left_ref[here, :]
        preact = part_ref[here, :] + dot(left, w1_ref[0:feature, :])
        hidden, slope = activations(preact)
        slope_ref[here, :] = slope
        part = dot(sum_matrix(target_ref[:, here], nodes), hidden)
        if at == 0:
            acc[...] = part
        else:
            acc[...] += part
    high, low = halves(acc[...])
    acc_out[...] = high
    summed = dot(high, w2_ref[...]) + dot(low, w2_ref[...])
    summed_ref[...] = summed
    _, normed = norm_of(summed)
    fine_new = own_ref[...].astype(F32) + normed * gain_ref[...]
    high, low = halves(fine_new)
    pool = sum_matrix(assign_ref[...], CNODE)
    pooled_ref[...] = (dot(pool, high) + dot(pool, low)).astype(BF)


def coarse_kernel(
    p0, p1, q0, q1, g0, g1, src_ref, dst_ref, w1_ref, w2_ref, gain_ref, cot_ref,
    assign_ref, place_ref, grad_fine_ref, pack_ref,
    table, slope, pick_t, sum_t, acc, by_src, by_dst,
):
    feature = p0.shape[1]
    edges = src_ref.shape[1]
    grad_c1 = g0[0:CNODE, :].astype(F32) + g1[0:CNODE, :].astype(F32)
    count = whole_count(g0[CNODE:, :]) + whole_count(g1[CNODE:, :])
    weight = spread_row(1.0 / jnp.maximum(count, 1.0))
    weight = jnp.concatenate([weight] * (feature // 128), axis=1)
    pooled = jnp.concatenate(
        [
            p0[...].astype(F32) + p1[...].astype(F32),
            q0[...].astype(F32) + q1[...].astype(F32),
        ],
        axis=0,
    )
    table[...] = (pooled * weight).astype(BF)
    for at in range(0, edges, CHUNK):
        here = slice(at, at + CHUNK)
        left = dot(pick_matrix(src_ref[:, here], CNODE), table[...]).astype(BF)
        pick = pick_matrix(dst_ref[:, here], CNODE)
        pick_t[here, :] = pick
        right = dot(pick, table[...]).astype(BF)
        preact = dot(left, w1_ref[0:feature, :]) + dot(right, w1_ref[feature:, :])
        hidden, slope[here, :] = activations(preact)
        adds = sum_matrix(dst_ref[:, here], CNODE)
        sum_t[:, here] = adds
        part = dot(adds, hidden)
        if at == 0:
            acc[...] = part
        else:
            acc[...] += part
    high, low = halves(acc[...])
    summed = dot(high, w2_ref[...]) + dot(low, w2_ref[...])
    grad_summed = summed_grad(grad_c1, gain_ref[...], summed)
    for at in range(0, edges, CHUNK):
        here = slice(at, at + CHUNK)
        grad_message = dot(pick_t[here, :], grad_summed).astype(BF)
        grad_preact = (dot_rt(grad_message, w2_ref[...]) * slope[here, :]).astype(BF)
        part_src = dot(sum_matrix(src_ref[:, here], CNODE), grad_preact)
        part_dst = dot(sum_t[:, here], grad_preact)
        if at == 0:
            by_src[...] = part_src
            by_dst[...] = part_dst
        else:
            by_src[...] += part_src
            by_dst[...] += part_dst
    grad_c0 = (
        grad_c1
        + dot_rt(by_src[...].astype(BF), w1_ref[0:feature, :])
        + dot_rt(by_dst[...].astype(BF), w1_ref[feature:, :])
    )
    high, low = halves(grad_c0 * weight)
    spread = pick_matrix(assign_ref[...], CNODE)
    grad_fine_ref[...] = cot_ref[...].astype(F32) + dot(spread, high) + dot(spread, low)
    own = pl.ds(pl.multiple_of(place_ref[0] * 128, 128), 128)
    for half, rows in enumerate((by_src, by_dst)):
        pack_ref[half, 0:256, :] = dot_lt(table[...], rows[:, own].astype(BF))
    second = dot_lt(acc[:, own].astype(BF), grad_summed)
    for half in range(2):
        for k in range(2):
            pack_ref[half, 256 + 64 * k : 320 + 64 * k, :] = second[
                64 * half : 64 * half + 64, 128 * k : 128 * k + 128
            ]


def fine_backward_kernel(
    grad_fine_ref, summed_ref, slope_ref, acc_ref, left_ref, own_ref, src_ref, target_ref,
    place_ref, w1_ref, w2_ref, gain_ref, coarse_ref,
    local_ref, give_ref, keep_ref, ghost_b, ghost_w, ghost_e, by_src, by_dst, ghost, grad_left,
):
    nodes, feature = grad_fine_ref.shape
    rim = ghost_b.shape[0]
    core = place_ref[1]
    grad_fine = grad_fine_ref[...]
    grad_summed = summed_grad(grad_fine, gain_ref[...], summed_ref[...])
    for at in range(0, src_ref.shape[1], CHUNK):
        here = slice(at, at + CHUNK)
        target = target_ref[:, here]
        grad_message = dot(pick_matrix(target, nodes), grad_summed).astype(BF)
        grad_preact = (dot_rt(grad_message, w2_ref[...]) * slope_ref[here, :]).astype(BF)
        back = dot_rt(grad_preact, w1_ref[0:feature, :]).astype(BF)
        part_src = dot(sum_matrix(src_ref[:, here], by_src.shape[0]), back)
        part_left = dot_lt(left_ref[here, :], grad_preact)
        part_dst = dot(sum_matrix(target, nodes), grad_preact)
        if at == 0:
            by_src[...] = part_src
            grad_left[...] = part_left
            by_dst[...] = part_dst
        else:
            by_src[...] += part_src
            grad_left[...] += part_left
            by_dst[...] += part_dst
    local_ref[...] = (
        grad_fine
        + by_src[0:nodes, :]
        + dot_rt(by_dst[...].astype(BF), w1_ref[feature:, :])
    )
    ghost[...] = by_src[nodes:, :].astype(BF)
    to_core = ghost[pl.ds(pl.multiple_of(rim * (1 - core), rim), rim), :]
    give_ref[1920 : 1920 + rim, :] = to_core[:, 0:128]
    give_ref[1920 + rim :, :] = to_core[:, 128:256]
    ghost_b[...] = ghost[pl.ds(pl.multiple_of(rim * core, rim), rim), :]
    for out, at in ((ghost_w, 2 * rim), (ghost_e, 3 * rim)):
        out[0:rim, :] = ghost[at : at + rim, 0:128]
        out[rim:, :] = ghost[at : at + rim, 128:256]
    for out, half in ((give_ref, 1 - core), (keep_ref, core)):
        part = pl.ds(pl.multiple_of(half * 256, 256), 256)
        first = grad_left[:, part].astype(out.dtype)
        second = dot_lt(own_ref[...], by_dst[:, part].astype(BF)).astype(out.dtype)
        third = dot_lt(acc_ref[:, part], grad_summed).astype(out.dtype)
        for k in range(2):
            lanes = slice(128 * k, 128 * k + 128)
            out[512 * k : 512 * k + 256, :] = first[:, lanes]
            out[512 * k + 256 : 512 * k + 512, :] = second[:, lanes]
            out[1024 + 256 * k : 1280 + 256 * k, :] = third[:, lanes]
        out[1536:1920, :] = coarse_ref[half].astype(out.dtype)


def split_kernel(keep_ref, got_ref, ghost_w, ghost_e, place_ref, total_ref, coarse_ref, *sends):
    col = place_ref[0]

    def block(step):
        rows = pl.ds(pl.multiple_of(lax.rem(col + step, 4) * 384, 384), 384)
        return keep_ref[rows, :] + got_ref[rows, :].astype(F32)

    total_ref[...] = block(0)
    coarse_ref[...] = keep_ref[1536:1920, :] + got_ref[1536:1920, :].astype(F32)
    for step, out in enumerate(sends, 1):
        out[0:384, :] = block(step).astype(BF)
    sends[0][384:, :] = ghost_e[...]
    sends[2][384:, :] = ghost_w[...]


def return_kernel(local_ref, from_core, from_b, from_west, from_east, export_ref, place_ref, out_ref):
    rim = export_ref.shape[1]
    adds = sum_matrix(export_ref[...], local_ref.shape[0])
    col = place_ref[0]

    def wide(ref):
        at = ref.shape[0] - 2 * rim
        rows = ref[at:, :].astype(F32)
        return jnp.concatenate([rows[0:rim, :], rows[rim:, :]], axis=1)

    west = wide(from_west) * jnp.where(col > 0, 1.0, 0.0)
    east = wide(from_east) * jnp.where(col < 3, 1.0, 0.0)
    beyond = from_b[...].astype(F32) * jnp.where(place_ref[3] > 0, 1.0, 0.0)
    arrived = (wide(from_core) + beyond) + (west + east)
    high, low = halves(arrived)
    out_ref[...] = local_ref[...] + dot(adds, high) + dot(adds, low)


def unpack_kernel(
    mine_ref, other_ref, place_ref, fine1_ref, fine2_ref, coarse1_ref, coarse2_ref,
    *, fine_scale, coarse_scale,
):
    for ref, half in ((mine_ref, place_ref[1]), (other_ref, 1 - place_ref[1])):
        for plane in range(16):
            for x in range(4):
                values = ref[plane * 4 + x].astype(F32)
                for at in range(0, 24, 8):
                    row = x * 384 + plane * 24 + at
                    piece = values[at : at + 8, :] * fine_scale
                    if row < 1024:
                        lanes = pl.ds(pl.multiple_of(half * 256 + row // 512 * 128, 128), 128)
                        fine1_ref[row % 512 : row % 512 + 8, lanes] = piece
                    else:
                        start = pl.multiple_of(half * 256 + row % 256, 8)
                        lane = (row - 1024) // 256 * 128
                        fine2_ref[pl.ds(start, 8), lane : lane + 128] = piece
                    row = plane * 24 + at
                    piece = values[24 + at : 32 + at, :] * coarse_scale
                    if row < 256:
                        start = pl.multiple_of(half * 256 + row, 8)
                        coarse1_ref[pl.ds(start, 8), x * 128 : x * 128 + 128] = piece
                    else:
                        start = pl.multiple_of(half * 64 + x * 128 + row % 64, 8)
                        lane = (row - 256) // 64 * 128
                        coarse2_ref[pl.ds(start, 8), lane : lane + 128] = piece


class Late:
    def __init__(self, source, held, sem):
        self.held = held
        self.shape = held.shape
        self.copy = pltpu.make_async_copy(source, held, sem)
        self.copy.start()

    def __getitem__(self, index):
        if self.copy is not None:
            self.copy.wait()
            self.copy = None
        return self.held[index]

    def finish(self):
        if self.copy is not None:
            self.copy.wait()
            self.copy = None


def run(kernel, outs, operands, scratch=(), scalars=(), late=(), inner=(), ahead=(), limit=16, work=0.1):
    size = sum(math.prod(x.shape) * x.dtype.itemsize for x in [*operands, *ahead]) + sum(
        math.prod(shape) * jnp.dtype(kind).itemsize for shape, kind in outs
    )
    shapes = [
        (pltpu.VMEM if i in inner else jax.ShapeDtypeStruct)(shape, kind)
        for i, (shape, kind) in enumerate(outs)
    ] + [pltpu.VMEM(x.shape, x.dtype) for x in ahead]
    operands = [
        pltpu.with_memory_space_constraint(x, pltpu.HBM) if i in late else x
        for i, x in enumerate(operands)
    ] + [pltpu.with_memory_space_constraint(x, pltpu.HBM) for x in ahead]
    count = len(operands) - len(ahead)
    first_out = len(operands)
    first_ahead = first_out + len(outs)
    first_scratch = first_ahead + len(ahead)
    first_held = first_scratch + len(scratch)

    def space(i):
        return pltpu.SMEM if i in scalars else pltpu.HBM if i in late or i >= count else pltpu.VMEM

    def body(*refs):
        sems = refs[-1]
        inputs = list(refs[:count])
        for k, i in enumerate(late):
            inputs[i] = Late(refs[i], refs[first_held + k], sems.at[k])
        fetched = [
            Late(refs[count + k], refs[first_ahead + k], sems.at[len(late) + k])
            for k in range(len(ahead))
        ]
        kernel(*inputs, *refs[first_out:first_ahead], *refs[first_scratch:first_held])
        for copy in [inputs[i] for i in late] + fetched:
            copy.finish()

    copies = len(late) + len(ahead)
    return pl.pallas_call(
        body if copies else kernel,
        out_shape=shapes,
        in_specs=[pl.BlockSpec(memory_space=space(i)) for i in range(first_out)],
        out_specs=[pl.BlockSpec(memory_space=pltpu.VMEM)] * len(shapes),
        scratch_shapes=[pltpu.VMEM(shape, kind) for shape, kind in scratch]
        + [pltpu.VMEM(operands[i].shape, operands[i].dtype) for i in late]
        + ([pltpu.SemaphoreType.DMA((copies,))] if copies else []),
        compiler_params=pltpu.CompilerParams(vmem_limit_bytes=limit * 1024 * 1024),
        cost_estimate=pl.CostEstimate(
            flops=int(2e9 * work), bytes_accessed=size, transcendentals=0
        ),
    )(*operands)


ROW = ("z", "y", "core")
PLANE = ("z", "y")
CHIPS = ("z", "y", "x")


def send(value, axis, step):
    size = lax.axis_size(axis)
    return lax.ppermute(value, axis, [(i, (i + step) % size) for i in range(size)])


def shards(
    latent, cotangent, fine_w1, fine_w2, fine_gain, coarse_w1, coarse_w2, coarse_gain,
    fine_src, fine_dst, live_blocks, export_rows, pool_assign, coarse_src, coarse_dst,
):
    own = latent[0, 0]
    cot = cotangent[0, 0]
    nodes, feature = own.shape
    export = export_rows[0]
    assign = pool_assign[0]
    src, dst = fine_src[0], fine_dst[0]
    rim_count = export.shape[1]
    hidden = fine_w1.shape[1]
    edges, coarse_edges = src.shape[1], coarse_src.shape[1]
    rows, cols = lax.axis_size(ROW), lax.axis_size("x")
    fine_gain = fine_gain[None, :]
    coarse_gain = coarse_gain[None, :]
    between = [(i, i + 1) for i in range(1, rows - 1, 2)]
    between = between + [(target, source) for source, target in between]
    between = between + [(rows - 1, 0), (0, rows - 1)]
    row = lax.axis_index(ROW)
    inside = jnp.logical_and(row > 0, row < rows - 1)
    place = jnp.stack(
        [lax.axis_index("x"), lax.axis_index("core"), 128 * live_blocks[0, 0], inside]
    )
    own, place = lax.optimization_barrier((own, place.astype(jnp.int32)))
    wide = 2 * feature

    rim, pack, target, own_in, src_in, w1_in, w2_in, gain_in, assign_in, export_in = run(
        start_kernel,
        [
            ((rim_count, feature), BF),
            ((CNODE + 32, feature), BF),
            ((1, edges), jnp.int32),
        ],
        [own, export, cot, assign, dst, place],
        scalars=(5,),
        late=(0, 1, 2, 3, 4),
        inner=(0, 1, 2),
        ahead=[own, src, fine_w1, fine_w2, fine_gain, assign, export],
    )
    near, far = [(0, 1), (1, 0), (2, 3), (3, 2)], [(1, 2), (2, 1), (3, 0), (0, 3)]
    pack_got = lax.ppermute(pack, "x", near)
    from_west, from_east = send(rim, "x", 1), send(rim, "x", 3)
    from_a = send(rim, "core", 1)
    from_b = lax.ppermute(rim, ROW, between)
    part, left, csrc_in, cdst_in, cw1_in, cw2_in, cgain_in, cot_in = run(
        own_kernel,
        [((edges, hidden), F32), ((edges, feature), BF)],
        [own_in, src_in, target, w1_in],
        inner=(0, 1),
        ahead=[coarse_src, coarse_dst, coarse_w1, coarse_w2, coarse_gain, cot],
        limit=LIMITS[0],
        work=1.1,
    )
    pack, pack_got, part = lax.optimization_barrier((pack, pack_got, part))
    (pair,) = run(add_kernel, [((CNODE + 32, feature), BF)], [pack, pack_got], inner=(0,))
    pair, part = lax.optimization_barrier((pair, part))
    pair_got = lax.ppermute(pair, "x", far)
    slope, acc, summed, pooled, left = run(
        fine_forward_kernel,
        [
            ((edges, hidden), F32),
            ((nodes, hidden), BF),
            ((nodes, feature), F32),
            ((CNODE, feature), BF),
            ((edges, feature), BF),
        ],
        [
            part, left, own_in, from_a, from_b, from_west, from_east, src_in, target, place,
            w1_in, w2_in, gain_in, assign_in,
        ],
        [((nodes + 4 * rim_count, feature), BF), ((nodes, hidden), F32)],
        scalars=(9,),
        inner=(0, 1, 2, 3, 4),
        limit=LIMITS[1],
        work=1.6,
    )
    pooled, pair_got = lax.optimization_barrier((pooled, pair_got))
    half_rows = CNODE // 2
    got = [
        lax.ppermute(pooled[:half_rows], "x", near),
        lax.ppermute(pooled[half_rows:], "x", far),
    ]
    first, second = run(
        pair_kernel, [((half_rows, feature), BF)] * 2, [pooled, *got], inner=(0, 1)
    )
    got = [lax.ppermute(first, "x", far), lax.ppermute(second, "x", near)]

    grad_fine, coarse_pack = run(
        coarse_kernel,
        [((nodes, feature), F32), ((2, 384, 128), F32)],
        [
            first, got[0], second, got[1], pair, pair_got, csrc_in, cdst_in, cw1_in, cw2_in, cgain_in,
            cot_in, assign_in, place,
        ],
        [
            ((CNODE, feature), BF),
            ((coarse_edges, hidden), F32),
            ((coarse_edges, CNODE), BF),
            ((CNODE, coarse_edges), BF),
            ((CNODE, hidden), F32),
            ((CNODE, hidden), F32),
            ((CNODE, hidden), F32),
        ],
        scalars=(13,),
        inner=(0, 1),
        limit=LIMITS[2],
        work=5.0,
    )

    local, give, keep, ghost_b, ghost_w, ghost_e = run(
        fine_backward_kernel,
        [
            ((nodes, feature), F32),
            ((1920 + 2 * rim_count, 128), BF),
            ((1920, 128), F32),
            ((rim_count, feature), BF),
            ((2 * rim_count, 128), BF),
            ((2 * rim_count, 128), BF),
        ],
        [
            grad_fine, summed, slope, acc, left, own_in, src_in, target, place,
            w1_in, w2_in, gain_in, coarse_pack,
        ],
        [
            ((nodes + 4 * rim_count, feature), F32),
            ((nodes, hidden), F32),
            ((4 * rim_count, feature), BF),
            ((feature, hidden), F32),
        ],
        scalars=(8,),
        inner=(0, 1, 2, 3, 4, 5),
        limit=LIMITS[3],
        work=2.8,
    )
    from_core = send(give, "core", 1)
    from_b = lax.ppermute(ghost_b, ROW, between)
    keep, from_b = lax.optimization_barrier((keep, from_b))
    total, coarse_total, to_east, to_cross, to_west = run(
        split_kernel,
        [
            ((384, 128), F32),
            ((384, 128), F32),
            ((384 + 2 * rim_count, 128), BF),
            ((384, 128), BF),
            ((384 + 2 * rim_count, 128), BF),
        ],
        [keep, from_core, ghost_w, ghost_e, place],
        scalars=(4,),
        inner=(0, 1, 2, 3, 4),
    )
    from_west = send(to_east, "x", 1)
    from_cross = send(to_cross, "x", 2)
    from_east = send(to_west, "x", 3)
    total = (
        total
        + from_west[0:384].astype(F32)
        + from_cross.astype(F32)
        + from_east[0:384].astype(F32)
    )
    both = jnp.concatenate(
        [total.reshape(16, 24, 128), coarse_total.reshape(16, 24, 128)], axis=1
    ).astype(BF)
    both = lax.all_to_all(both, PLANE, 0, 0, tiled=True)
    both = jnp.sum(both.astype(F32), axis=0).astype(BF)
    copies = jnp.broadcast_to(both[None], (64,) + both.shape)
    mine = lax.all_to_all(copies, CHIPS, 0, 0, tiled=True)
    mine, local = lax.optimization_barrier((mine, local))
    other = send(mine, "core", 1)
    (grad_latent,) = run(
        return_kernel,
        [((nodes, feature), F32)],
        [local, from_core, from_b, from_west, from_east, export_in, place],
        scalars=(6,),
    )
    unpack = functools.partial(
        unpack_kernel,
        fine_scale=1.0 / math.sqrt(edges * rows * cols),
        coarse_scale=1.0 / math.sqrt(coarse_edges * rows),
    )
    weight_grads = run(
        unpack,
        [
            ((2 * feature, hidden), F32),
            ((hidden, feature), F32),
            ((2 * feature, hidden), F32),
            ((hidden, feature), F32),
        ],
        [mine, other, place],
        scalars=(2,),
    )
    return (grad_latent[None, None], *weight_grads)


def solution(mesh):
    shape = (4, 4, 2, 4)
    inner = Mesh(mesh.devices.reshape(shape), ("z", "y", "core", "x"))
    node_sharded = P(ROW, "x", None, None)
    index_sharded = P(ROW, "x", None)
    placed = (
        node_sharded,
        node_sharded,
        P(),
        P(),
        P(),
        P(),
        P(),
        P(),
        index_sharded,
        index_sharded,
        P(ROW, "x"),
        index_sharded,
        index_sharded,
        P(ROW, None),
        P(ROW, None),
    )
    return jax.shard_map(
        shards,
        mesh=inner,
        in_specs=placed,
        out_specs=(node_sharded, P(), P(), P(), P()),
        check_vma=False,
    )
```

```python
import functools
import math

import jax
import jax.numpy as jnp
from jax import lax
from jax.experimental import pallas as pl
from jax.experimental.pallas import tpu as pltpu
from jax.sharding import Mesh
from jax.sharding import PartitionSpec as P

EPS = 1e-05
CNODE = 512
CHUNK = 1024
LIMITS = (20, 20, 36, 22)
BF = jnp.bfloat16
F32 = jnp.float32


def dot(left, right):
    return lax.dot_general(left, right, (((1,), (0,)), ((), ())), preferred_element_type=F32)


def dot_rt(left, right):
    return lax.dot_general(left, right, (((1,), (1,)), ((), ())), preferred_element_type=F32)


def dot_lt(left, right):
    return lax.dot_general(left, right, (((0,), (0,)), ((), ())), preferred_element_type=F32)


def halves(value):
    high = value.astype(BF)
    return high, (value - high.astype(F32)).astype(BF)


def spread_row(row):
    count = row.shape[1]
    return jnp.concatenate(
        [
            jnp.broadcast_to(row[:, at : at + 128], (128, 128)).T
            for at in range(0, count, 128)
        ],
        axis=0,
    )


def pick_matrix(row, width):
    column = spread_row(row)
    wide = jnp.concatenate([column] * (width // 128), axis=1)
    hit = wide == lax.broadcasted_iota(jnp.int32, wide.shape, 1)
    return jnp.where(hit, 1.0, 0.0).astype(BF)


def sum_matrix(row, width):
    shape = (width, row.shape[1])
    hit = lax.broadcasted_iota(jnp.int32, shape, 0) == row
    return jnp.where(hit, 1.0, 0.0).astype(BF)


def norm_of(summed):
    inverse = lax.rsqrt(jnp.mean(summed * summed, axis=-1, keepdims=True) + EPS)
    return inverse, summed * inverse


def summed_grad(grad_new, gain, summed):
    inverse, normed = norm_of(summed)
    grad_normed = grad_new * gain
    mean = jnp.mean(grad_normed * normed, axis=-1, keepdims=True)
    return (inverse * (grad_normed - normed * mean)).astype(BF)


def activations(preact):
    sig = jax.nn.sigmoid(preact)
    return (preact * sig).astype(BF), sig * (1.0 + preact * (1.0 - sig))


def split_count(count):
    many = jnp.floor(count * (1.0 / 256.0)) * 256.0
    upper = lax.broadcasted_iota(jnp.int32, count.shape, 0) < 8
    return jnp.where(upper, many, count - many).astype(BF)


def whole_count(rows):
    rows = rows.astype(F32)
    parts = [rows[at : at + 1, :] + rows[at + 8 : at + 9, :] for at in (0, 16)]
    return jnp.concatenate(parts, axis=1)


def start_kernel(
    own_ref, export_ref, cot_ref, assign_ref, dst_ref, place_ref, rim_ref, pack_ref, target_ref
):
    rim_ref[...] = dot(pick_matrix(export_ref[...], own_ref.shape[0]), own_ref[...]).astype(BF)
    pool = sum_matrix(assign_ref[...], CNODE)
    pack_ref[0:CNODE, :] = dot(pool, cot_ref[...]).astype(BF)
    packed = split_count(dot_rt(jnp.ones((16, pool.shape[1]), BF), pool))
    pack_ref[CNODE : CNODE + 16, :] = packed[:, :256]
    pack_ref[CNODE + 16 : CNODE + 32, :] = packed[:, 256:]
    slot = lax.broadcasted_iota(jnp.int32, dst_ref.shape, 1)
    target_ref[...] = jnp.where(slot < place_ref[2], dst_ref[...], -1)


def add_kernel(mine_ref, got_ref, out_ref):
    out_ref[0:CNODE, :] = (
        mine_ref[0:CNODE, :].astype(F32) + got_ref[0:CNODE, :].astype(F32)
    ).astype(BF)
    count = whole_count(mine_ref[CNODE:, :]) + whole_count(got_ref[CNODE:, :])
    packed = split_count(jnp.broadcast_to(count, (16, CNODE)))
    out_ref[CNODE : CNODE + 16, :] = packed[:, :256]
    out_ref[CNODE + 16 : CNODE + 32, :] = packed[:, 256:]


def pair_kernel(mine_ref, near_ref, far_ref, first_ref, second_ref):
    half = near_ref.shape[0]
    mine = mine_ref[...].astype(F32)
    first_ref[...] = (mine[0:half] + near_ref[...].astype(F32)).astype(BF)
    second_ref[...] = (mine[half:] + far_ref[...].astype(F32)).astype(BF)


def own_kernel(own_ref, src_ref, target_ref, w1_ref, part_ref, left_ref):
    nodes, feature = own_ref.shape
    for at in range(0, src_ref.shape[1], CHUNK):
        here = slice(at, at + CHUNK)
        left = dot(pick_matrix(src_ref[:, here], nodes), own_ref[...]).astype(BF)
        left_ref[here, :] = left
        right = dot(pick_matrix(target_ref[:, here], nodes), own_ref[...]).astype(BF)
        part_ref[here, :] = dot(left, w1_ref[0:feature, :]) + dot(right, w1_ref[feature:, :])


def fine_forward_kernel(
    part_ref, left_ref, own_ref, ra, rb, rw, re, src_ref, target_ref, place_ref,
    w1_ref, w2_ref, gain_ref, assign_ref, slope_ref, acc_out, summed_ref, pooled_ref, pair_ref, table, acc,
):
    nodes, feature = own_ref.shape
    rim = ra.shape[0]
    col, core = place_ref[0], place_ref[1]
    table[0:nodes, :] = own_ref[...]
    table[pl.ds(pl.multiple_of(nodes + rim * (1 - core), rim), rim), :] = ra[...]
    beyond = rb[...].astype(F32) * jnp.where(place_ref[3] > 0, 1.0, 0.0)
    table[pl.ds(pl.multiple_of(nodes + rim * core, rim), rim), :] = beyond.astype(BF)
    west = rw[...].astype(F32) * jnp.where(col > 0, 1.0, 0.0)
    east = re[...].astype(F32) * jnp.where(col < 3, 1.0, 0.0)
    table[nodes + 2 * rim : nodes + 3 * rim, :] = west.astype(BF)
    table[nodes + 3 * rim :, :] = east.astype(BF)
    for at in range(0, src_ref.shape[1], CHUNK):
        here = slice(at, at + CHUNK)
        picks = pick_matrix(src_ref[:, here] - nodes, 4 * rim)
        left = dot(picks, table[nodes:, :]).astype(BF)
        pair_ref[here, :] = left + left_ref[here, :]
        preact = part_ref[here, :] + dot(left, w1_ref[0:feature, :])
        hidden, slope = activations(preact)
        slope_ref[here, :] = slope
        part = dot(sum_matrix(target_ref[:, here], nodes), hidden)
        if at == 0:
            acc[...] = part
        else:
            acc[...] += part
    high, low = halves(acc[...])
    acc_out[...] = high
    summed = dot(high, w2_ref[...]) + dot(low, w2_ref[...])
    summed_ref[...] = summed
    _, normed = norm_of(summed)
    fine_new = own_ref[...].astype(F32) + normed * gain_ref[...]
    pool = sum_matrix(assign_ref[...], CNODE)
    pooled_ref[...] = dot(pool, fine_new.astype(BF)).astype(BF)


def coarse_kernel(
    p0, p1, q0, q1, g0, g1, src_ref, dst_ref, w1_ref, w2_ref, gain_ref, cot_ref,
    assign_ref, place_ref, grad_fine_ref, pack_ref,
    table, slope, pick_t, sum_t, acc, by_src, by_dst,
):
    feature = p0.shape[1]
    edges = src_ref.shape[1]
    grad_c1 = g0[0:CNODE, :].astype(F32) + g1[0:CNODE, :].astype(F32)
    count = whole_count(g0[CNODE:, :]) + whole_count(g1[CNODE:, :])
    weight = spread_row(1.0 / jnp.maximum(count, 1.0))
    weight = jnp.concatenate([weight] * (feature // 128), axis=1)
    pooled = jnp.concatenate(
        [
            p0[...].astype(F32) + p1[...].astype(F32),
            q0[...].astype(F32) + q1[...].astype(F32),
        ],
        axis=0,
    )
    table[...] = (pooled * weight).astype(BF)
    for at in range(0, edges, CHUNK):
        here = slice(at, at + CHUNK)
        left = dot(pick_matrix(src_ref[:, here], CNODE), table[...]).astype(BF)
        pick = pick_matrix(dst_ref[:, here], CNODE)
        pick_t[here, :] = pick
        right = dot(pick, table[...]).astype(BF)
        preact = dot(left, w1_ref[0:feature, :]) + dot(right, w1_ref[feature:, :])
        hidden, slope[here, :] = activations(preact)
        adds = sum_matrix(dst_ref[:, here], CNODE)
        sum_t[:, here] = adds
        part = dot(adds, hidden)
        if at == 0:
            acc[...] = part
        else:
            acc[...] += part
    high, low = halves(acc[...])
    summed = dot(high, w2_ref[...]) + dot(low, w2_ref[...])
    grad_summed = summed_grad(grad_c1, gain_ref[...], summed)
    for at in range(0, edges, CHUNK):
        here = slice(at, at + CHUNK)
        grad_message = dot(pick_t[here, :], grad_summed).astype(BF)
        grad_preact = (dot_rt(grad_message, w2_ref[...]) * slope[here, :]).astype(BF)
        part_src = dot(sum_matrix(src_ref[:, here], CNODE), grad_preact)
        part_dst = dot(sum_t[:, here], grad_preact)
        if at == 0:
            by_src[...] = part_src
            by_dst[...] = part_dst
        else:
            by_src[...] += part_src
            by_dst[...] += part_dst
    grad_c0 = (
        grad_c1
        + dot_rt(by_src[...].astype(BF), w1_ref[0:feature, :])
        + dot_rt(by_dst[...].astype(BF), w1_ref[feature:, :])
    )
    spread = dot(pick_matrix(assign_ref[...], CNODE), (grad_c0 * weight).astype(BF))
    grad_fine_ref[...] = cot_ref[...].astype(F32) + spread
    own = pl.ds(pl.multiple_of(place_ref[0] * 128, 128), 128)
    for half, rows in enumerate((by_src, by_dst)):
        pack_ref[half, 0:256, :] = dot_lt(table[...], rows[:, own].astype(BF))
    second = dot_lt(acc[:, own].astype(BF), grad_summed)
    for half in range(2):
        for k in range(2):
            pack_ref[half, 256 + 64 * k : 320 + 64 * k, :] = second[
                64 * half : 64 * half + 64, 128 * k : 128 * k + 128
            ]


def fine_backward_kernel(
    grad_fine_ref, summed_ref, slope_ref, acc_ref, left_ref, own_ref, src_ref, target_ref,
    place_ref, w1_ref, w2_ref, gain_ref, coarse_ref,
    local_ref, give_ref, keep_ref, ghost_b, ghost_w, ghost_e, by_src, by_dst, ghost, grad_left,
):
    nodes, feature = grad_fine_ref.shape
    rim = ghost_b.shape[0]
    core = place_ref[1]
    grad_fine = grad_fine_ref[...]
    grad_summed = summed_grad(grad_fine, gain_ref[...], summed_ref[...])
    for at in range(0, src_ref.shape[1], CHUNK):
        here = slice(at, at + CHUNK)
        target = target_ref[:, here]
        grad_message = dot(pick_matrix(target, nodes), grad_summed).astype(BF)
        grad_preact = (dot_rt(grad_message, w2_ref[...]) * slope_ref[here, :]).astype(BF)
        back = dot_rt(grad_preact, w1_ref[0:feature, :]).astype(BF)
        part_src = dot(sum_matrix(src_ref[:, here], by_src.shape[0]), back)
        part_left = dot_lt(left_ref[here, :], grad_preact)
        part_dst = dot(sum_matrix(target, nodes), grad_preact)
        if at == 0:
            by_src[...] = part_src
            grad_left[...] = part_left
            by_dst[...] = part_dst
        else:
            by_src[...] += part_src
            grad_left[...] += part_left
            by_dst[...] += part_dst
    local_ref[...] = (
        grad_fine
        + by_src[0:nodes, :]
        + dot_rt(by_dst[...].astype(BF), w1_ref[feature:, :])
    )
    ghost[...] = by_src[nodes:, :].astype(BF)
    to_core = ghost[pl.ds(pl.multiple_of(rim * (1 - core), rim), rim), :]
    give_ref[1920 : 1920 + rim, :] = to_core[:, 0:128]
    give_ref[1920 + rim :, :] = to_core[:, 128:256]
    ghost_b[...] = ghost[pl.ds(pl.multiple_of(rim * core, rim), rim), :]
    for out, at in ((ghost_w, 2 * rim), (ghost_e, 3 * rim)):
        out[0:rim, :] = ghost[at : at + rim, 0:128]
        out[rim:, :] = ghost[at : at + rim, 128:256]
    for out, half in ((give_ref, 1 - core), (keep_ref, core)):
        part = pl.ds(pl.multiple_of(half * 256, 256), 256)
        first = grad_left[:, part].astype(out.dtype)
        second = dot_lt(own_ref[...], by_dst[:, part].astype(BF)).astype(out.dtype)
        third = dot_lt(acc_ref[:, part], grad_summed).astype(out.dtype)
        for k in range(2):
            lanes = slice(128 * k, 128 * k + 128)
            out[512 * k : 512 * k + 256, :] = first[:, lanes]
            out[512 * k + 256 : 512 * k + 512, :] = second[:, lanes]
            out[1024 + 256 * k : 1280 + 256 * k, :] = third[:, lanes]
        out[1536:1920, :] = coarse_ref[half].astype(out.dtype)


def split_kernel(keep_ref, got_ref, ghost_w, ghost_e, place_ref, total_ref, coarse_ref, *sends):
    col = place_ref[0]

    def block(step):
        rows = pl.ds(pl.multiple_of(lax.rem(col + step, 4) * 384, 384), 384)
        return keep_ref[rows, :] + got_ref[rows, :].astype(F32)

    total_ref[...] = block(0)
    coarse_ref[...] = keep_ref[1536:1920, :] + got_ref[1536:1920, :].astype(F32)
    for step, out in enumerate(sends, 1):
        out[0:384, :] = block(step).astype(BF)
    sends[0][384:, :] = ghost_e[...]
    sends[2][384:, :] = ghost_w[...]


def return_kernel(local_ref, from_core, from_b, from_west, from_east, export_ref, place_ref, out_ref):
    rim = export_ref.shape[1]
    adds = sum_matrix(export_ref[...], local_ref.shape[0])
    col = place_ref[0]

    def wide(ref):
        at = ref.shape[0] - 2 * rim
        rows = ref[at:, :].astype(F32)
        return jnp.concatenate([rows[0:rim, :], rows[rim:, :]], axis=1)

    west = wide(from_west) * jnp.where(col > 0, 1.0, 0.0)
    east = wide(from_east) * jnp.where(col < 3, 1.0, 0.0)
    beyond = from_b[...].astype(F32) * jnp.where(place_ref[3] > 0, 1.0, 0.0)
    arrived = (wide(from_core) + beyond) + (west + east)
    high, low = halves(arrived)
    out_ref[...] = local_ref[...] + dot(adds, high) + dot(adds, low)


def unpack_kernel(
    mine_ref, other_ref, place_ref, fine1_ref, fine2_ref, coarse1_ref, coarse2_ref,
    *, fine_scale, coarse_scale,
):
    for ref, half in ((mine_ref, place_ref[1]), (other_ref, 1 - place_ref[1])):
        for plane in range(16):
            for x in range(4):
                values = ref[plane * 4 + x].astype(F32)
                for at in range(0, 24, 8):
                    row = x * 384 + plane * 24 + at
                    piece = values[at : at + 8, :] * fine_scale
                    if row < 1024:
                        lanes = pl.ds(pl.multiple_of(half * 256 + row // 512 * 128, 128), 128)
                        fine1_ref[row % 512 : row % 512 + 8, lanes] = piece
                    else:
                        start = pl.multiple_of(half * 256 + row % 256, 8)
                        lane = (row - 1024) // 256 * 128
                        fine2_ref[pl.ds(start, 8), lane : lane + 128] = piece
                    row = plane * 24 + at
                    piece = values[24 + at : 32 + at, :] * coarse_scale
                    if row < 256:
                        start = pl.multiple_of(half * 256 + row, 8)
                        coarse1_ref[pl.ds(start, 8), x * 128 : x * 128 + 128] = piece
                    else:
                        start = pl.multiple_of(half * 64 + x * 128 + row % 64, 8)
                        lane = (row - 256) // 64 * 128
                        coarse2_ref[pl.ds(start, 8), lane : lane + 128] = piece


class Late:
    def __init__(self, source, held, sem):
        self.held = held
        self.shape = held.shape
        self.copy = pltpu.make_async_copy(source, held, sem)
        self.copy.start()

    def __getitem__(self, index):
        if self.copy is not None:
            self.copy.wait()
            self.copy = None
        return self.held[index]

    def finish(self):
        if self.copy is not None:
            self.copy.wait()
            self.copy = None


def run(kernel, outs, operands, scratch=(), scalars=(), late=(), inner=(), ahead=(), limit=16, work=0.1):
    size = sum(math.prod(x.shape) * x.dtype.itemsize for x in [*operands, *ahead]) + sum(
        math.prod(shape) * jnp.dtype(kind).itemsize for shape, kind in outs
    )
    shapes = [
        (pltpu.VMEM if i in inner else jax.ShapeDtypeStruct)(shape, kind)
        for i, (shape, kind) in enumerate(outs)
    ] + [pltpu.VMEM(x.shape, x.dtype) for x in ahead]
    operands = [
        pltpu.with_memory_space_constraint(x, pltpu.HBM) if i in late else x
        for i, x in enumerate(operands)
    ] + [pltpu.with_memory_space_constraint(x, pltpu.HBM) for x in ahead]
    count = len(operands) - len(ahead)
    first_out = len(operands)
    first_ahead = first_out + len(outs)
    first_scratch = first_ahead + len(ahead)
    first_held = first_scratch + len(scratch)

    def space(i):
        return pltpu.SMEM if i in scalars else pltpu.HBM if i in late or i >= count else pltpu.VMEM

    def body(*refs):
        sems = refs[-1]
        inputs = list(refs[:count])
        for k, i in enumerate(late):
            inputs[i] = Late(refs[i], refs[first_held + k], sems.at[k])
        fetched = [
            Late(refs[count + k], refs[first_ahead + k], sems.at[len(late) + k])
            for k in range(len(ahead))
        ]
        kernel(*inputs, *refs[first_out:first_ahead], *refs[first_scratch:first_held])
        for copy in [inputs[i] for i in late] + fetched:
            copy.finish()

    copies = len(late) + len(ahead)
    return pl.pallas_call(
        body if copies else kernel,
        out_shape=shapes,
        in_specs=[pl.BlockSpec(memory_space=space(i)) for i in range(first_out)],
        out_specs=[pl.BlockSpec(memory_space=pltpu.VMEM)] * len(shapes),
        scratch_shapes=[pltpu.VMEM(shape, kind) for shape, kind in scratch]
        + [pltpu.VMEM(operands[i].shape, operands[i].dtype) for i in late]
        + ([pltpu.SemaphoreType.DMA((copies,))] if copies else []),
        compiler_params=pltpu.CompilerParams(vmem_limit_bytes=limit * 1024 * 1024),
        cost_estimate=pl.CostEstimate(
            flops=int(2e9 * work), bytes_accessed=size, transcendentals=0
        ),
    )(*operands)


ROW = ("z", "y", "core")
PLANE = ("z", "y")
CHIPS = ("z", "y", "x")


def send(value, axis, step):
    size = lax.axis_size(axis)
    return lax.ppermute(value, axis, [(i, (i + step) % size) for i in range(size)])


def shards(
    latent, cotangent, fine_w1, fine_w2, fine_gain, coarse_w1, coarse_w2, coarse_gain,
    fine_src, fine_dst, live_blocks, export_rows, pool_assign, coarse_src, coarse_dst,
):
    own = latent[0, 0]
    cot = cotangent[0, 0]
    nodes, feature = own.shape
    export = export_rows[0]
    assign = pool_assign[0]
    src, dst = fine_src[0], fine_dst[0]
    rim_count = export.shape[1]
    hidden = fine_w1.shape[1]
    edges, coarse_edges = src.shape[1], coarse_src.shape[1]
    rows, cols = lax.axis_size(ROW), lax.axis_size("x")
    fine_gain = fine_gain[None, :]
    coarse_gain = coarse_gain[None, :]
    between = [(i, i + 1) for i in range(1, rows - 1, 2)]
    between = between + [(target, source) for source, target in between]
    between = between + [(rows - 1, 0), (0, rows - 1)]
    row = lax.axis_index(ROW)
    inside = jnp.logical_and(row > 0, row < rows - 1)
    place = jnp.stack(
        [lax.axis_index("x"), lax.axis_index("core"), 128 * live_blocks[0, 0], inside]
    )
    own, place = lax.optimization_barrier((own, place.astype(jnp.int32)))
    wide = 2 * feature

    rim, pack, target, own_in, src_in, w1_in = run(
        start_kernel,
        [
            ((rim_count, feature), BF),
            ((CNODE + 32, feature), BF),
            ((1, edges), jnp.int32),
        ],
        [own, export, cot, assign, dst, place],
        scalars=(5,),
        late=(0, 1, 2, 3, 4),
        inner=(0, 1, 2),
        ahead=[own, src, fine_w1],
    )
    near, far = [(0, 1), (1, 0), (2, 3), (3, 2)], [(1, 2), (2, 1), (3, 0), (0, 3)]
    pack_got = lax.ppermute(pack, "x", near)
    from_west, from_east = send(rim, "x", 1), send(rim, "x", 3)
    from_a = send(rim, "core", 1)
    from_b = lax.ppermute(rim, ROW, between)
    (
        part, left, csrc_in, cdst_in, cw1_in, cw2_in, cgain_in, cot_in,
        w2_in, gain_in, assign_in, export_in,
    ) = run(
        own_kernel,
        [((edges, hidden), F32), ((edges, feature), BF)],
        [own_in, src_in, target, w1_in],
        inner=(0, 1),
        ahead=[
            coarse_src, coarse_dst, coarse_w1, coarse_w2, coarse_gain, cot,
            fine_w2, fine_gain, assign, export,
        ],
        limit=LIMITS[0],
        work=1.1,
    )
    pack, pack_got, part = lax.optimization_barrier((pack, pack_got, part))
    (pair,) = run(add_kernel, [((CNODE + 32, feature), BF)], [pack, pack_got], inner=(0,))
    pair, part = lax.optimization_barrier((pair, part))
    pair_got = lax.ppermute(pair, "x", far)
    slope, acc, summed, pooled, left = run(
        fine_forward_kernel,
        [
            ((edges, hidden), F32),
            ((nodes, hidden), BF),
            ((nodes, feature), F32),
            ((CNODE, feature), BF),
            ((edges, feature), BF),
        ],
        [
            part, left, own_in, from_a, from_b, from_west, from_east, src_in, target, place,
            w1_in, w2_in, gain_in, assign_in,
        ],
        [((nodes + 4 * rim_count, feature), BF), ((nodes, hidden), F32)],
        scalars=(9,),
        inner=(0, 1, 2, 3, 4),
        limit=LIMITS[1],
        work=1.6,
    )
    pooled, pair_got = lax.optimization_barrier((pooled, pair_got))
    half_rows = CNODE // 2
    got = [
        lax.ppermute(pooled[:half_rows], "x", near),
        lax.ppermute(pooled[half_rows:], "x", far),
    ]
    first, second = run(
        pair_kernel, [((half_rows, feature), BF)] * 2, [pooled, *got], inner=(0, 1)
    )
    got = [lax.ppermute(first, "x", far), lax.ppermute(second, "x", near)]

    grad_fine, coarse_pack = run(
        coarse_kernel,
        [((nodes, feature), F32), ((2, 384, 128), F32)],
        [
            first, got[0], second, got[1], pair, pair_got, csrc_in, cdst_in, cw1_in, cw2_in, cgain_in,
            cot_in, assign_in, place,
        ],
        [
            ((CNODE, feature), BF),
            ((coarse_edges, hidden), F32),
            ((coarse_edges, CNODE), BF),
            ((CNODE, coarse_edges), BF),
            ((CNODE, hidden), F32),
            ((CNODE, hidden), F32),
            ((CNODE, hidden), F32),
        ],
        scalars=(13,),
        inner=(0, 1),
        limit=LIMITS[2],
        work=5.0,
    )

    local, give, keep, ghost_b, ghost_w, ghost_e = run(
        fine_backward_kernel,
        [
            ((nodes, feature), F32),
            ((1920 + 2 * rim_count, 128), BF),
            ((1920, 128), F32),
            ((rim_count, feature), BF),
            ((2 * rim_count, 128), BF),
            ((2 * rim_count, 128), BF),
        ],
        [
            grad_fine, summed, slope, acc, left, own_in, src_in, target, place,
            w1_in, w2_in, gain_in, coarse_pack,
        ],
        [
            ((nodes + 4 * rim_count, feature), F32),
            ((nodes, hidden), F32),
            ((4 * rim_count, feature), BF),
            ((feature, hidden), F32),
        ],
        scalars=(8,),
        inner=(0, 1, 2, 3, 4, 5),
        limit=LIMITS[3],
        work=2.8,
    )
    from_core = send(give, "core", 1)
    from_b = lax.ppermute(ghost_b, ROW, between)
    total, coarse_total, to_east, to_cross, to_west = run(
        split_kernel,
        [
            ((384, 128), F32),
            ((384, 128), F32),
            ((384 + 2 * rim_count, 128), BF),
            ((384, 128), BF),
            ((384 + 2 * rim_count, 128), BF),
        ],
        [keep, from_core, ghost_w, ghost_e, place],
        scalars=(4,),
        inner=(0, 1, 2, 3, 4),
    )
    from_west = send(to_east, "x", 1)
    from_cross = send(to_cross, "x", 2)
    from_east = send(to_west, "x", 3)
    total = (
        total
        + from_west[0:384].astype(F32)
        + from_cross.astype(F32)
        + from_east[0:384].astype(F32)
    )
    both = jnp.concatenate(
        [total.reshape(16, 24, 128), coarse_total.reshape(16, 24, 128)], axis=1
    ).astype(BF)
    both, from_b = lax.optimization_barrier((both, from_b))
    both = lax.all_to_all(both, PLANE, 0, 0, tiled=True)
    both = jnp.sum(both.astype(F32), axis=0).astype(BF)
    copies = jnp.broadcast_to(both[None], (64,) + both.shape)
    mine = lax.all_to_all(copies, CHIPS, 0, 0, tiled=True)
    mine, local = lax.optimization_barrier((mine, local))
    other = send(mine, "core", 1)
    (grad_latent,) = run(
        return_kernel,
        [((nodes, feature), F32)],
        [local, from_core, from_b, from_west, from_east, export_in, place],
        scalars=(6,),
    )
    unpack = functools.partial(
        unpack_kernel,
        fine_scale=1.0 / math.sqrt(edges * rows * cols),
        coarse_scale=1.0 / math.sqrt(coarse_edges * rows),
    )
    weight_grads = run(
        unpack,
        [
            ((2 * feature, hidden), F32),
            ((hidden, feature), F32),
            ((2 * feature, hidden), F32),
            ((hidden, feature), F32),
        ],
        [mine, other, place],
        scalars=(2,),
    )
    return (grad_latent[None, None], *weight_grads)


def solution(mesh):
    shape = (4, 4, 2, 4)
    inner = Mesh(mesh.devices.reshape(shape), ("z", "y", "core", "x"))
    node_sharded = P(ROW, "x", None, None)
    index_sharded = P(ROW, "x", None)
    placed = (
        node_sharded,
        node_sharded,
        P(),
        P(),
        P(),
        P(),
        P(),
        P(),
        index_sharded,
        index_sharded,
        P(ROW, "x"),
        index_sharded,
        index_sharded,
        P(ROW, None),
        P(ROW, None),
    )
    return jax.shard_map(
        shards,
        mesh=inner,
        in_specs=placed,
        out_specs=(node_sharded, P(), P(), P(), P()),
        check_vma=False,
    )
```

```python
import functools
import math

import jax
import jax.numpy as jnp
from jax import lax
from jax.experimental import pallas as pl
from jax.experimental.pallas import tpu as pltpu
from jax.sharding import Mesh
from jax.sharding import PartitionSpec as P

EPS = 1e-05
CNODE = 512
CHUNK = 1024
LIMITS = (20, 20, 36, 22)
BF = jnp.bfloat16
F32 = jnp.float32


def dot(left, right):
    return lax.dot_general(left, right, (((1,), (0,)), ((), ())), preferred_element_type=F32)


def dot_rt(left, right):
    return lax.dot_general(left, right, (((1,), (1,)), ((), ())), preferred_element_type=F32)


def dot_lt(left, right):
    return lax.dot_general(left, right, (((0,), (0,)), ((), ())), preferred_element_type=F32)


def halves(value):
    high = value.astype(BF)
    return high, (value - high.astype(F32)).astype(BF)


def spread_row(row):
    count = row.shape[1]
    return jnp.concatenate(
        [
            jnp.broadcast_to(row[:, at : at + 128], (128, 128)).T
            for at in range(0, count, 128)
        ],
        axis=0,
    )


def pick_matrix(row, width):
    column = spread_row(row)
    wide = jnp.concatenate([column] * (width // 128), axis=1)
    hit = wide == lax.broadcasted_iota(jnp.int32, wide.shape, 1)
    return jnp.where(hit, 1.0, 0.0).astype(BF)


def sum_matrix(row, width):
    shape = (width, row.shape[1])
    hit = lax.broadcasted_iota(jnp.int32, shape, 0) == row
    return jnp.where(hit, 1.0, 0.0).astype(BF)


def norm_of(summed):
    inverse = lax.rsqrt(jnp.mean(summed * summed, axis=-1, keepdims=True) + EPS)
    return inverse, summed * inverse


def summed_grad(grad_new, gain, summed):
    inverse, normed = norm_of(summed)
    grad_normed = grad_new * gain
    mean = jnp.mean(grad_normed * normed, axis=-1, keepdims=True)
    return (inverse * (grad_normed - normed * mean)).astype(BF)


def activations(preact):
    sig = jax.nn.sigmoid(preact)
    return (preact * sig).astype(BF), sig * (1.0 + preact * (1.0 - sig))


def split_count(count):
    many = jnp.floor(count * (1.0 / 256.0)) * 256.0
    upper = lax.broadcasted_iota(jnp.int32, count.shape, 0) < 8
    return jnp.where(upper, many, count - many).astype(BF)


def whole_count(rows):
    rows = rows.astype(F32)
    parts = [rows[at : at + 1, :] + rows[at + 8 : at + 9, :] for at in (0, 16)]
    return jnp.concatenate(parts, axis=1)


def start_kernel(
    own_ref, export_ref, cot_ref, assign_ref, dst_ref, place_ref, rim_ref, pack_ref, target_ref
):
    rim_ref[...] = dot(pick_matrix(export_ref[...], own_ref.shape[0]), own_ref[...]).astype(BF)
    pool = sum_matrix(assign_ref[...], CNODE)
    pack_ref[0:CNODE, :] = dot(pool, cot_ref[...]).astype(BF)
    packed = split_count(dot_rt(jnp.ones((16, pool.shape[1]), BF), pool))
    pack_ref[CNODE : CNODE + 16, :] = packed[:, :256]
    pack_ref[CNODE + 16 : CNODE + 32, :] = packed[:, 256:]
    slot = lax.broadcasted_iota(jnp.int32, dst_ref.shape, 1)
    target_ref[...] = jnp.where(slot < place_ref[2], dst_ref[...], -1)


def add_kernel(mine_ref, got_ref, out_ref):
    out_ref[0:CNODE, :] = (
        mine_ref[0:CNODE, :].astype(F32) + got_ref[0:CNODE, :].astype(F32)
    ).astype(BF)
    count = whole_count(mine_ref[CNODE:, :]) + whole_count(got_ref[CNODE:, :])
    packed = split_count(jnp.broadcast_to(count, (16, CNODE)))
    out_ref[CNODE : CNODE + 16, :] = packed[:, :256]
    out_ref[CNODE + 16 : CNODE + 32, :] = packed[:, 256:]


def pair_kernel(upper_ref, near_ref, lower_ref, far_ref, first_ref, second_ref):
    first_ref[...] = (upper_ref[...].astype(F32) + near_ref[...].astype(F32)).astype(BF)
    second_ref[...] = (lower_ref[...].astype(F32) + far_ref[...].astype(F32)).astype(BF)


def own_kernel(own_ref, src_ref, target_ref, w1_ref, part_ref, left_ref):
    nodes, feature = own_ref.shape
    for at in range(0, src_ref.shape[1], CHUNK):
        here = slice(at, at + CHUNK)
        left = dot(pick_matrix(src_ref[:, here], nodes), own_ref[...]).astype(BF)
        left_ref[here, :] = left
        right = dot(pick_matrix(target_ref[:, here], nodes), own_ref[...]).astype(BF)
        part_ref[here, :] = dot(left, w1_ref[0:feature, :]) + dot(right, w1_ref[feature:, :])


def fine_forward_kernel(
    part_ref, left_ref, own_ref, ra, rb, rw, re, src_ref, target_ref, place_ref,
    w1_ref, w2_ref, gain_ref, assign_ref, slope_ref, acc_out, summed_ref, upper_ref, lower_ref, pair_ref, table, acc,
):
    nodes, feature = own_ref.shape
    rim = ra.shape[0]
    col, core = place_ref[0], place_ref[1]
    table[0:nodes, :] = own_ref[...]
    table[pl.ds(pl.multiple_of(nodes + rim * (1 - core), rim), rim), :] = ra[...]
    beyond = rb[...].astype(F32) * jnp.where(place_ref[3] > 0, 1.0, 0.0)
    table[pl.ds(pl.multiple_of(nodes + rim * core, rim), rim), :] = beyond.astype(BF)
    west = rw[...].astype(F32) * jnp.where(col > 0, 1.0, 0.0)
    east = re[...].astype(F32) * jnp.where(col < 3, 1.0, 0.0)
    table[nodes + 2 * rim : nodes + 3 * rim, :] = west.astype(BF)
    table[nodes + 3 * rim :, :] = east.astype(BF)
    for at in range(0, src_ref.shape[1], CHUNK):
        here = slice(at, at + CHUNK)
        picks = pick_matrix(src_ref[:, here] - nodes, 4 * rim)
        left = dot(picks, table[nodes:, :]).astype(BF)
        pair_ref[here, :] = left + left_ref[here, :]
        preact = part_ref[here, :] + dot(left, w1_ref[0:feature, :])
        hidden, slope = activations(preact)
        slope_ref[here, :] = slope
        part = dot(sum_matrix(target_ref[:, here], nodes), hidden)
        if at == 0:
            acc[...] = part
        else:
            acc[...] += part
    high, low = halves(acc[...])
    acc_out[...] = high
    summed = dot(high, w2_ref[...]) + dot(low, w2_ref[...])
    summed_ref[...] = summed
    _, normed = norm_of(summed)
    fine_new = own_ref[...].astype(F32) + normed * gain_ref[...]
    pool = sum_matrix(assign_ref[...], CNODE)
    pooled = dot(pool, fine_new.astype(BF)).astype(BF)
    upper_ref[...] = pooled[0 : CNODE // 2, :]
    lower_ref[...] = pooled[CNODE // 2 :, :]


def coarse_kernel(
    p0, p1, q0, q1, g0, g1, src_ref, dst_ref, w1_ref, w2_ref, gain_ref, cot_ref,
    assign_ref, place_ref, grad_fine_ref, pack_ref,
    table, slope, pick_t, sum_t, acc, by_src, by_dst,
):
    feature = p0.shape[1]
    edges = src_ref.shape[1]
    grad_c1 = g0[0:CNODE, :].astype(F32) + g1[0:CNODE, :].astype(F32)
    count = whole_count(g0[CNODE:, :]) + whole_count(g1[CNODE:, :])
    weight = spread_row(1.0 / jnp.maximum(count, 1.0))
    weight = jnp.concatenate([weight] * (feature // 128), axis=1)
    pooled = jnp.concatenate(
        [
            p0[...].astype(F32) + p1[...].astype(F32),
            q0[...].astype(F32) + q1[...].astype(F32),
        ],
        axis=0,
    )
    table[...] = (pooled * weight).astype(BF)
    for at in range(0, edges, CHUNK):
        here = slice(at, at + CHUNK)
        left = dot(pick_matrix(src_ref[:, here], CNODE), table[...]).astype(BF)
        pick = pick_matrix(dst_ref[:, here], CNODE)
        pick_t[here, :] = pick
        right = dot(pick, table[...]).astype(BF)
        preact = dot(left, w1_ref[0:feature, :]) + dot(right, w1_ref[feature:, :])
        hidden, slope[here, :] = activations(preact)
        adds = sum_matrix(dst_ref[:, here], CNODE)
        sum_t[:, here] = adds
        part = dot(adds, hidden)
        if at == 0:
            acc[...] = part
        else:
            acc[...] += part
    high, low = halves(acc[...])
    summed = dot(high, w2_ref[...]) + dot(low, w2_ref[...])
    grad_summed = summed_grad(grad_c1, gain_ref[...], summed)
    for at in range(0, edges, CHUNK):
        here = slice(at, at + CHUNK)
        grad_message = dot(pick_t[here, :], grad_summed).astype(BF)
        grad_preact = (dot_rt(grad_message, w2_ref[...]) * slope[here, :]).astype(BF)
        part_src = dot(sum_matrix(src_ref[:, here], CNODE), grad_preact)
        part_dst = dot(sum_t[:, here], grad_preact)
        if at == 0:
            by_src[...] = part_src
            by_dst[...] = part_dst
        else:
            by_src[...] += part_src
            by_dst[...] += part_dst
    grad_c0 = (
        grad_c1
        + dot_rt(by_src[...].astype(BF), w1_ref[0:feature, :])
        + dot_rt(by_dst[...].astype(BF), w1_ref[feature:, :])
    )
    spread = dot(pick_matrix(assign_ref[...], CNODE), (grad_c0 * weight).astype(BF))
    grad_fine_ref[...] = cot_ref[...].astype(F32) + spread
    own = pl.ds(pl.multiple_of(place_ref[0] * 128, 128), 128)
    for half, rows in enumerate((by_src, by_dst)):
        pack_ref[half, 0:256, :] = dot_lt(table[...], rows[:, own].astype(BF))
    second = dot_lt(acc[:, own].astype(BF), grad_summed)
    for half in range(2):
        for k in range(2):
            pack_ref[half, 256 + 64 * k : 320 + 64 * k, :] = second[
                64 * half : 64 * half + 64, 128 * k : 128 * k + 128
            ]


def fine_backward_kernel(
    grad_fine_ref, summed_ref, slope_ref, acc_ref, left_ref, own_ref, src_ref, target_ref,
    place_ref, w1_ref, w2_ref, gain_ref, coarse_ref,
    local_ref, give_ref, keep_ref, ghost_b, ghost_w, ghost_e, by_src, by_dst, ghost, grad_left,
):
    nodes, feature = grad_fine_ref.shape
    rim = ghost_b.shape[0]
    core = place_ref[1]
    grad_fine = grad_fine_ref[...]
    grad_summed = summed_grad(grad_fine, gain_ref[...], summed_ref[...])
    for at in range(0, src_ref.shape[1], CHUNK):
        here = slice(at, at + CHUNK)
        target = target_ref[:, here]
        grad_message = dot(pick_matrix(target, nodes), grad_summed).astype(BF)
        grad_preact = (dot_rt(grad_message, w2_ref[...]) * slope_ref[here, :]).astype(BF)
        back = dot_rt(grad_preact, w1_ref[0:feature, :]).astype(BF)
        part_src = dot(sum_matrix(src_ref[:, here], by_src.shape[0]), back)
        part_left = dot_lt(left_ref[here, :], grad_preact)
        part_dst = dot(sum_matrix(target, nodes), grad_preact)
        if at == 0:
            by_src[...] = part_src
            grad_left[...] = part_left
            by_dst[...] = part_dst
        else:
            by_src[...] += part_src
            grad_left[...] += part_left
            by_dst[...] += part_dst
    local_ref[...] = (
        grad_fine
        + by_src[0:nodes, :]
        + dot_rt(by_dst[...].astype(BF), w1_ref[feature:, :])
    )
    ghost[...] = by_src[nodes:, :].astype(BF)
    to_core = ghost[pl.ds(pl.multiple_of(rim * (1 - core), rim), rim), :]
    give_ref[1920 : 1920 + rim, :] = to_core[:, 0:128]
    give_ref[1920 + rim :, :] = to_core[:, 128:256]
    ghost_b[...] = ghost[pl.ds(pl.multiple_of(rim * core, rim), rim), :]
    for out, at in ((ghost_w, 2 * rim), (ghost_e, 3 * rim)):
        out[0:rim, :] = ghost[at : at + rim, 0:128]
        out[rim:, :] = ghost[at : at + rim, 128:256]
    for out, half in ((give_ref, 1 - core), (keep_ref, core)):
        part = pl.ds(pl.multiple_of(half * 256, 256), 256)
        first = grad_left[:, part].astype(out.dtype)
        second = dot_lt(own_ref[...], by_dst[:, part].astype(BF)).astype(out.dtype)
        third = dot_lt(acc_ref[:, part], grad_summed).astype(out.dtype)
        for k in range(2):
            lanes = slice(128 * k, 128 * k + 128)
            out[512 * k : 512 * k + 256, :] = first[:, lanes]
            out[512 * k + 256 : 512 * k + 512, :] = second[:, lanes]
            out[1024 + 256 * k : 1280 + 256 * k, :] = third[:, lanes]
        out[1536:1920, :] = coarse_ref[half].astype(out.dtype)


def split_kernel(keep_ref, got_ref, ghost_w, ghost_e, place_ref, total_ref, coarse_ref, *sends):
    col = place_ref[0]

    def block(step):
        rows = pl.ds(pl.multiple_of(lax.rem(col + step, 4) * 384, 384), 384)
        return keep_ref[rows, :] + got_ref[rows, :].astype(F32)

    total_ref[...] = block(0)
    coarse_ref[...] = keep_ref[1536:1920, :] + got_ref[1536:1920, :].astype(F32)
    for step, out in enumerate(sends, 1):
        out[0:384, :] = block(step).astype(BF)
    sends[0][384:, :] = ghost_e[...]
    sends[2][384:, :] = ghost_w[...]


def return_kernel(local_ref, from_core, from_b, from_west, from_east, export_ref, place_ref, out_ref):
    rim = export_ref.shape[1]
    adds = sum_matrix(export_ref[...], local_ref.shape[0])
    col = place_ref[0]

    def wide(ref):
        at = ref.shape[0] - 2 * rim
        rows = ref[at:, :].astype(F32)
        return jnp.concatenate([rows[0:rim, :], rows[rim:, :]], axis=1)

    west = wide(from_west) * jnp.where(col > 0, 1.0, 0.0)
    east = wide(from_east) * jnp.where(col < 3, 1.0, 0.0)
    beyond = from_b[...].astype(F32) * jnp.where(place_ref[3] > 0, 1.0, 0.0)
    arrived = (wide(from_core) + beyond) + (west + east)
    high, low = halves(arrived)
    out_ref[...] = local_ref[...] + dot(adds, high) + dot(adds, low)


def unpack_kernel(
    mine_ref, other_ref, place_ref, fine1_ref, fine2_ref, coarse1_ref, coarse2_ref,
    *, fine_scale, coarse_scale,
):
    for ref, half in ((mine_ref, place_ref[1]), (other_ref, 1 - place_ref[1])):
        for plane in range(16):
            for x in range(4):
                values = ref[plane * 4 + x].astype(F32)
                for at in range(0, 24, 8):
                    row = x * 384 + plane * 24 + at
                    piece = values[at : at + 8, :] * fine_scale
                    if row < 1024:
                        lanes = pl.ds(pl.multiple_of(half * 256 + row // 512 * 128, 128), 128)
                        fine1_ref[row % 512 : row % 512 + 8, lanes] = piece
                    else:
                        start = pl.multiple_of(half * 256 + row % 256, 8)
                        lane = (row - 1024) // 256 * 128
                        fine2_ref[pl.ds(start, 8), lane : lane + 128] = piece
                    row = plane * 24 + at
                    piece = values[24 + at : 32 + at, :] * coarse_scale
                    if row < 256:
                        start = pl.multiple_of(half * 256 + row, 8)
                        coarse1_ref[pl.ds(start, 8), x * 128 : x * 128 + 128] = piece
                    else:
                        start = pl.multiple_of(half * 64 + x * 128 + row % 64, 8)
                        lane = (row - 256) // 64 * 128
                        coarse2_ref[pl.ds(start, 8), lane : lane + 128] = piece


class Late:
    def __init__(self, source, held, sem):
        self.held = held
        self.shape = held.shape
        self.copy = pltpu.make_async_copy(source, held, sem)
        self.copy.start()

    def __getitem__(self, index):
        if self.copy is not None:
            self.copy.wait()
            self.copy = None
        return self.held[index]

    def finish(self):
        if self.copy is not None:
            self.copy.wait()
            self.copy = None


def run(kernel, outs, operands, scratch=(), scalars=(), late=(), inner=(), ahead=(), limit=16, work=0.1):
    size = sum(math.prod(x.shape) * x.dtype.itemsize for x in [*operands, *ahead]) + sum(
        math.prod(shape) * jnp.dtype(kind).itemsize for shape, kind in outs
    )
    shapes = [
        (pltpu.VMEM if i in inner else jax.ShapeDtypeStruct)(shape, kind)
        for i, (shape, kind) in enumerate(outs)
    ] + [pltpu.VMEM(x.shape, x.dtype) for x in ahead]
    operands = [
        pltpu.with_memory_space_constraint(x, pltpu.HBM) if i in late else x
        for i, x in enumerate(operands)
    ] + [pltpu.with_memory_space_constraint(x, pltpu.HBM) for x in ahead]
    count = len(operands) - len(ahead)
    first_out = len(operands)
    first_ahead = first_out + len(outs)
    first_scratch = first_ahead + len(ahead)
    first_held = first_scratch + len(scratch)

    def space(i):
        return pltpu.SMEM if i in scalars else pltpu.HBM if i in late or i >= count else pltpu.VMEM

    def body(*refs):
        sems = refs[-1]
        inputs = list(refs[:count])
        for k, i in enumerate(late):
            inputs[i] = Late(refs[i], refs[first_held + k], sems.at[k])
        fetched = [
            Late(refs[count + k], refs[first_ahead + k], sems.at[len(late) + k])
            for k in range(len(ahead))
        ]
        kernel(*inputs, *refs[first_out:first_ahead], *refs[first_scratch:first_held])
        for copy in [inputs[i] for i in late] + fetched:
            copy.finish()

    copies = len(late) + len(ahead)
    return pl.pallas_call(
        body if copies else kernel,
        out_shape=shapes,
        in_specs=[pl.BlockSpec(memory_space=space(i)) for i in range(first_out)],
        out_specs=[pl.BlockSpec(memory_space=pltpu.VMEM)] * len(shapes),
        scratch_shapes=[pltpu.VMEM(shape, kind) for shape, kind in scratch]
        + [pltpu.VMEM(operands[i].shape, operands[i].dtype) for i in late]
        + ([pltpu.SemaphoreType.DMA((copies,))] if copies else []),
        compiler_params=pltpu.CompilerParams(vmem_limit_bytes=limit * 1024 * 1024),
        cost_estimate=pl.CostEstimate(
            flops=int(2e9 * work), bytes_accessed=size, transcendentals=0
        ),
    )(*operands)


ROW = ("z", "y", "core")
PLANE = ("z", "y")
CHIPS = ("z", "y", "x")


def send(value, axis, step):
    size = lax.axis_size(axis)
    return lax.ppermute(value, axis, [(i, (i + step) % size) for i in range(size)])


def shards(
    latent, cotangent, fine_w1, fine_w2, fine_gain, coarse_w1, coarse_w2, coarse_gain,
    fine_src, fine_dst, live_blocks, export_rows, pool_assign, coarse_src, coarse_dst,
):
    own = latent[0, 0]
    cot = cotangent[0, 0]
    nodes, feature = own.shape
    export = export_rows[0]
    assign = pool_assign[0]
    src, dst = fine_src[0], fine_dst[0]
    rim_count = export.shape[1]
    hidden = fine_w1.shape[1]
    edges, coarse_edges = src.shape[1], coarse_src.shape[1]
    rows, cols = lax.axis_size(ROW), lax.axis_size("x")
    fine_gain = fine_gain[None, :]
    coarse_gain = coarse_gain[None, :]
    between = [(i, i + 1) for i in range(1, rows - 1, 2)]
    between = between + [(target, source) for source, target in between]
    between = between + [(rows - 1, 0), (0, rows - 1)]
    row = lax.axis_index(ROW)
    inside = jnp.logical_and(row > 0, row < rows - 1)
    place = jnp.stack(
        [lax.axis_index("x"), lax.axis_index("core"), 128 * live_blocks[0, 0], inside]
    )
    own, place = lax.optimization_barrier((own, place.astype(jnp.int32)))
    wide = 2 * feature

    rim, pack, target, own_in, src_in, w1_in, w2_in, gain_in, assign_in, export_in = run(
        start_kernel,
        [
            ((rim_count, feature), BF),
            ((CNODE + 32, feature), BF),
            ((1, edges), jnp.int32),
        ],
        [own, export, cot, assign, dst, place],
        scalars=(5,),
        late=(0, 1, 2, 3, 4),
        inner=(0, 1, 2),
        ahead=[own, src, fine_w1, fine_w2, fine_gain, assign, export],
    )
    near, far = [(0, 1), (1, 0), (2, 3), (3, 2)], [(1, 2), (2, 1), (3, 0), (0, 3)]
    pack_got = lax.ppermute(pack, "x", near)
    from_west, from_east = send(rim, "x", 1), send(rim, "x", 3)
    from_a = send(rim, "core", 1)
    from_b = lax.ppermute(rim, ROW, between)
    part, left, csrc_in, cdst_in, cw1_in, cw2_in, cgain_in, cot_in = run(
        own_kernel,
        [((edges, hidden), F32), ((edges, feature), BF)],
        [own_in, src_in, target, w1_in],
        inner=(0, 1),
        ahead=[coarse_src, coarse_dst, coarse_w1, coarse_w2, coarse_gain, cot],
        limit=LIMITS[0],
        work=1.1,
    )
    pack, pack_got, part = lax.optimization_barrier((pack, pack_got, part))
    (pair,) = run(add_kernel, [((CNODE + 32, feature), BF)], [pack, pack_got], inner=(0,))
    pair, part = lax.optimization_barrier((pair, part))
    pair_got = lax.ppermute(pair, "x", far)
    slope, acc, summed, upper, lower, left = run(
        fine_forward_kernel,
        [
            ((edges, hidden), F32),
            ((nodes, hidden), BF),
            ((nodes, feature), F32),
            ((CNODE // 2, feature), BF),
            ((CNODE // 2, feature), BF),
            ((edges, feature), BF),
        ],
        [
            part, left, own_in, from_a, from_b, from_west, from_east, src_in, target, place,
            w1_in, w2_in, gain_in, assign_in,
        ],
        [((nodes + 4 * rim_count, feature), BF), ((nodes, hidden), F32)],
        scalars=(9,),
        inner=(0, 1, 2, 3, 4, 5),
        limit=LIMITS[1],
        work=1.6,
    )
    upper, lower, pair_got = lax.optimization_barrier((upper, lower, pair_got))
    near_got = lax.ppermute(upper, "x", near)
    far_got = lax.ppermute(lower, "x", far)
    first, second = run(
        pair_kernel,
        [((CNODE // 2, feature), BF)] * 2,
        [upper, near_got, lower, far_got],
        inner=(0, 1),
    )
    got = [lax.ppermute(first, "x", far), lax.ppermute(second, "x", near)]

    grad_fine, coarse_pack = run(
        coarse_kernel,
        [((nodes, feature), F32), ((2, 384, 128), F32)],
        [
            first, got[0], second, got[1], pair, pair_got, csrc_in, cdst_in, cw1_in, cw2_in, cgain_in,
            cot_in, assign_in, place,
        ],
        [
            ((CNODE, feature), BF),
            ((coarse_edges, hidden), F32),
            ((coarse_edges, CNODE), BF),
            ((CNODE, coarse_edges), BF),
            ((CNODE, hidden), F32),
            ((CNODE, hidden), F32),
            ((CNODE, hidden), F32),
        ],
        scalars=(13,),
        inner=(0, 1),
        limit=LIMITS[2],
        work=5.0,
    )

    local, give, keep, ghost_b, ghost_w, ghost_e = run(
        fine_backward_kernel,
        [
            ((nodes, feature), F32),
            ((1920 + 2 * rim_count, 128), BF),
            ((1920, 128), F32),
            ((rim_count, feature), BF),
            ((2 * rim_count, 128), BF),
            ((2 * rim_count, 128), BF),
        ],
        [
            grad_fine, summed, slope, acc, left, own_in, src_in, target, place,
            w1_in, w2_in, gain_in, coarse_pack,
        ],
        [
            ((nodes + 4 * rim_count, feature), F32),
            ((nodes, hidden), F32),
            ((4 * rim_count, feature), BF),
            ((feature, hidden), F32),
        ],
        scalars=(8,),
        inner=(0, 1, 2, 3, 4, 5),
        limit=LIMITS[3],
        work=2.8,
    )
    from_core = send(give, "core", 1)
    from_b = lax.ppermute(ghost_b, ROW, between)
    total, coarse_total, to_east, to_cross, to_west = run(
        split_kernel,
        [
            ((384, 128), F32),
            ((384, 128), F32),
            ((384 + 2 * rim_count, 128), BF),
            ((384, 128), BF),
            ((384 + 2 * rim_count, 128), BF),
        ],
        [keep, from_core, ghost_w, ghost_e, place],
        scalars=(4,),
        inner=(0, 1, 2, 3, 4),
    )
    from_west = send(to_east, "x", 1)
    from_cross = send(to_cross, "x", 2)
    from_east = send(to_west, "x", 3)
    total = (
        total
        + from_west[0:384].astype(F32)
        + from_cross.astype(F32)
        + from_east[0:384].astype(F32)
    )
    both = jnp.concatenate(
        [total.reshape(16, 24, 128), coarse_total.reshape(16, 24, 128)], axis=1
    ).astype(BF)
    both, from_b = lax.optimization_barrier((both, from_b))
    both = lax.all_to_all(both, PLANE, 0, 0, tiled=True)
    both = jnp.sum(both.astype(F32), axis=0).astype(BF)
    copies = jnp.broadcast_to(both[None], (64,) + both.shape)
    mine = lax.all_to_all(copies, CHIPS, 0, 0, tiled=True)
    mine, local = lax.optimization_barrier((mine, local))
    other = send(mine, "core", 1)
    (grad_latent,) = run(
        return_kernel,
        [((nodes, feature), F32)],
        [local, from_core, from_b, from_west, from_east, export_in, place],
        scalars=(6,),
    )
    unpack = functools.partial(
        unpack_kernel,
        fine_scale=1.0 / math.sqrt(edges * rows * cols),
        coarse_scale=1.0 / math.sqrt(coarse_edges * rows),
    )
    weight_grads = run(
        unpack,
        [
            ((2 * feature, hidden), F32),
            ((hidden, feature), F32),
            ((2 * feature, hidden), F32),
            ((hidden, feature), F32),
        ],
        [mine, other, place],
        scalars=(2,),
    )
    return (grad_latent[None, None], *weight_grads)


def solution(mesh):
    shape = (4, 4, 2, 4)
    inner = Mesh(mesh.devices.reshape(shape), ("z", "y", "core", "x"))
    node_sharded = P(ROW, "x", None, None)
    index_sharded = P(ROW, "x", None)
    placed = (
        node_sharded,
        node_sharded,
        P(),
        P(),
        P(),
        P(),
        P(),
        P(),
        index_sharded,
        index_sharded,
        P(ROW, "x"),
        index_sharded,
        index_sharded,
        P(ROW, None),
        P(ROW, None),
    )
    return jax.shard_map(
        shards,
        mesh=inner,
        in_specs=placed,
        out_specs=(node_sharded, P(), P(), P(), P()),
        check_vma=False,
    )
```

```python
import functools
import math

import jax
import jax.numpy as jnp
from jax import lax
from jax.experimental import pallas as pl
from jax.experimental.pallas import tpu as pltpu
from jax.sharding import Mesh
from jax.sharding import PartitionSpec as P

EPS = 1e-05
CNODE = 512
CHUNK = 1024
FINE_CHUNK = 2048
LIMITS = (28, 28, 36, 30)
BF = jnp.bfloat16
F32 = jnp.float32


def dot(left, right):
    return lax.dot_general(left, right, (((1,), (0,)), ((), ())), preferred_element_type=F32)


def dot_rt(left, right):
    return lax.dot_general(left, right, (((1,), (1,)), ((), ())), preferred_element_type=F32)


def dot_lt(left, right):
    return lax.dot_general(left, right, (((0,), (0,)), ((), ())), preferred_element_type=F32)


def halves(value):
    high = value.astype(BF)
    return high, (value - high.astype(F32)).astype(BF)


def spread_row(row):
    count = row.shape[1]
    return jnp.concatenate(
        [
            jnp.broadcast_to(row[:, at : at + 128], (128, 128)).T
            for at in range(0, count, 128)
        ],
        axis=0,
    )


def pick_matrix(row, width):
    column = spread_row(row)
    wide = jnp.concatenate([column] * (width // 128), axis=1)
    hit = wide == lax.broadcasted_iota(jnp.int32, wide.shape, 1)
    return jnp.where(hit, 1.0, 0.0).astype(BF)


def sum_matrix(row, width):
    shape = (width, row.shape[1])
    hit = lax.broadcasted_iota(jnp.int32, shape, 0) == row
    return jnp.where(hit, 1.0, 0.0).astype(BF)


def norm_of(summed):
    inverse = lax.rsqrt(jnp.mean(summed * summed, axis=-1, keepdims=True) + EPS)
    return inverse, summed * inverse


def summed_grad(grad_new, gain, summed):
    inverse, normed = norm_of(summed)
    grad_normed = grad_new * gain
    mean = jnp.mean(grad_normed * normed, axis=-1, keepdims=True)
    return (inverse * (grad_normed - normed * mean)).astype(BF)


def activations(preact):
    sig = jax.nn.sigmoid(preact)
    return (preact * sig).astype(BF), sig * (1.0 + preact * (1.0 - sig))


def split_count(count):
    many = jnp.floor(count * (1.0 / 256.0)) * 256.0
    upper = lax.broadcasted_iota(jnp.int32, count.shape, 0) < 8
    return jnp.where(upper, many, count - many).astype(BF)


def whole_count(rows):
    rows = rows.astype(F32)
    parts = [rows[at : at + 1, :] + rows[at + 8 : at + 9, :] for at in (0, 16)]
    return jnp.concatenate(parts, axis=1)


def start_kernel(
    own_ref, export_ref, cot_ref, assign_ref, dst_ref, place_ref, rim_ref, pack_ref, target_ref
):
    rim_ref[...] = dot(pick_matrix(export_ref[...], own_ref.shape[0]), own_ref[...]).astype(BF)
    pool = sum_matrix(assign_ref[...], CNODE)
    pack_ref[0:CNODE, :] = dot(pool, cot_ref[...]).astype(BF)
    packed = split_count(dot_rt(jnp.ones((16, pool.shape[1]), BF), pool))
    pack_ref[CNODE : CNODE + 16, :] = packed[:, :256]
    pack_ref[CNODE + 16 : CNODE + 32, :] = packed[:, 256:]
    slot = lax.broadcasted_iota(jnp.int32, dst_ref.shape, 1)
    target_ref[...] = jnp.where(slot < place_ref[2], dst_ref[...], -1)


def add_kernel(mine_ref, got_ref, out_ref):
    out_ref[0:CNODE, :] = (
        mine_ref[0:CNODE, :].astype(F32) + got_ref[0:CNODE, :].astype(F32)
    ).astype(BF)
    count = whole_count(mine_ref[CNODE:, :]) + whole_count(got_ref[CNODE:, :])
    packed = split_count(jnp.broadcast_to(count, (16, CNODE)))
    out_ref[CNODE : CNODE + 16, :] = packed[:, :256]
    out_ref[CNODE + 16 : CNODE + 32, :] = packed[:, 256:]


def pair_kernel(upper_ref, near_ref, lower_ref, far_ref, first_ref, second_ref):
    first_ref[...] = (upper_ref[...].astype(F32) + near_ref[...].astype(F32)).astype(BF)
    second_ref[...] = (lower_ref[...].astype(F32) + far_ref[...].astype(F32)).astype(BF)


def own_kernel(own_ref, src_ref, target_ref, w1_ref, part_ref, left_ref):
    nodes, feature = own_ref.shape
    for at in range(0, src_ref.shape[1], FINE_CHUNK):
        here = slice(at, at + FINE_CHUNK)
        left = dot(pick_matrix(src_ref[:, here], nodes), own_ref[...]).astype(BF)
        left_ref[here, :] = left
        right = dot(pick_matrix(target_ref[:, here], nodes), own_ref[...]).astype(BF)
        part_ref[here, :] = dot(left, w1_ref[0:feature, :]) + dot(right, w1_ref[feature:, :])


def fine_forward_kernel(
    part_ref, left_ref, own_ref, ra, rb, rw, re, src_ref, target_ref, place_ref,
    w1_ref, w2_ref, gain_ref, assign_ref, slope_ref, acc_out, summed_ref, upper_ref, lower_ref, pair_ref, table, acc,
):
    nodes, feature = own_ref.shape
    rim = ra.shape[0]
    col, core = place_ref[0], place_ref[1]
    table[0:nodes, :] = own_ref[...]
    table[pl.ds(pl.multiple_of(nodes + rim * (1 - core), rim), rim), :] = ra[...]
    beyond = rb[...].astype(F32) * jnp.where(place_ref[3] > 0, 1.0, 0.0)
    table[pl.ds(pl.multiple_of(nodes + rim * core, rim), rim), :] = beyond.astype(BF)
    west = rw[...].astype(F32) * jnp.where(col > 0, 1.0, 0.0)
    east = re[...].astype(F32) * jnp.where(col < 3, 1.0, 0.0)
    table[nodes + 2 * rim : nodes + 3 * rim, :] = west.astype(BF)
    table[nodes + 3 * rim :, :] = east.astype(BF)
    for at in range(0, src_ref.shape[1], FINE_CHUNK):
        here = slice(at, at + FINE_CHUNK)
        picks = pick_matrix(src_ref[:, here] - nodes, 4 * rim)
        left = dot(picks, table[nodes:, :]).astype(BF)
        pair_ref[here, :] = left + left_ref[here, :]
        preact = part_ref[here, :] + dot(left, w1_ref[0:feature, :])
        hidden, slope = activations(preact)
        slope_ref[here, :] = slope
        part = dot(sum_matrix(target_ref[:, here], nodes), hidden)
        if at == 0:
            acc[...] = part
        else:
            acc[...] += part
    high, low = halves(acc[...])
    acc_out[...] = high
    summed = dot(high, w2_ref[...]) + dot(low, w2_ref[...])
    summed_ref[...] = summed
    _, normed = norm_of(summed)
    fine_new = own_ref[...].astype(F32) + normed * gain_ref[...]
    pool = sum_matrix(assign_ref[...], CNODE)
    pooled = dot(pool, fine_new.astype(BF)).astype(BF)
    upper_ref[...] = pooled[0 : CNODE // 2, :]
    lower_ref[...] = pooled[CNODE // 2 :, :]


def coarse_kernel(
    p0, p1, q0, q1, g0, g1, src_ref, dst_ref, w1_ref, w2_ref, gain_ref, cot_ref,
    assign_ref, place_ref, grad_fine_ref, pack_ref,
    table, slope, pick_t, sum_t, acc, by_src, by_dst,
):
    feature = p0.shape[1]
    edges = src_ref.shape[1]
    grad_c1 = g0[0:CNODE, :].astype(F32) + g1[0:CNODE, :].astype(F32)
    count = whole_count(g0[CNODE:, :]) + whole_count(g1[CNODE:, :])
    weight = spread_row(1.0 / jnp.maximum(count, 1.0))
    weight = jnp.concatenate([weight] * (feature // 128), axis=1)
    pooled = jnp.concatenate(
        [
            p0[...].astype(F32) + p1[...].astype(F32),
            q0[...].astype(F32) + q1[...].astype(F32),
        ],
        axis=0,
    )
    table[...] = (pooled * weight).astype(BF)
    for at in range(0, edges, CHUNK):
        here = slice(at, at + CHUNK)
        left = dot(pick_matrix(src_ref[:, here], CNODE), table[...]).astype(BF)
        pick = pick_matrix(dst_ref[:, here], CNODE)
        pick_t[here, :] = pick
        right = dot(pick, table[...]).astype(BF)
        preact = dot(left, w1_ref[0:feature, :]) + dot(right, w1_ref[feature:, :])
        hidden, slope[here, :] = activations(preact)
        adds = sum_matrix(dst_ref[:, here], CNODE)
        sum_t[:, here] = adds
        part = dot(adds, hidden)
        if at == 0:
            acc[...] = part
        else:
            acc[...] += part
    high, low = halves(acc[...])
    summed = dot(high, w2_ref[...]) + dot(low, w2_ref[...])
    grad_summed = summed_grad(grad_c1, gain_ref[...], summed)
    for at in range(0, edges, CHUNK):
        here = slice(at, at + CHUNK)
        grad_message = dot(pick_t[here, :], grad_summed).astype(BF)
        grad_preact = (dot_rt(grad_message, w2_ref[...]) * slope[here, :]).astype(BF)
        part_src = dot(sum_matrix(src_ref[:, here], CNODE), grad_preact)
        part_dst = dot(sum_t[:, here], grad_preact)
        if at == 0:
            by_src[...] = part_src
            by_dst[...] = part_dst
        else:
            by_src[...] += part_src
            by_dst[...] += part_dst
    grad_c0 = (
        grad_c1
        + dot_rt(by_src[...].astype(BF), w1_ref[0:feature, :])
        + dot_rt(by_dst[...].astype(BF), w1_ref[feature:, :])
    )
    spread = dot(pick_matrix(assign_ref[...], CNODE), (grad_c0 * weight).astype(BF))
    grad_fine_ref[...] = cot_ref[...].astype(F32) + spread
    own = pl.ds(pl.multiple_of(place_ref[0] * 128, 128), 128)
    for half, rows in enumerate((by_src, by_dst)):
        pack_ref[half, 0:256, :] = dot_lt(table[...], rows[:, own].astype(BF))
    second = dot_lt(acc[:, own].astype(BF), grad_summed)
    for half in range(2):
        for k in range(2):
            pack_ref[half, 256 + 64 * k : 320 + 64 * k, :] = second[
                64 * half : 64 * half + 64, 128 * k : 128 * k + 128
            ]


def fine_backward_kernel(
    grad_fine_ref, summed_ref, slope_ref, acc_ref, left_ref, own_ref, src_ref, target_ref,
    place_ref, w1_ref, w2_ref, gain_ref, coarse_ref,
    local_ref, give_ref, keep_ref, ghost_b, ghost_w, ghost_e, by_src, by_dst, ghost, grad_left,
):
    nodes, feature = grad_fine_ref.shape
    rim = ghost_b.shape[0]
    core = place_ref[1]
    grad_fine = grad_fine_ref[...]
    grad_summed = summed_grad(grad_fine, gain_ref[...], summed_ref[...])
    for at in range(0, src_ref.shape[1], FINE_CHUNK):
        here = slice(at, at + FINE_CHUNK)
        target = target_ref[:, here]
        grad_message = dot(pick_matrix(target, nodes), grad_summed).astype(BF)
        grad_preact = (dot_rt(grad_message, w2_ref[...]) * slope_ref[here, :]).astype(BF)
        back = dot_rt(grad_preact, w1_ref[0:feature, :]).astype(BF)
        part_src = dot(sum_matrix(src_ref[:, here], by_src.shape[0]), back)
        part_left = dot_lt(left_ref[here, :], grad_preact)
        part_dst = dot(sum_matrix(target, nodes), grad_preact)
        if at == 0:
            by_src[...] = part_src
            grad_left[...] = part_left
            by_dst[...] = part_dst
        else:
            by_src[...] += part_src
            grad_left[...] += part_left
            by_dst[...] += part_dst
    local_ref[...] = (
        grad_fine
        + by_src[0:nodes, :]
        + dot_rt(by_dst[...].astype(BF), w1_ref[feature:, :])
    )
    ghost[...] = by_src[nodes:, :].astype(BF)
    to_core = ghost[pl.ds(pl.multiple_of(rim * (1 - core), rim), rim), :]
    give_ref[1920 : 1920 + rim, :] = to_core[:, 0:128]
    give_ref[1920 + rim :, :] = to_core[:, 128:256]
    ghost_b[...] = ghost[pl.ds(pl.multiple_of(rim * core, rim), rim), :]
    for out, at in ((ghost_w, 2 * rim), (ghost_e, 3 * rim)):
        out[0:rim, :] = ghost[at : at + rim, 0:128]
        out[rim:, :] = ghost[at : at + rim, 128:256]
    for out, half in ((give_ref, 1 - core), (keep_ref, core)):
        part = pl.ds(pl.multiple_of(half * 256, 256), 256)
        first = grad_left[:, part].astype(out.dtype)
        second = dot_lt(own_ref[...], by_dst[:, part].astype(BF)).astype(out.dtype)
        third = dot_lt(acc_ref[:, part], grad_summed).astype(out.dtype)
        for k in range(2):
            lanes = slice(128 * k, 128 * k + 128)
            out[512 * k : 512 * k + 256, :] = first[:, lanes]
            out[512 * k + 256 : 512 * k + 512, :] = second[:, lanes]
            out[1024 + 256 * k : 1280 + 256 * k, :] = third[:, lanes]
        out[1536:1920, :] = coarse_ref[half].astype(out.dtype)


def split_kernel(keep_ref, got_ref, ghost_w, ghost_e, place_ref, total_ref, coarse_ref, *sends):
    col = place_ref[0]

    def block(step):
        rows = pl.ds(pl.multiple_of(lax.rem(col + step, 4) * 384, 384), 384)
        return keep_ref[rows, :] + got_ref[rows, :].astype(F32)

    total_ref[...] = block(0)
    coarse_ref[...] = keep_ref[1536:1920, :] + got_ref[1536:1920, :].astype(F32)
    for step, out in enumerate(sends, 1):
        out[0:384, :] = block(step).astype(BF)
    sends[0][384:, :] = ghost_e[...]
    sends[2][384:, :] = ghost_w[...]


def return_kernel(local_ref, from_core, from_b, from_west, from_east, export_ref, place_ref, out_ref):
    rim = export_ref.shape[1]
    adds = sum_matrix(export_ref[...], local_ref.shape[0])
    col = place_ref[0]

    def wide(ref):
        at = ref.shape[0] - 2 * rim
        rows = ref[at:, :].astype(F32)
        return jnp.concatenate([rows[0:rim, :], rows[rim:, :]], axis=1)

    west = wide(from_west) * jnp.where(col > 0, 1.0, 0.0)
    east = wide(from_east) * jnp.where(col < 3, 1.0, 0.0)
    beyond = from_b[...].astype(F32) * jnp.where(place_ref[3] > 0, 1.0, 0.0)
    arrived = (wide(from_core) + beyond) + (west + east)
    high, low = halves(arrived)
    out_ref[...] = local_ref[...] + dot(adds, high) + dot(adds, low)


def unpack_kernel(
    mine_ref, other_ref, place_ref, fine1_ref, fine2_ref, coarse1_ref, coarse2_ref,
    *, fine_scale, coarse_scale,
):
    for ref, half in ((mine_ref, place_ref[1]), (other_ref, 1 - place_ref[1])):
        for plane in range(16):
            for x in range(4):
                values = ref[plane * 4 + x].astype(F32)
                for at in range(0, 24, 8):
                    row = x * 384 + plane * 24 + at
                    piece = values[at : at + 8, :] * fine_scale
                    if row < 1024:
                        lanes = pl.ds(pl.multiple_of(half * 256 + row // 512 * 128, 128), 128)
                        fine1_ref[row % 512 : row % 512 + 8, lanes] = piece
                    else:
                        start = pl.multiple_of(half * 256 + row % 256, 8)
                        lane = (row - 1024) // 256 * 128
                        fine2_ref[pl.ds(start, 8), lane : lane + 128] = piece
                    row = plane * 24 + at
                    piece = values[24 + at : 32 + at, :] * coarse_scale
                    if row < 256:
                        start = pl.multiple_of(half * 256 + row, 8)
                        coarse1_ref[pl.ds(start, 8), x * 128 : x * 128 + 128] = piece
                    else:
                        start = pl.multiple_of(half * 64 + x * 128 + row % 64, 8)
                        lane = (row - 256) // 64 * 128
                        coarse2_ref[pl.ds(start, 8), lane : lane + 128] = piece


class Late:
    def __init__(self, source, held, sem):
        self.held = held
        self.shape = held.shape
        self.copy = pltpu.make_async_copy(source, held, sem)
        self.copy.start()

    def __getitem__(self, index):
        if self.copy is not None:
            self.copy.wait()
            self.copy = None
        return self.held[index]

    def finish(self):
        if self.copy is not None:
            self.copy.wait()
            self.copy = None


def run(kernel, outs, operands, scratch=(), scalars=(), late=(), inner=(), ahead=(), limit=16, work=0.1):
    size = sum(math.prod(x.shape) * x.dtype.itemsize for x in [*operands, *ahead]) + sum(
        math.prod(shape) * jnp.dtype(kind).itemsize for shape, kind in outs
    )
    shapes = [
        (pltpu.VMEM if i in inner else jax.ShapeDtypeStruct)(shape, kind)
        for i, (shape, kind) in enumerate(outs)
    ] + [pltpu.VMEM(x.shape, x.dtype) for x in ahead]
    operands = [
        pltpu.with_memory_space_constraint(x, pltpu.HBM) if i in late else x
        for i, x in enumerate(operands)
    ] + [pltpu.with_memory_space_constraint(x, pltpu.HBM) for x in ahead]
    count = len(operands) - len(ahead)
    first_out = len(operands)
    first_ahead = first_out + len(outs)
    first_scratch = first_ahead + len(ahead)
    first_held = first_scratch + len(scratch)

    def space(i):
        return pltpu.SMEM if i in scalars else pltpu.HBM if i in late or i >= count else pltpu.VMEM

    def body(*refs):
        sems = refs[-1]
        inputs = list(refs[:count])
        for k, i in enumerate(late):
            inputs[i] = Late(refs[i], refs[first_held + k], sems.at[k])
        fetched = [
            Late(refs[count + k], refs[first_ahead + k], sems.at[len(late) + k])
            for k in range(len(ahead))
        ]
        kernel(*inputs, *refs[first_out:first_ahead], *refs[first_scratch:first_held])
        for copy in [inputs[i] for i in late] + fetched:
            copy.finish()

    copies = len(late) + len(ahead)
    return pl.pallas_call(
        body if copies else kernel,
        out_shape=shapes,
        in_specs=[pl.BlockSpec(memory_space=space(i)) for i in range(first_out)],
        out_specs=[pl.BlockSpec(memory_space=pltpu.VMEM)] * len(shapes),
        scratch_shapes=[pltpu.VMEM(shape, kind) for shape, kind in scratch]
        + [pltpu.VMEM(operands[i].shape, operands[i].dtype) for i in late]
        + ([pltpu.SemaphoreType.DMA((copies,))] if copies else []),
        compiler_params=pltpu.CompilerParams(vmem_limit_bytes=limit * 1024 * 1024),
        cost_estimate=pl.CostEstimate(
            flops=int(2e9 * work), bytes_accessed=size, transcendentals=0
        ),
    )(*operands)


ROW = ("z", "y", "core")
PLANE = ("z", "y")
CHIPS = ("z", "y", "x")


def send(value, axis, step):
    size = lax.axis_size(axis)
    return lax.ppermute(value, axis, [(i, (i + step) % size) for i in range(size)])


def shards(
    latent, cotangent, fine_w1, fine_w2, fine_gain, coarse_w1, coarse_w2, coarse_gain,
    fine_src, fine_dst, live_blocks, export_rows, pool_assign, coarse_src, coarse_dst,
):
    own = latent[0, 0]
    cot = cotangent[0, 0]
    nodes, feature = own.shape
    export = export_rows[0]
    assign = pool_assign[0]
    src, dst = fine_src[0], fine_dst[0]
    rim_count = export.shape[1]
    hidden = fine_w1.shape[1]
    edges, coarse_edges = src.shape[1], coarse_src.shape[1]
    rows, cols = lax.axis_size(ROW), lax.axis_size("x")
    fine_gain = fine_gain[None, :]
    coarse_gain = coarse_gain[None, :]
    between = [(i, i + 1) for i in range(1, rows - 1, 2)]
    between = between + [(target, source) for source, target in between]
    between = between + [(rows - 1, 0), (0, rows - 1)]
    row = lax.axis_index(ROW)
    inside = jnp.logical_and(row > 0, row < rows - 1)
    place = jnp.stack(
        [lax.axis_index("x"), lax.axis_index("core"), 128 * live_blocks[0, 0], inside]
    )
    own, place = lax.optimization_barrier((own, place.astype(jnp.int32)))
    wide = 2 * feature

    rim, pack, target, own_in, src_in, w1_in, w2_in, gain_in, assign_in, export_in = run(
        start_kernel,
        [
            ((rim_count, feature), BF),
            ((CNODE + 32, feature), BF),
            ((1, edges), jnp.int32),
        ],
        [own, export, cot, assign, dst, place],
        scalars=(5,),
        late=(0, 1, 2, 3, 4),
        inner=(0, 1, 2),
        ahead=[own, src, fine_w1, fine_w2, fine_gain, assign, export],
    )
    near, far = [(0, 1), (1, 0), (2, 3), (3, 2)], [(1, 2), (2, 1), (3, 0), (0, 3)]
    pack_got = lax.ppermute(pack, "x", near)
    from_west, from_east = send(rim, "x", 1), send(rim, "x", 3)
    from_a = send(rim, "core", 1)
    from_b = lax.ppermute(rim, ROW, between)
    part, left, csrc_in, cdst_in, cw1_in, cw2_in, cgain_in, cot_in = run(
        own_kernel,
        [((edges, hidden), F32), ((edges, feature), BF)],
        [own_in, src_in, target, w1_in],
        inner=(0, 1),
        ahead=[coarse_src, coarse_dst, coarse_w1, coarse_w2, coarse_gain, cot],
        limit=LIMITS[0],
        work=1.1,
    )
    pack, pack_got, part = lax.optimization_barrier((pack, pack_got, part))
    (pair,) = run(add_kernel, [((CNODE + 32, feature), BF)], [pack, pack_got], inner=(0,))
    pair, part = lax.optimization_barrier((pair, part))
    pair_got = lax.ppermute(pair, "x", far)
    slope, acc, summed, upper, lower, left = run(
        fine_forward_kernel,
        [
            ((edges, hidden), F32),
            ((nodes, hidden), BF),
            ((nodes, feature), F32),
            ((CNODE // 2, feature), BF),
            ((CNODE // 2, feature), BF),
            ((edges, feature), BF),
        ],
        [
            part, left, own_in, from_a, from_b, from_west, from_east, src_in, target, place,
            w1_in, w2_in, gain_in, assign_in,
        ],
        [((nodes + 4 * rim_count, feature), BF), ((nodes, hidden), F32)],
        scalars=(9,),
        inner=(0, 1, 2, 3, 4, 5),
        limit=LIMITS[1],
        work=1.6,
    )
    upper, lower, pair_got = lax.optimization_barrier((upper, lower, pair_got))
    near_got = lax.ppermute(upper, "x", near)
    far_got = lax.ppermute(lower, "x", far)
    first, second = run(
        pair_kernel,
        [((CNODE // 2, feature), BF)] * 2,
        [upper, near_got, lower, far_got],
        inner=(0, 1),
    )
    got = [lax.ppermute(first, "x", far), lax.ppermute(second, "x", near)]

    grad_fine, coarse_pack = run(
        coarse_kernel,
        [((nodes, feature), F32), ((2, 384, 128), F32)],
        [
            first, got[0], second, got[1], pair, pair_got, csrc_in, cdst_in, cw1_in, cw2_in, cgain_in,
            cot_in, assign_in, place,
        ],
        [
            ((CNODE, feature), BF),
            ((coarse_edges, hidden), F32),
            ((coarse_edges, CNODE), BF),
            ((CNODE, coarse_edges), BF),
            ((CNODE, hidden), F32),
            ((CNODE, hidden), F32),
            ((CNODE, hidden), F32),
        ],
        scalars=(13,),
        inner=(0, 1),
        limit=LIMITS[2],
        work=5.0,
    )

    local, give, keep, ghost_b, ghost_w, ghost_e = run(
        fine_backward_kernel,
        [
            ((nodes, feature), F32),
            ((1920 + 2 * rim_count, 128), BF),
            ((1920, 128), F32),
            ((rim_count, feature), BF),
            ((2 * rim_count, 128), BF),
            ((2 * rim_count, 128), BF),
        ],
        [
            grad_fine, summed, slope, acc, left, own_in, src_in, target, place,
            w1_in, w2_in, gain_in, coarse_pack,
        ],
        [
            ((nodes + 4 * rim_count, feature), F32),
            ((nodes, hidden), F32),
            ((4 * rim_count, feature), BF),
            ((feature, hidden), F32),
        ],
        scalars=(8,),
        inner=(0, 1, 2, 3, 4, 5),
        limit=LIMITS[3],
        work=2.8,
    )
    from_core = send(give, "core", 1)
    from_b = lax.ppermute(ghost_b, ROW, between)
    total, coarse_total, to_east, to_cross, to_west = run(
        split_kernel,
        [
            ((384, 128), F32),
            ((384, 128), F32),
            ((384 + 2 * rim_count, 128), BF),
            ((384, 128), BF),
            ((384 + 2 * rim_count, 128), BF),
        ],
        [keep, from_core, ghost_w, ghost_e, place],
        scalars=(4,),
        inner=(0, 1, 2, 3, 4),
    )
    from_west = send(to_east, "x", 1)
    from_cross = send(to_cross, "x", 2)
    from_east = send(to_west, "x", 3)
    total = (
        total
        + from_west[0:384].astype(F32)
        + from_cross.astype(F32)
        + from_east[0:384].astype(F32)
    )
    both = jnp.concatenate(
        [total.reshape(16, 24, 128), coarse_total.reshape(16, 24, 128)], axis=1
    ).astype(BF)
    both, from_b = lax.optimization_barrier((both, from_b))
    both = lax.all_to_all(both, PLANE, 0, 0, tiled=True)
    both = jnp.sum(both.astype(F32), axis=0).astype(BF)
    copies = jnp.broadcast_to(both[None], (64,) + both.shape)
    mine = lax.all_to_all(copies, CHIPS, 0, 0, tiled=True)
    mine, local = lax.optimization_barrier((mine, local))
    other = send(mine, "core", 1)
    (grad_latent,) = run(
        return_kernel,
        [((nodes, feature), F32)],
        [local, from_core, from_b, from_west, from_east, export_in, place],
        scalars=(6,),
    )
    unpack = functools.partial(
        unpack_kernel,
        fine_scale=1.0 / math.sqrt(edges * rows * cols),
        coarse_scale=1.0 / math.sqrt(coarse_edges * rows),
    )
    weight_grads = run(
        unpack,
        [
            ((2 * feature, hidden), F32),
            ((hidden, feature), F32),
            ((2 * feature, hidden), F32),
            ((hidden, feature), F32),
        ],
        [mine, other, place],
        scalars=(2,),
    )
    return (grad_latent[None, None], *weight_grads)


def solution(mesh):
    shape = (4, 4, 2, 4)
    inner = Mesh(mesh.devices.reshape(shape), ("z", "y", "core", "x"))
    node_sharded = P(ROW, "x", None, None)
    index_sharded = P(ROW, "x", None)
    placed = (
        node_sharded,
        node_sharded,
        P(),
        P(),
        P(),
        P(),
        P(),
        P(),
        index_sharded,
        index_sharded,
        P(ROW, "x"),
        index_sharded,
        index_sharded,
        P(ROW, None),
        P(ROW, None),
    )
    return jax.shard_map(
        shards,
        mesh=inner,
        in_specs=placed,
        out_specs=(node_sharded, P(), P(), P(), P()),
        check_vma=False,
    )
```
